32 devices in a mesh: events: 8 (over y, x, core), mp: 4 (over z).
Axes of the slice: x: 2, y: 2, z: 4, core: 2. Of those that a mesh axis runs over, the one named last changes fastest.
Arguments:
- event_x: bfloat16 [24576, 1024], P(('events', 'mp')), may hold values from -6 to 6
- event_visit: int32 [24576], P(('events', 'mp')), may hold values from -1 to 191, as said below
- visit_count: int32 [192], P(('events', 'mp')), may hold values from 1 to 128
- visit_patient: int32 [192], P('events'), may hold values from 0 to 191, as said below
- treatment: int32 [192], P('events'), may hold values 0 or 1
- outcome_target: float32 [192], P('events'), may hold values from -6 to 6
- enc_gain: float32 [1024], replicated, may hold values from 0.1 to 1.9
- enc_qkv: bfloat16 [1024, 3072], replicated, may hold values from -0.1875 to 0.1875
- enc_out: bfloat16 [1024, 1024], replicated, may hold values from -0.1875 to 0.1875
- visit_gain: float32 [2048], replicated, may hold values from 0.1 to 1.9
- visit_qkv: bfloat16 [3, 2048, 2048], P(None, 'events', 'mp'), may hold values from -0.125 to 0.125
- ffn_gain: float32 [2048], replicated, may hold values from 0.1 to 1.9
- ffn_in: bfloat16 [2048, 8192], P('events', 'mp'), may hold values from -0.125 to 0.125
- ffn_out: bfloat16 [8192, 2048], P('mp', 'events'), may hold values from -0.0625 to 0.0625
- head_weight: float32 [2048, 2], replicated, may hold values from -0.125 to 0.125
- head_bias: float32 [2], replicated, may hold values from -4 to 4
Outputs:
- outcomes: float32 [192, 2], P('events')
- event_grads: bfloat16 [24576, 1024], P(('events', 'mp'))
The draws below stay inside these ranges and needn't reach their ends.
Inputs may be any that keep to these rules, and one draw needn't show every extreme that they name: `event_visit`: the visit of each event row, or -1 for an empty row. Visit v is owned by the device of index v // 6 along events+mp, whose mp index equals that of every device holding one of its events. One device holds at most 96 events of the visits owned by any one device, and some owner receives exactly 96 from every device of its mp index. Visit v has exactly visit_count[v] rows. `visit_patient`: A patient's visits are consecutive and owned by one device.
All inputs are finite; a program needn't handle non-finite values. No bound on the sum of `treatment` on one device may be relied on, other than what follows from the above.
Results may differ from the reference program's by a relative error of at most 0.025.
Values may be sent and summed in bfloat16 or wider, within the bound.
No kernel may reach another device: no remote copies, remote signals or barrier semaphores. Data moves between devices by JAX's collectives and lax.ppermute only.
A program may use at most 128 MiB of HBM per device.

```python
import jax
import jax.numpy as jnp
from jax import lax

D = 1024
HEADS = 16
HDIM = 64
VB = 128
DV = 2048
VHEADS = 16
VHDIM = 128
FF = 8192
VIS_DEV = 6
EV_DEV = 768
CAP = 96
GROUP = 24
VISITS = 192
EVENTS = 24576
N_EVENTS = 8
N_MP = 4


def routing_table(key):
    devices = N_EVENTS * N_MP
    counts = jax.random.randint(jax.random.fold_in(key, 11), (devices, VIS_DEV), 1, VB + 1)
    first_full = jax.random.randint(jax.random.fold_in(key, 12), (devices,), 0, VIS_DEV)
    visit_slots = jnp.arange(VIS_DEV, dtype=jnp.int32)
    counts = jnp.where(visit_slots[None, :] == first_full[:, None], VB, counts)
    full_device = jax.random.randint(jax.random.fold_in(key, 13), (), 0, devices)
    counts = jnp.where((jnp.arange(devices, dtype=jnp.int32) == full_device)[:, None], VB, counts)
    totals = jnp.sum(counts, axis=1)
    bounds = jnp.cumsum(counts, axis=1)
    sources = jnp.arange(N_EVENTS, dtype=jnp.int32)[:, None, None, None]
    mp_lanes = jnp.arange(N_MP, dtype=jnp.int32)[None, :, None, None]
    spans = jnp.arange(N_EVENTS, dtype=jnp.int32)[None, None, :, None]
    within = jnp.arange(CAP, dtype=jnp.int32)[None, None, None, :]
    full_shape = (N_EVENTS, N_MP, N_EVENTS, CAP)
    target_dev = jnp.broadcast_to((sources - spans) % N_EVENTS * N_MP + mp_lanes, full_shape)
    event_rank = jnp.broadcast_to(spans * CAP + within, full_shape)
    live_event = event_rank < totals[target_dev]
    visit_local = jnp.sum((bounds[target_dev] <= event_rank[..., None]).astype(jnp.int32), axis=-1)
    visit_ids = jnp.where(live_event, target_dev * VIS_DEV + visit_local, -1)
    visit_ids = visit_ids.reshape(devices, EV_DEV)
    row_scores = jax.random.randint(jax.random.fold_in(key, 14), (devices, EV_DEV), 0, 2 ** 19) * EV_DEV + jnp.arange(EV_DEV, dtype=jnp.int32)[None, :]
    order_rows = jnp.argsort(row_scores, axis=1)
    visit_ids = jnp.take_along_axis(visit_ids, order_rows, axis=1)
    return (visit_ids.reshape(EVENTS).astype(jnp.int32), counts.reshape(VISITS).astype(jnp.int32))


def draw_event_visit(key, part):
    return routing_table(key)[0]


def draw_visit_count(key, part):
    return routing_table(key)[1]


def draw_visit_patient(key, part):
    devices = N_EVENTS * N_MP
    starts = jax.random.randint(jax.random.fold_in(key, 21), (devices, VIS_DEV), 0, 2)
    starts = starts.at[:, 0].set(1)
    starts = starts.at[devices - 1, :].set(1)
    numbers = jnp.cumsum(starts, axis=1) - 1
    patient_ids = jnp.arange(devices, dtype=jnp.int32)[:, None] * VIS_DEV + numbers
    return patient_ids.reshape(VISITS).astype(jnp.int32)


def set_ends(drawn, key, smallest, top_value):
    longest = drawn.shape.index(max(drawn.shape))
    spots = []
    for shift in (0, 1):
        where = [jax.random.randint(jax.random.fold_in(key, axis), (), 0, length) for axis, length in enumerate(drawn.shape)]
        where[longest] = (where[longest] + shift) % drawn.shape[longest]
        spots.append(tuple(where))
    return drawn.at[spots[0]].set(smallest).at[spots[1]].set(top_value)


def shard_levels(own_key, shape, pieces, low, top_value):
    loudness, own = 1.0, jax.random.fold_in(own_key, 6)
    for axis_at, blocks in pieces:
        heights = jnp.exp(jax.random.uniform(jax.random.fold_in(own, axis_at), (blocks,), jnp.float32, low / len(pieces), top_value / len(pieces)))
        loudness = loudness * jnp.repeat(heights, shape[axis_at] // blocks).reshape([-1 if axis == axis_at else 1 for axis in range(len(shape))])
    return loudness


def centred(key, shape, width, reach, cuts=(), kind=jnp.bfloat16):
    entries = width * jax.random.normal(key, shape, jnp.float32)
    if cuts:
        entries = entries * shard_levels(key, shape, cuts, -0.22, 0.18)
    return jnp.clip(entries, -reach, reach).astype(kind)


def setup_inputs(seed: int = 0) -> dict:
    streams_of = jax.random.split(jax.random.key(seed), 17)
    return {
        "event_x": centred(streams_of[0], (EVENTS, D), 1.0, 6.0, ((0, 32),)),
        "event_visit": draw_event_visit(jax.random.fold_in(streams_of[16], 71), 0),
        "visit_count": draw_visit_count(jax.random.fold_in(streams_of[16], 71), 0),
        "visit_patient": draw_visit_patient(jax.random.fold_in(streams_of[16], 71), 0),
        "treatment": set_ends((jax.random.randint(streams_of[4], (VISITS,), 0, 2) < 1).astype(jnp.int32), jax.random.fold_in(streams_of[4], 1), 0, 1),
        "outcome_target": centred(streams_of[5], (VISITS,), 1.0, 6.0, ((0, 8),), jnp.float32),
        "enc_gain": jnp.clip(1.0 + 0.18 * jax.random.normal(streams_of[6], (D,), jnp.float32), 0.1, 1.9),
        "enc_qkv": centred(streams_of[7], (D, 3 * D), D ** -0.5, 0.1875),
        "enc_out": centred(streams_of[8], (D, D), D ** -0.5, 0.1875),
        "visit_gain": jnp.clip(1.0 + 0.18 * jax.random.normal(streams_of[9], (DV,), jnp.float32), 0.1, 1.9),
        "visit_qkv": centred(streams_of[10], (3, DV, DV), DV ** -0.5, 0.125, ((1, 8), (2, 4))),
        "ffn_gain": jnp.clip(1.0 + 0.18 * jax.random.normal(streams_of[11], (DV,), jnp.float32), 0.1, 1.9),
        "ffn_in": centred(streams_of[12], (DV, FF), DV ** -0.5, 0.125, ((0, 8), (1, 4))),
        "ffn_out": centred(streams_of[13], (FF, DV), FF ** -0.5, 0.0625, ((0, 4), (1, 8))),
        "head_weight": centred(streams_of[14], (DV, 2), DV ** -0.5, 0.125, (), jnp.float32),
        "head_bias": centred(streams_of[15], (2,), 1.0, 4.0, (), jnp.float32),
    }


def rms_scale(values, gain):
    return values * lax.rsqrt(lax.optimization_barrier(jnp.mean(values * values, axis=-1, keepdims=True)) + 1e-05) * gain

def rms_back(grad_norm, values, gain):
    factor = lax.rsqrt(lax.optimization_barrier(jnp.mean(values * values, axis=-1, keepdims=True)) + 1e-05)
    scaled = grad_norm * gain
    return factor * (scaled - values * factor * factor * lax.optimization_barrier(jnp.mean(scaled * values, axis=-1, keepdims=True)))

def encode_device(blocks, counts, enc_gain, enc_qkv, enc_out):
    normed = rms_scale(blocks.astype(jnp.float32), enc_gain).astype(jnp.bfloat16)
    mixed_qkv = jnp.dot(normed, enc_qkv, preferred_element_type=jnp.float32).astype(jnp.bfloat16)
    queries = mixed_qkv[:, :D].reshape(VIS_DEV, VB, HEADS, HDIM).astype(jnp.float32)
    key_rows = mixed_qkv[:, D:2 * D].reshape(VIS_DEV, VB, HEADS, HDIM).astype(jnp.float32)
    values = mixed_qkv[:, 2 * D:].reshape(VIS_DEV, VB, HEADS, HDIM).astype(jnp.float32)
    scores = jnp.einsum('vqhd,vkhd->vhqk', queries, key_rows) * HDIM ** (-0.5)
    live_slots = jnp.arange(VB, dtype=jnp.int32)[None, :] < counts[:, None]
    scores = jnp.where(live_slots[:, None, None, :], scores, -1e+30)
    attn_b16 = jax.nn.softmax(scores, axis=-1).astype(jnp.bfloat16)
    attended = jnp.einsum('vhqk,vkhd->vqhd', attn_b16.astype(jnp.float32), values)
    attended = attended.astype(jnp.bfloat16).reshape(VIS_DEV * VB, D)
    hidden = blocks.astype(jnp.float32) + jnp.dot(attended, enc_out, preferred_element_type=jnp.float32)
    weights_live = live_slots.astype(jnp.float32)[:, :, None]
    denom = counts.astype(jnp.float32)[:, None]
    mean_hidden = lax.optimization_barrier(jnp.sum(hidden.reshape(VIS_DEV, VB, D) * weights_live, axis=1)) / denom
    mean_input = lax.optimization_barrier(jnp.sum(blocks.astype(jnp.float32).reshape(VIS_DEV, VB, D) * weights_live, axis=1)) / denom
    return jnp.concatenate([mean_hidden, mean_input], axis=1)

def visit_group(visit_vec, patient, treated, target, counts, visit_gain, visit_qkv, ffn_gain, ffn_in, ffn_out, head_weight, head_bias):
    rows_all = visit_vec.shape[0]
    normed = rms_scale(visit_vec, visit_gain).astype(jnp.bfloat16)
    mixed_qkv = jnp.einsum('rd,tde->rte', normed.astype(jnp.float32), visit_qkv.astype(jnp.float32)).astype(jnp.bfloat16)
    queries = mixed_qkv[:, 0].reshape(rows_all, VHEADS, VHDIM).astype(jnp.float32)
    key_rows = mixed_qkv[:, 1].reshape(rows_all, VHEADS, VHDIM).astype(jnp.float32)
    values = mixed_qkv[:, 2].reshape(rows_all, VHEADS, VHDIM).astype(jnp.float32)
    positions = jnp.arange(rows_all, dtype=jnp.int32)
    allowed = (patient[:, None] == patient[None, :]) & (positions[None, :] <= positions[:, None])
    scores = jnp.einsum('qhd,khd->hqk', queries, key_rows) * VHDIM ** (-0.5)
    attn_f32 = jax.nn.softmax(jnp.where(allowed[None], scores, -1e+30), axis=-1)
    attn_b16 = attn_f32.astype(jnp.bfloat16).astype(jnp.float32)
    attended = jnp.einsum('hqk,khd->qhd', attn_b16, values).astype(jnp.bfloat16).reshape(rows_all, DV)
    middle = visit_vec + attended.astype(jnp.float32)
    middle_in = rms_scale(middle, ffn_gain).astype(jnp.bfloat16)
    pre_act = jnp.dot(middle_in, ffn_in, preferred_element_type=jnp.float32)
    activated = jax.nn.silu(pre_act).astype(jnp.bfloat16)
    ffn_res = jnp.dot(activated, ffn_out, preferred_element_type=jnp.float32)
    combined = middle + ffn_res
    outcome_rows = jnp.dot(combined, head_weight, precision=lax.Precision.HIGHEST) + head_bias
    picker = (jnp.arange(2, dtype=jnp.int32)[None, :] == treated[:, None]).astype(jnp.float32)
    factual = lax.optimization_barrier(jnp.sum(outcome_rows * picker, axis=1))
    grad_out = picker * (4096.0 * (factual - target))[:, None]
    grad_c = jnp.dot(grad_out, head_weight.T, precision=lax.Precision.HIGHEST)
    grad_cf = grad_c.astype(jnp.bfloat16)
    grad_act = jnp.dot(grad_cf, ffn_out.T, preferred_element_type=jnp.float32)
    sigma = jax.nn.sigmoid(pre_act)
    grad_pre = (grad_act * sigma * (1.0 + pre_act * (1.0 - sigma))).astype(jnp.bfloat16)
    grad_min = jnp.dot(grad_pre, ffn_in.T, preferred_element_type=jnp.float32)
    grad_mid = grad_c + rms_back(grad_min, middle, ffn_gain)
    grad_cb = grad_mid.astype(jnp.bfloat16).reshape(rows_all, VHEADS, VHDIM).astype(jnp.float32)
    grad_p = jnp.einsum('qhd,khd->hqk', grad_cb, values)
    grad_s = attn_f32 * (grad_p - lax.optimization_barrier(jnp.sum(grad_p * attn_f32, axis=-1, keepdims=True))) * VHDIM ** (-0.5)
    grad_s = grad_s.astype(jnp.bfloat16).astype(jnp.float32)
    grad_q = jnp.einsum('hqk,khd->qhd', grad_s, key_rows).astype(jnp.bfloat16).reshape(rows_all, DV)
    grad_k = jnp.einsum('hqk,qhd->khd', grad_s, queries).astype(jnp.bfloat16).reshape(rows_all, DV)
    grad_v = jnp.einsum('hqk,qhd->khd', attn_b16, grad_cb).astype(jnp.bfloat16).reshape(rows_all, DV)
    grad_three = jnp.stack([grad_q, grad_k, grad_v], axis=1).astype(jnp.float32)
    grad_in = jnp.einsum('rte,tde->rd', grad_three, visit_qkv.astype(jnp.float32))
    grad_vec = grad_mid + rms_back(grad_in, visit_vec, visit_gain)
    visit_grad = (grad_vec[:, :D] / counts.astype(jnp.float32)[:, None]).astype(jnp.bfloat16)
    return (outcome_rows, visit_grad)

def reference(event_x, event_visit, visit_count, visit_patient, treatment, outcome_target, enc_gain, enc_qkv, enc_out, visit_gain, visit_qkv, ffn_gain, ffn_in, ffn_out, head_weight, head_bias):
    devices = N_EVENTS * N_MP
    sort_keys = jnp.where(event_visit >= 0, event_visit, VISITS).astype(jnp.int32)
    order_rows = jnp.argsort(sort_keys, stable=True).astype(jnp.int32)
    sorted_keys = sort_keys[order_rows]
    first_rows = jnp.searchsorted(sorted_keys, sorted_keys, side='left').astype(jnp.int32)
    slot_rank = jnp.arange(EVENTS, dtype=jnp.int32) - first_rows
    dest_rows = jnp.where(sorted_keys < VISITS, sorted_keys * VB + slot_rank, VISITS * VB).astype(jnp.int32)
    blocks = jnp.zeros((VISITS * VB, D), jnp.bfloat16).at[dest_rows].set(event_x[order_rows], mode='drop')

    def encode_one(packed):
        return encode_device(packed[0], packed[1], enc_gain, enc_qkv, enc_out)
    visit_vec = lax.map(encode_one, (blocks.reshape(devices, VIS_DEV * VB, D), visit_count.reshape(devices, VIS_DEV)))
    visit_vec = visit_vec.reshape(N_EVENTS, GROUP, DV)

    def group_one(packed):
        return visit_group(packed[0], packed[1], packed[2], packed[3], packed[4], visit_gain, visit_qkv, ffn_gain, ffn_in, ffn_out, head_weight, head_bias)
    outcome_all, grad_all = lax.map(group_one, (visit_vec, visit_patient.reshape(N_EVENTS, GROUP), treatment.reshape(N_EVENTS, GROUP), outcome_target.reshape(N_EVENTS, GROUP), visit_count.reshape(N_EVENTS, GROUP)))
    outcomes = outcome_all.reshape(VISITS, 2)
    grad_rows = grad_all.reshape(VISITS, D)
    picked = grad_rows[jnp.clip(event_visit, 0, VISITS - 1).astype(jnp.int32)]
    event_grads = jnp.where((event_visit >= 0)[:, None], picked, jnp.zeros_like(picked))
    return (outcomes, event_grads)
```

```python
import functools

import jax
import jax.numpy as jnp
from jax import lax
from jax.experimental import pallas as pl
from jax.experimental.pallas import tpu as pltpu
from jax.sharding import PartitionSpec as P

D = 1024
HEADS = 16
HDIM = 64
VB = 128
DV = 2048
VHDIM = 128
VPAD = 8
LANES = 128
EPS = 1e-5
F32 = jnp.float32
BF16 = jnp.bfloat16
VMEM_LIMIT = 48 * 1024 * 1024

NT = (((1,), (1,)), ((), ()))
TN = (((0,), (0,)), ((), ()))
NN = (((1,), (0,)), ((), ()))


def dot(a, b, dims=NN):
    return lax.dot_general(a, b, dims, preferred_element_type=F32)


def vmem():
    return pl.BlockSpec(memory_space=pltpu.VMEM)


def smem():
    return pl.BlockSpec(memory_space=pltpu.SMEM)


def hbm():
    return pl.BlockSpec(memory_space=pl.ANY)


def params():
    return pltpu.CompilerParams(vmem_limit_bytes=VMEM_LIMIT)


def strict_upper(rows):
    a = lax.broadcasted_iota(jnp.int32, (rows, rows), 0)
    b = lax.broadcasted_iota(jnp.int32, (rows, rows), 1)
    return (a < b).astype(BF16)


def pick_rows(position, first, count, rows):
    slots = lax.broadcasted_iota(jnp.int32, (count, rows), 0) + first
    return (slots == position).astype(BF16)


def pack_kernel(senders, per_owner, visits_dev, where_ref, ids_ref, x_ref, out_ref):
    rows = x_ref.shape[0]
    cap_rows = rows // senders
    ids = ids_ref[...]
    owners = lax.broadcasted_iota(jnp.int32, (senders, rows), 0)
    hot = (ids >= owners * per_owner) & (ids < (owners + 1) * per_owner)
    hot_f = hot.astype(F32)
    before = dot(hot.astype(BF16), strict_upper(rows))
    base = (owners * cap_rows + 1).astype(F32)
    position = (jnp.sum(hot_f * (base + before), axis=0, keepdims=True)).astype(jnp.int32) - 1
    first = (owners * per_owner + where_ref[1] * visits_dev).astype(F32)
    label = jnp.sum(hot_f * (ids.astype(F32) - first + 1.0), axis=0, keepdims=True)
    label = jnp.broadcast_to(label, (LANES, rows)).astype(BF16)
    step = rows // 3
    for c in range(3):
        chosen = pick_rows(position, c * step, step, rows)
        out_ref[c * step : (c + 1) * step, :D] = dot(chosen, x_ref[...]).astype(BF16)
        out_ref[c * step : (c + 1) * step, D:] = dot(chosen, label, NT).astype(BF16)


def encode_kernel(
    visits_dev,
    count_ref,
    got_ref,
    gain_ref,
    qkv_ref,
    proj_ref,
    vec_ref,
    wqk,
    wv,
    wo,
    normed,
    qk,
    pbar,
    ctx,
    sems,
):
    rows = got_ref.shape[0]
    slots = visits_dev * VB
    copies = [
        pltpu.make_async_copy(qkv_ref.at[:, : 2 * D], wqk, sems.at[0]),
        pltpu.make_async_copy(qkv_ref.at[:, 2 * D :], wv, sems.at[1]),
        pltpu.make_async_copy(proj_ref, wo, sems.at[2]),
    ]
    for copy in copies:
        copy.start()
    lane0 = (lax.broadcasted_iota(jnp.int32, (VPAD, LANES), 1) == 0).astype(BF16)
    label = dot(lane0, got_ref[:, D:], NT)[:1]
    visits = lax.broadcasted_iota(jnp.int32, (VPAD, rows), 0)
    hot = label == (visits + 1).astype(F32)
    hot_b = hot.astype(BF16)
    hot_f = hot.astype(F32)
    before = dot(hot_b, strict_upper(rows))
    base = (visits * VB + 1).astype(F32)
    position = (jnp.sum(hot_f * (base + before), axis=0, keepdims=True)).astype(jnp.int32) - 1
    sums = dot(hot_b, got_ref[:, :D])
    gain = gain_ref[...]
    step = 2 * VB
    for c in range(slots // step):
        part = dot(pick_rows(position, c * step, step, rows), got_ref[:, :D])
        scale = lax.rsqrt(jnp.mean(part * part, axis=-1, keepdims=True) + EPS)
        normed[c * step : (c + 1) * step, :] = (part * scale * gain).astype(BF16)
    copies[0].wait()
    wide = 512
    for c in range(2 * D // wide):
        cols = slice(c * wide, (c + 1) * wide)
        qk[:, cols] = dot(normed[...], wqk[:, cols]).astype(BF16)

    lanes = lax.broadcasted_iota(jnp.int32, (VB, LANES), 1)
    low = (lanes < HDIM).astype(F32) * HDIM ** (-0.5)
    high = (lanes >= HDIM).astype(F32) * HDIM ** (-0.5)
    key_slot = lax.broadcasted_iota(jnp.int32, (VB, 2 * VB), 0)
    query_lane = lax.broadcasted_iota(jnp.int32, (1, 2 * VB), 1)
    query_slot = jnp.where(query_lane >= VB, query_lane - VB, query_lane)
    rows8 = lax.broadcasted_iota(jnp.int32, (VPAD, 2 * VB), 0)
    lanes8 = lax.broadcasted_iota(jnp.int32, (VPAD, 2 * VB), 1)
    halves = ((lanes8 >= rows8 * VB) & (lanes8 < (rows8 + 1) * VB)).astype(BF16)

    def one_visit(v, carry):
        count = count_ref[v]
        at = pl.ds(pl.multiple_of(v * VB, VB), VB)
        live_key = key_slot < count
        weight = (query_slot < count).astype(F32) / count.astype(F32)
        for p in range(HEADS // 2):
            q = qk[at, p * LANES : (p + 1) * LANES].astype(F32)
            k = qk[at, D + p * LANES : D + (p + 1) * LANES]
            both = jnp.concatenate([(q * low).astype(BF16), (q * high).astype(BF16)], axis=0)
            scores = jnp.where(live_key, dot(k, both, NT), -1e30)
            top = jnp.max(scores, axis=0, keepdims=True)
            grown = jnp.exp(scores - top)
            total = jnp.sum(grown, axis=0, keepdims=True)
            shares = (grown * (weight / total)).astype(BF16)
            pbar[v, 2 * p : 2 * p + 2, :] = dot(halves, shares, NT)[:2]
        ctx[v] = dot(pbar[v].astype(BF16), normed[at, :]).astype(BF16)
        return carry

    lax.fori_loop(0, visits_dev, one_visit, 0)
    copies[1].wait()
    copies[2].wait()
    vals = dot(ctx[...].reshape(visits_dev * HEADS, D), wv[...]).reshape(visits_dev, HEADS, D)
    head_row = lax.broadcasted_iota(jnp.int32, (1, HEADS, D), 1) * HDIM
    col = lax.broadcasted_iota(jnp.int32, (1, HEADS, D), 2)
    own = (col >= head_row) & (col < head_row + HDIM)
    attended = jnp.sum(jnp.where(own, vals, 0.0), axis=1)
    attended = jnp.concatenate([attended, jnp.zeros((VPAD - visits_dev, D), F32)], axis=0)
    head_part = attended.astype(BF16)
    rest = (attended - head_part.astype(F32)).astype(BF16)
    mixed = dot(head_part, wo[...]) + dot(rest, wo[...])
    row = lax.broadcasted_iota(jnp.int32, (VPAD, 1), 0)
    inverse = jnp.zeros((VPAD, 1), F32)
    for v in range(visits_dev):
        inverse = jnp.where(row == v, 1.0 / count_ref[v].astype(F32), inverse)
    mean_input = sums * inverse
    vec_ref[:, :D] = (mean_input + mixed).astype(BF16)
    vec_ref[:, D:] = mean_input.astype(BF16)


def rms_factor(values):
    return lax.rsqrt(jnp.mean(values * values, axis=-1, keepdims=True) + EPS)


def fetch(pieces, scratch, sems):
    copies = [
        pltpu.make_async_copy(piece, buffer, sems.at[i])
        for i, (piece, buffer) in enumerate(zip(pieces, scratch, strict=True))
    ]
    for copy in copies:
        copy.start()
    return copies


def project_kernel(
    n_mp, n_ev, plan, where_ref, meta_ref, patient_ref, gain_ref, *refs
):
    n = len(plan)
    vec_in, refs = refs[:n_mp], refs[n_mp:]
    pieces, refs = refs[:n], refs[n:]
    vec_ref, attended_ref, qkv_ref, prob_ref = refs[:4]
    scratch, refs = refs[4 : 4 + n], refs[4 + n :]
    vec, blocks, sems = refs
    copies = fetch(pieces, scratch, sems)
    e, m = where_ref[0], where_ref[1]
    for k in range(n_mp):
        vec[m ^ k] = vec_in[k][...].astype(F32)
    rows = n_mp * VPAD
    full = vec[...].reshape(rows, DV)
    vec_ref[...] = full
    normed = (full * rms_factor(full) * gain_ref[...]).astype(BF16)
    width = DV // n_ev
    for j in range(n_ev):
        blocks[j] = normed[:, j * width : (j + 1) * width]
    cols = attended_ref.shape[1]
    totals = [jnp.zeros((rows, cols), F32) for _ in range(3)]
    for i, (k, lo, size) in enumerate(plan):
        copies[i].wait()
        block = blocks[e ^ k][:, lo : lo + size]
        for t in range(3):
            totals[t] = totals[t] + dot(block, scratch[i][t])
    parts = [total.astype(BF16) for total in totals]
    for t in range(3):
        qkv_ref[t] = parts[t]
    q_at = lax.broadcasted_iota(jnp.int32, (rows, rows), 0)
    k_at = lax.broadcasted_iota(jnp.int32, (rows, rows), 1)
    allowed = (meta_ref[:, 2:3] == patient_ref[...]) & (k_at <= q_at)
    for h in range(cols // VHDIM):
        span = slice(h * VHDIM, (h + 1) * VHDIM)
        scores = dot(parts[0][:, span], parts[1][:, span], NT) * VHDIM ** (-0.5)
        scores = jnp.where(allowed, scores, -1e30)
        grown = jnp.exp(scores - jnp.max(scores, axis=-1, keepdims=True))
        prob = grown / jnp.sum(grown, axis=-1, keepdims=True)
        prob_ref[h] = prob
        attended_ref[:, span] = dot(prob.astype(BF16), parts[2][:, span]).astype(BF16)


def pack_scalars(columns, rows):
    lane = lax.broadcasted_iota(jnp.int32, (rows, LANES), 1)
    spread = jnp.zeros((rows, LANES), F32)
    for c, column in enumerate(columns):
        at = (lane == c) | (lane == 8 + c) | (lane == 16 + c)
        spread = jnp.where(at, column, spread)
    one = spread.astype(BF16).astype(F32)
    two = (spread - one).astype(BF16).astype(F32)
    three = spread - one - two
    return jnp.where(lane < 8, one, jnp.where(lane < 16, two, three)).astype(BF16)


def unpack_scalar(packed, c):
    return packed[:, c : c + 1] + packed[:, 8 + c : 9 + c] + packed[:, 16 + c : 17 + c]


def ffn_kernel(
    n_mp, n_ev, plan, where_ref, meta_ref, vec_ref, gain_ref, fw_ref, head_ref, bias_ref, *refs
):
    n = len(plan)
    attn_in, refs = refs[:n_mp], refs[n_mp:]
    pieces, refs = refs[:n], refs[n:]
    outs, refs = refs[:n_mp], refs[n_mp:]
    mid_ref, refs = refs[0], refs[1:]
    scratch, refs = refs[:n], refs[n:]
    attn, blocks, grads, sems = refs
    copies = fetch(pieces, scratch, sems)
    e, m = where_ref[0], where_ref[1]
    rows = vec_ref.shape[0]
    for k in range(n_mp):
        attn[m ^ k] = attn_in[k][...].astype(F32)
    mid = vec_ref[...] + jnp.concatenate([attn[k] for k in range(n_mp)], axis=1)
    mid_ref[...] = mid
    gain = gain_ref[...]
    normed = (mid * rms_factor(mid) * gain).astype(BF16)
    width = DV // n_ev
    for j in range(n_ev):
        blocks[j] = normed[:, j * width : (j + 1) * width]
    pre = jnp.zeros((rows, fw_ref.shape[1]), F32)
    for i, (k, lo, size) in enumerate(plan):
        copies[i].wait()
        pre = pre + dot(blocks[e ^ k][:, lo : lo + size], scratch[i][...])
    sigma = 1.0 / (1.0 + jnp.exp(-pre))
    act = (pre * sigma).astype(BF16).astype(F32)
    first = (m == 0).astype(F32)
    outcome = []
    for j in range(2):
        base = jnp.sum(mid * head_ref[j : j + 1, :], axis=-1, keepdims=True) + bias_ref[j]
        outcome.append(jnp.sum(act * fw_ref[j : j + 1, :], axis=-1, keepdims=True) + first * base)
    chosen = jnp.where(meta_ref[:, 0:1] > 0.5, fw_ref[1:2, :], fw_ref[0:1, :])
    slope = (chosen * sigma * (1.0 + pre * (1.0 - sigma))).astype(BF16)
    for i, (k, lo, size) in enumerate(plan):
        grads[e ^ k, :, lo : lo + size] = dot(slope, scratch[i][...], NT)
    moment = jnp.zeros((rows, 1), F32)
    for j in range(n_ev):
        span = slice(j * width, (j + 1) * width)
        moment = moment + jnp.sum(grads[j] * gain[:, span] * mid[:, span], axis=-1, keepdims=True)
    scalars = pack_scalars([outcome[0], outcome[1], moment], rows)
    each = n_ev // n_mp
    cols = DV // n_mp
    for k in range(n_mp):
        for j in range(each):
            outs[k][:, j * width : (j + 1) * width] = grads[(m ^ k) * each + j].astype(BF16)
        outs[k][:, cols:] = scalars


def back_kernel(
    n_mp, n_ev, plan, where_ref, meta_ref, vec_ref, mid_ref, gain_ref, vgain_ref, head_ref,
    qkv_ref, prob_ref, *refs
):
    n = len(plan)
    pay_in, refs = refs[:n_mp], refs[n_mp:]
    pieces, refs = refs[:n], refs[n:]
    outs, refs = refs[:n_mp], refs[n_mp:]
    outcome_ref, refs = refs[0], refs[1:]
    scratch, refs = refs[:n], refs[n:]
    grads, table, sems = refs
    copies = fetch(pieces, scratch, sems)
    e, m = where_ref[0], where_ref[1]
    rows = vec_ref.shape[0]
    cols = DV // n_mp
    total = pay_in[0][...].astype(F32)
    for k in range(1, n_mp):
        total = total + pay_in[k][...].astype(F32)
    packed = total[:, cols:]
    outcome = [unpack_scalar(packed, 0), unpack_scalar(packed, 1)]
    moment = unpack_scalar(packed, 2) * (1.0 / DV)
    lane = lax.broadcasted_iota(jnp.int32, (rows, LANES), 1)
    outcome_ref[...] = jnp.where(lane == 0, outcome[0], outcome[1])
    treated = meta_ref[:, 0:1] > 0.5
    delta = 4096.0 * (jnp.where(treated, outcome[1], outcome[0]) - meta_ref[:, 1:2])
    factor = rms_factor(mid_ref[...])
    at = pl.ds(pl.multiple_of(m * cols, cols), cols)
    mid = mid_ref[:, at]
    head = jnp.where(treated, head_ref[1:2, at], head_ref[0:1, at])
    scaled = total[:, :cols] * gain_ref[:, at]
    grad_mid = delta * (head + factor * (scaled - mid * (factor * factor * moment)))
    grad_c = grad_mid.astype(BF16)
    three = [[], [], []]
    for h in range(cols // VHDIM):
        span = slice(h * VHDIM, (h + 1) * VHDIM)
        prob = prob_ref[h]
        grad_p = dot(grad_c[:, span], qkv_ref[2, :, span], NT)
        grad_s = prob * (grad_p - jnp.sum(grad_p * prob, axis=-1, keepdims=True))
        grad_s = (grad_s * VHDIM ** (-0.5)).astype(BF16)
        three[0].append(dot(grad_s, qkv_ref[1, :, span]).astype(BF16))
        three[1].append(dot(grad_s, qkv_ref[0, :, span], TN).astype(BF16))
        three[2].append(dot(prob.astype(BF16), grad_c[:, span], TN).astype(BF16))
    three = [jnp.concatenate(parts, axis=1) for parts in three]
    for i, (k, lo, size) in enumerate(plan):
        copies[i].wait()
        part = dot(three[0], scratch[i][0], NT)
        part = part + dot(three[1], scratch[i][1], NT)
        part = part + dot(three[2], scratch[i][2], NT)
        grads[e ^ k, :, lo : lo + size] = part
    width = DV // n_ev
    vec = vec_ref[...]
    spread = rms_factor(vec)
    moment = jnp.zeros((rows, 1), F32)
    for j in range(n_ev):
        span = slice(j * width, (j + 1) * width)
        scaled = grads[j] * vgain_ref[:, span]
        moment = moment + jnp.sum(scaled * vec[:, span], axis=-1, keepdims=True)
        if (j + 1) * width <= D:
            table[:, :, span] = (scaled * spread).reshape(n_mp, VPAD, width)

    @pl.when(m * cols < D)
    def _():
        here = pl.ds(pl.multiple_of(m * cols, cols), cols)
        table[:, :, here] = table[:, :, here] + grad_mid.reshape(n_mp, VPAD, cols)

    scalars = pack_scalars([moment], rows).astype(F32)
    table[:, :, D:] = scalars.reshape(n_mp, VPAD, LANES)
    for k in range(n_mp):
        outs[k][...] = table[m ^ k].astype(BF16)


def finish_kernel(n_mp, visits_dev, count_ref, own_ref, *refs):
    pays, out_ref = refs[:n_mp], refs[n_mp]
    total = pays[0][...].astype(F32)
    for k in range(1, n_mp):
        total = total + pays[k][...].astype(F32)
    vec = own_ref[...].astype(F32)
    spread = rms_factor(vec)
    moment = unpack_scalar(total[:, D:], 0) * (1.0 / DV)
    grad = total[:, :D] - vec[:, :D] * (spread * spread * spread * moment)
    row = lax.broadcasted_iota(jnp.int32, (VPAD, 1), 0)
    inverse = jnp.zeros((VPAD, 1), F32)
    for v in range(visits_dev):
        inverse = jnp.where(row == v, 1.0 / count_ref[v].astype(F32), inverse)
    out_ref[...] = (grad * inverse).astype(BF16)


def swap(x, axis, size, k):
    return lax.ppermute(x, axis, [(i, i ^ k) for i in range(size)])


def gather_weights(shard, n_ev, row_axis):
    rows = shard.shape[row_axis]
    if n_ev != 8:
        pieces = [shard] + [swap(shard, "events", n_ev, k) for k in range(1, n_ev)]
        return pieces, [(k, 0, rows) for k in range(n_ev)]
    half = rows // 2
    from_x = swap(shard, "events", n_ev, 2)
    from_y = swap(shard, "events", n_ev, 4)
    low = swap(lax.slice_in_dim(from_x, 0, half, axis=row_axis), "events", n_ev, 4)
    high = swap(lax.slice_in_dim(from_y, half, rows, axis=row_axis), "events", n_ev, 2)
    near = [shard, from_x, from_y, low, high]
    plan = [(0, 0, rows), (2, 0, rows), (4, 0, rows), (6, 0, half), (6, half, half)]
    far = [swap(piece, "events", n_ev, 1) for piece in near]
    return near + far, plan + [(k ^ 1, lo, size) for k, lo, size in plan]


def gather_events(block, n_ev):
    if n_ev != 8:
        return jnp.concatenate(
            [block] + [swap(block, "events", n_ev, k) for k in range(1, n_ev)], axis=0
        )
    pair = jnp.concatenate([block, swap(block, "events", n_ev, 1)], axis=0)
    return jnp.concatenate([pair] + [swap(pair, "events", n_ev, k) for k in (2, 4, 6)], axis=0)


def local(
    event_x,
    event_visit,
    visit_count,
    visit_patient,
    treatment,
    outcome_target,
    enc_gain,
    enc_qkv,
    enc_out,
    visit_gain,
    visit_qkv,
    ffn_gain,
    ffn_in,
    ffn_out,
    head_weight,
    head_bias,
):
    n_ev = lax.axis_size("events")
    n_mp = lax.axis_size("mp")
    e = lax.axis_index("events")
    m = lax.axis_index("mp")
    rows_dev = event_x.shape[0]
    visits_dev = visit_count.shape[0]
    per_owner = visits_dev * n_mp
    group = n_mp * VPAD
    cols = DV // n_mp
    hidden = ffn_in.shape[1]
    where = jnp.stack([e, m]).astype(jnp.int32)
    ids = event_visit.reshape(1, rows_dev)

    send = pl.pallas_call(
        functools.partial(pack_kernel, n_ev, per_owner, visits_dev),
        out_shape=jax.ShapeDtypeStruct((rows_dev, D + LANES), BF16),
        in_specs=[smem(), vmem(), vmem()],
        out_specs=vmem(),
        compiler_params=params(),
        name="pack",
    )(where, ids, event_x)
    got = lax.all_to_all(
        send.reshape(n_ev, rows_dev // n_ev, D + LANES), "events", split_axis=0, concat_axis=0,
        tiled=True,
    ).reshape(rows_dev, D + LANES)

    qkv_pieces, qkv_plan = gather_weights(visit_qkv, n_ev, 1)
    ffn_pieces, ffn_plan = gather_weights(ffn_in, n_ev, 0)

    head_t = head_weight.T
    width = DV // n_ev
    own_head = lax.dynamic_slice_in_dim(head_t, e * width, width, 1)
    head_hi = own_head.astype(BF16)
    head_mid = (own_head - head_hi.astype(F32)).astype(BF16)
    head_lo = (own_head - head_hi.astype(F32) - head_mid.astype(F32)).astype(BF16)
    fw = dot(jnp.concatenate([head_hi, head_mid, head_lo], axis=0), ffn_out, NT)
    fw = fw[0:2] + fw[2:4] + fw[4:6]
    step = 1
    while step < n_ev:
        fw = fw + swap(fw, "events", n_ev, step)
        step *= 2

    def spread_rows(values, fill):
        values = values.astype(F32).reshape(n_mp, visits_dev)
        return jnp.pad(values, ((0, 0), (0, VPAD - visits_dev)), constant_values=fill).reshape(group)

    patient = spread_rows(visit_patient, -1.0)
    meta = jnp.stack(
        [spread_rows(treatment, 0.0), spread_rows(outcome_target, 0.0), patient], axis=1
    )
    patient_row = patient.reshape(1, group)

    vec = pl.pallas_call(
        functools.partial(encode_kernel, visits_dev),
        out_shape=jax.ShapeDtypeStruct((VPAD, DV), BF16),
        in_specs=[smem(), vmem(), vmem(), hbm(), hbm()],
        out_specs=vmem(),
        scratch_shapes=[
            pltpu.VMEM((D, 2 * D), BF16),
            pltpu.VMEM((D, D), BF16),
            pltpu.VMEM((D, D), BF16),
            pltpu.VMEM((visits_dev * VB, D), BF16),
            pltpu.VMEM((visits_dev * VB, 2 * D), BF16),
            pltpu.VMEM((visits_dev, HEADS, VB), F32),
            pltpu.VMEM((visits_dev, HEADS, D), BF16),
            pltpu.SemaphoreType.DMA((3,)),
        ],
        compiler_params=params(),
        name="encode",
    )(visit_count, got, enc_gain.reshape(1, D), enc_qkv, enc_out)

    vecs = [vec] + [swap(vec, "mp", n_mp, k) for k in range(1, n_mp)]
    n_q = len(qkv_plan)
    all_vec, attended, qkv, prob = pl.pallas_call(
        functools.partial(project_kernel, n_mp, n_ev, qkv_plan),
        out_shape=(
            jax.ShapeDtypeStruct((group, DV), F32),
            jax.ShapeDtypeStruct((group, cols), BF16),
            jax.ShapeDtypeStruct((3, group, cols), BF16),
            jax.ShapeDtypeStruct((cols // VHDIM, group, group), F32),
        ),
        in_specs=[smem()] + [vmem()] * (3 + n_mp) + [hbm()] * n_q,
        out_specs=(vmem(),) * 4,
        scratch_shapes=[pltpu.VMEM(piece.shape, BF16) for piece in qkv_pieces]
        + [
            pltpu.VMEM((n_mp, VPAD, DV), F32),
            pltpu.VMEM((n_ev, group, width), BF16),
            pltpu.SemaphoreType.DMA((n_q,)),
        ],
        compiler_params=params(),
        name="project",
    )(where, meta, patient_row, visit_gain.reshape(1, DV), *vecs, *qkv_pieces)

    attns = [attended] + [swap(attended, "mp", n_mp, k) for k in range(1, n_mp)]
    n_f = len(ffn_plan)
    ffn_outs = pl.pallas_call(
        functools.partial(ffn_kernel, n_mp, n_ev, ffn_plan),
        out_shape=[jax.ShapeDtypeStruct((group, cols + LANES), BF16)] * n_mp
        + [jax.ShapeDtypeStruct((group, DV), F32)],
        in_specs=[smem()] + [vmem()] * 5 + [smem()] + [vmem()] * n_mp + [hbm()] * n_f,
        out_specs=[vmem()] * (n_mp + 1),
        scratch_shapes=[pltpu.VMEM(piece.shape, BF16) for piece in ffn_pieces]
        + [
            pltpu.VMEM((n_mp, group, cols), F32),
            pltpu.VMEM((n_ev, group, width), BF16),
            pltpu.VMEM((n_ev, group, width), F32),
            pltpu.SemaphoreType.DMA((n_f,)),
        ],
        compiler_params=params(),
        name="ffn",
    )(where, meta, all_vec, ffn_gain.reshape(1, DV), fw, head_t, head_bias, *attns, *ffn_pieces)
    mid = ffn_outs[n_mp]
    pays = [ffn_outs[0]] + [swap(ffn_outs[k], "mp", n_mp, k) for k in range(1, n_mp)]

    back_outs = pl.pallas_call(
        functools.partial(back_kernel, n_mp, n_ev, qkv_plan),
        out_shape=[jax.ShapeDtypeStruct((VPAD, D + LANES), BF16)] * n_mp
        + [jax.ShapeDtypeStruct((group, LANES), F32)],
        in_specs=[smem()] + [vmem()] * (8 + n_mp) + [hbm()] * n_q,
        out_specs=[vmem()] * (n_mp + 1),
        scratch_shapes=[pltpu.VMEM(piece.shape, BF16) for piece in qkv_pieces]
        + [
            pltpu.VMEM((n_ev, group, width), F32),
            pltpu.VMEM((n_mp, VPAD, D + LANES), F32),
            pltpu.SemaphoreType.DMA((n_q,)),
        ],
        compiler_params=params(),
        name="back",
    )(
        where, meta, all_vec, mid, ffn_gain.reshape(1, DV), visit_gain.reshape(1, DV), head_t, qkv,
        prob, *pays, *qkv_pieces,
    )
    outcomes = back_outs[n_mp][:, :2].reshape(n_mp, VPAD, 2)[:, :visits_dev].reshape(per_owner, 2)
    shares = [back_outs[0]] + [swap(back_outs[k], "mp", n_mp, k) for k in range(1, n_mp)]
    visit_grad = pl.pallas_call(
        functools.partial(finish_kernel, n_mp, visits_dev),
        out_shape=jax.ShapeDtypeStruct((VPAD, D), BF16),
        in_specs=[smem()] + [vmem()] * (1 + n_mp),
        out_specs=vmem(),
        compiler_params=params(),
        name="finish",
    )(visit_count, vec, *shares)

    table = gather_events(visit_grad, n_ev)
    slot = jnp.arange(n_ev * VPAD, dtype=jnp.int32)
    inner = slot % VPAD
    named = ((slot // VPAD) ^ e) * per_owner + m * visits_dev + inner
    named = jnp.where(inner < visits_dev, named, -2)
    chosen = (event_visit[:, None] == named[None, :]).astype(BF16)
    event_grads = dot(chosen, table).astype(BF16)
    return (outcomes, event_grads)


def solution(mesh):
    in_specs = (
        P(("events", "mp"), None),
        P(("events", "mp")),
        P(("events", "mp")),
        P("events"),
        P("events"),
        P("events"),
        P(),
        P(),
        P(),
        P(),
        P(None, "events", "mp"),
        P(),
        P("events", "mp"),
        P("mp", "events"),
        P(),
        P(),
    )
    out_specs = (P("events", None), P(("events", "mp"), None))
    return jax.shard_map(local, mesh=mesh, in_specs=in_specs, out_specs=out_specs, check_vma=False)
```

```python
import functools

import jax
import jax.numpy as jnp
from jax import lax
from jax.experimental import pallas as pl
from jax.experimental.pallas import tpu as pltpu
from jax.sharding import PartitionSpec as P

D = 1024
HEADS = 16
HDIM = 64
VB = 128
DV = 2048
VHDIM = 128
VPAD = 8
FW_ROWS = 16
LANES = 128
EPS = 1e-5
F32 = jnp.float32
BF16 = jnp.bfloat16
VMEM_LIMIT = 48 * 1024 * 1024

NT = (((1,), (1,)), ((), ()))
TN = (((0,), (0,)), ((), ()))
NN = (((1,), (0,)), ((), ()))


def dot(a, b, dims=NN):
    return lax.dot_general(a, b, dims, preferred_element_type=F32)


def vmem():
    return pl.BlockSpec(memory_space=pltpu.VMEM)


def smem():
    return pl.BlockSpec(memory_space=pltpu.SMEM)


def hbm():
    return pl.BlockSpec(memory_space=pl.ANY)


def params():
    return pltpu.CompilerParams(vmem_limit_bytes=VMEM_LIMIT)


def cost(micros):
    return pl.CostEstimate(
        flops=int(micros * 1e9) + 1, bytes_accessed=int(micros * 1e6) + 1, transcendentals=0
    )


def after(value, *others):
    return lax.optimization_barrier((value, *others))[0]


def strict_upper(rows):
    a = lax.broadcasted_iota(jnp.int32, (rows, rows), 0)
    b = lax.broadcasted_iota(jnp.int32, (rows, rows), 1)
    return (a < b).astype(BF16)


def pick_rows(position, first, count, rows):
    slots = lax.broadcasted_iota(jnp.int32, (count, rows), 0) + first
    return (slots == position).astype(BF16)


def pack_kernel(senders, per_owner, visits_dev, where_ref, ids_ref, x_ref, out_ref):
    rows = x_ref.shape[0]
    cap_rows = rows // senders
    ids = ids_ref[...]
    owners = lax.broadcasted_iota(jnp.int32, (senders, rows), 0)
    hot = (ids >= owners * per_owner) & (ids < (owners + 1) * per_owner)
    hot_f = hot.astype(F32)
    before = dot(hot.astype(BF16), strict_upper(rows))
    base = (owners * cap_rows + 1).astype(F32)
    position = (jnp.sum(hot_f * (base + before), axis=0, keepdims=True)).astype(jnp.int32) - 1
    first = (owners * per_owner + where_ref[1] * visits_dev).astype(F32)
    label = jnp.sum(hot_f * (ids.astype(F32) - first + 1.0), axis=0, keepdims=True)
    label = jnp.broadcast_to(label, (LANES, rows)).astype(BF16)
    step = rows // 3
    for c in range(3):
        chosen = pick_rows(position, c * step, step, rows)
        out_ref[c * step : (c + 1) * step, :D] = dot(chosen, x_ref[...]).astype(BF16)
        out_ref[c * step : (c + 1) * step, D:] = dot(chosen, label, NT).astype(BF16)


def fold_kernel(weight_ref, head_ref, qkv_ref, out_ref):
    rows, cols = qkv_ref.shape[1:]
    out_ref[:, :rows, :] = qkv_ref[...]
    folded = dot(head_ref[...], weight_ref[...], NT)
    folded = folded[0:2] + folded[2:4] + folded[4:6]
    one = folded.astype(BF16).astype(F32)
    two = (folded - one).astype(BF16).astype(F32)
    parts = (one, two, folded - one - two)
    chunks = folded.shape[1] // cols
    blank = jnp.zeros((FW_ROWS - 2 * chunks, cols), F32)
    for t in range(3):
        lines = [
            parts[t][j : j + 1, c * cols : (c + 1) * cols] for j in range(2) for c in range(chunks)
        ]
        out_ref[t, rows:, :] = jnp.concatenate(lines + [blank], axis=0).astype(BF16)


def encode_kernel(
    visits_dev,
    count_ref,
    got_ref,
    gain_ref,
    qkv_ref,
    proj_ref,
    vec_ref,
    wqk,
    wv,
    wo,
    normed,
    qk,
    pbar,
    ctx,
    sems,
):
    rows = got_ref.shape[0]
    slots = visits_dev * VB
    copies = [
        pltpu.make_async_copy(qkv_ref.at[:, : 2 * D], wqk, sems.at[0]),
        pltpu.make_async_copy(qkv_ref.at[:, 2 * D :], wv, sems.at[1]),
        pltpu.make_async_copy(proj_ref, wo, sems.at[2]),
    ]
    for copy in copies:
        copy.start()
    lane0 = (lax.broadcasted_iota(jnp.int32, (VPAD, LANES), 1) == 0).astype(BF16)
    label = dot(lane0, got_ref[:, D:], NT)[:1]
    visits = lax.broadcasted_iota(jnp.int32, (VPAD, rows), 0)
    hot = label == (visits + 1).astype(F32)
    hot_b = hot.astype(BF16)
    hot_f = hot.astype(F32)
    before = dot(hot_b, strict_upper(rows))
    base = (visits * VB + 1).astype(F32)
    position = (jnp.sum(hot_f * (base + before), axis=0, keepdims=True)).astype(jnp.int32) - 1
    sums = dot(hot_b, got_ref[:, :D])
    gain = gain_ref[...]
    step = 2 * VB
    for c in range(slots // step):
        part = dot(pick_rows(position, c * step, step, rows), got_ref[:, :D])
        scale = lax.rsqrt(jnp.mean(part * part, axis=-1, keepdims=True) + EPS)
        normed[c * step : (c + 1) * step, :] = (part * scale * gain).astype(BF16)
    copies[0].wait()
    wide = 512
    for c in range(2 * D // wide):
        cols = slice(c * wide, (c + 1) * wide)
        qk[:, cols] = dot(normed[...], wqk[:, cols]).astype(BF16)

    lanes = lax.broadcasted_iota(jnp.int32, (VB, LANES), 1)
    low = (lanes < HDIM).astype(F32) * HDIM ** (-0.5)
    high = (lanes >= HDIM).astype(F32) * HDIM ** (-0.5)
    key_slot = lax.broadcasted_iota(jnp.int32, (VB, 2 * VB), 0)
    query_lane = lax.broadcasted_iota(jnp.int32, (1, 2 * VB), 1)
    query_slot = jnp.where(query_lane >= VB, query_lane - VB, query_lane)
    rows8 = lax.broadcasted_iota(jnp.int32, (VPAD, 2 * VB), 0)
    lanes8 = lax.broadcasted_iota(jnp.int32, (VPAD, 2 * VB), 1)
    halves = ((lanes8 >= rows8 * VB) & (lanes8 < (rows8 + 1) * VB)).astype(BF16)

    def one_visit(v, carry):
        count = count_ref[v]
        at = pl.ds(pl.multiple_of(v * VB, VB), VB)
        live_key = key_slot < count
        weight = (query_slot < count).astype(F32) / count.astype(F32)
        for p in range(HEADS // 2):
            q = qk[at, p * LANES : (p + 1) * LANES].astype(F32)
            k = qk[at, D + p * LANES : D + (p + 1) * LANES]
            both = jnp.concatenate([(q * low).astype(BF16), (q * high).astype(BF16)], axis=0)
            scores = jnp.where(live_key, dot(k, both, NT), -1e30)
            top = jnp.max(scores, axis=0, keepdims=True)
            grown = jnp.exp(scores - top)
            total = jnp.sum(grown, axis=0, keepdims=True)
            shares = (grown * (weight / total)).astype(BF16)
            pbar[v, 2 * p : 2 * p + 2, :] = dot(halves, shares, NT)[:2]
        ctx[v] = dot(pbar[v].astype(BF16), normed[at, :]).astype(BF16)
        return carry

    lax.fori_loop(0, visits_dev, one_visit, 0)
    copies[1].wait()
    copies[2].wait()
    vals = dot(ctx[...].reshape(visits_dev * HEADS, D), wv[...]).reshape(visits_dev, HEADS, D)
    head_row = lax.broadcasted_iota(jnp.int32, (1, HEADS, D), 1) * HDIM
    col = lax.broadcasted_iota(jnp.int32, (1, HEADS, D), 2)
    own = (col >= head_row) & (col < head_row + HDIM)
    attended = jnp.sum(jnp.where(own, vals, 0.0), axis=1)
    attended = jnp.concatenate([attended, jnp.zeros((VPAD - visits_dev, D), F32)], axis=0)
    head_part = attended.astype(BF16)
    rest = (attended - head_part.astype(F32)).astype(BF16)
    mixed = dot(head_part, wo[...]) + dot(rest, wo[...])
    row = lax.broadcasted_iota(jnp.int32, (VPAD, 1), 0)
    inverse = jnp.zeros((VPAD, 1), F32)
    for v in range(visits_dev):
        inverse = jnp.where(row == v, 1.0 / count_ref[v].astype(F32), inverse)
    mean_input = sums * inverse
    vec_ref[:, :D] = (mean_input + mixed).astype(BF16)
    vec_ref[:, D:] = mean_input.astype(BF16)


def rms_factor(values):
    return lax.rsqrt(jnp.mean(values * values, axis=-1, keepdims=True) + EPS)


def fetch(pieces, scratch, sems):
    copies = [
        pltpu.make_async_copy(piece, buffer, sems.at[i])
        for i, (piece, buffer) in enumerate(zip(pieces, scratch, strict=True))
    ]
    for copy in copies:
        copy.start()
    return copies


def project_kernel(
    n_mp, n_ev, plan, where_ref, meta_ref, patient_ref, gain_ref, *refs
):
    n = len(plan)
    vec_in, refs = refs[:n_mp], refs[n_mp:]
    pieces, refs = refs[:n], refs[n:]
    vec_ref, attended_ref, qkv_ref, prob_ref, fw_ref = refs[:5]
    scratch, refs = refs[5 : 5 + n], refs[5 + n :]
    vec, blocks, sems = refs
    copies = fetch(pieces, scratch, sems)
    e, m = where_ref[0], where_ref[1]
    for k in range(n_mp):
        vec[m ^ k] = vec_in[k][...].astype(F32)
    rows = n_mp * VPAD
    full = vec[...].reshape(rows, DV)
    vec_ref[...] = full
    normed = (full * rms_factor(full) * gain_ref[...]).astype(BF16)
    width = DV // n_ev
    for j in range(n_ev):
        blocks[j] = normed[:, j * width : (j + 1) * width]
    cols = attended_ref.shape[1]
    totals = [jnp.zeros((rows, cols), F32) for _ in range(3)]
    fw = jnp.zeros(fw_ref.shape, F32)
    for i, (k, lo, size) in enumerate(plan):
        copies[i].wait()
        block = blocks[e ^ k][:, lo : lo + size]
        for t in range(3):
            totals[t] = totals[t] + dot(block, scratch[i][t, :size, :])
            if scratch[i].shape[1] > size:
                fw = fw + scratch[i][t, size:, :].astype(F32)
    fw_ref[...] = fw
    parts = [total.astype(BF16) for total in totals]
    for t in range(3):
        qkv_ref[t] = parts[t]
    q_at = lax.broadcasted_iota(jnp.int32, (rows, rows), 0)
    k_at = lax.broadcasted_iota(jnp.int32, (rows, rows), 1)
    allowed = (meta_ref[:, 2:3] == patient_ref[...]) & (k_at <= q_at)
    for h in range(cols // VHDIM):
        span = slice(h * VHDIM, (h + 1) * VHDIM)
        scores = dot(parts[0][:, span], parts[1][:, span], NT) * VHDIM ** (-0.5)
        scores = jnp.where(allowed, scores, -1e30)
        grown = jnp.exp(scores - jnp.max(scores, axis=-1, keepdims=True))
        prob = grown / jnp.sum(grown, axis=-1, keepdims=True)
        prob_ref[h] = prob
        attended_ref[:, span] = dot(prob.astype(BF16), parts[2][:, span]).astype(BF16)


def pack_scalars(columns, rows):
    lane = lax.broadcasted_iota(jnp.int32, (rows, LANES), 1)
    spread = jnp.zeros((rows, LANES), F32)
    for c, column in enumerate(columns):
        at = (lane == c) | (lane == 8 + c) | (lane == 16 + c)
        spread = jnp.where(at, column, spread)
    one = spread.astype(BF16).astype(F32)
    two = (spread - one).astype(BF16).astype(F32)
    three = spread - one - two
    return jnp.where(lane < 8, one, jnp.where(lane < 16, two, three)).astype(BF16)


def unpack_scalar(packed, c):
    return packed[:, c : c + 1] + packed[:, 8 + c : 9 + c] + packed[:, 16 + c : 17 + c]


def ffn_kernel(
    n_mp, n_ev, plan, where_ref, meta_ref, vec_ref, gain_ref, fw_ref, head_ref, bias_ref, *refs
):
    n = len(plan)
    attn_in, refs = refs[:n_mp], refs[n_mp:]
    pieces, refs = refs[:n], refs[n:]
    outs, refs = refs[:n_mp], refs[n_mp:]
    mid_ref, refs = refs[0], refs[1:]
    scratch, refs = refs[:n], refs[n:]
    attn, blocks, grads, sems = refs
    copies = fetch(pieces, scratch, sems)
    e, m = where_ref[0], where_ref[1]
    rows = vec_ref.shape[0]
    for k in range(n_mp):
        attn[m ^ k] = attn_in[k][...].astype(F32)
    mid = vec_ref[...] + jnp.concatenate([attn[k] for k in range(n_mp)], axis=1)
    mid_ref[...] = mid
    gain = gain_ref[...]
    normed = (mid * rms_factor(mid) * gain).astype(BF16)
    width = DV // n_ev
    for j in range(n_ev):
        blocks[j] = normed[:, j * width : (j + 1) * width]
    hidden = scratch[0].shape[1]
    pre = jnp.zeros((rows, hidden), F32)
    chunks = hidden // fw_ref.shape[1]
    fw = [
        jnp.concatenate([fw_ref[j * chunks + c : j * chunks + c + 1, :] for c in range(chunks)], axis=1)
        for j in range(2)
    ]
    for i, (k, lo, size) in enumerate(plan):
        copies[i].wait()
        pre = pre + dot(blocks[e ^ k][:, lo : lo + size], scratch[i][...])
    sigma = 1.0 / (1.0 + jnp.exp(-pre))
    act = (pre * sigma).astype(BF16).astype(F32)
    first = (m == 0).astype(F32)
    outcome = []
    for j in range(2):
        base = jnp.sum(mid * head_ref[j : j + 1, :], axis=-1, keepdims=True) + bias_ref[j]
        outcome.append(jnp.sum(act * fw[j], axis=-1, keepdims=True) + first * base)
    chosen = jnp.where(meta_ref[:, 0:1] > 0.5, fw[1], fw[0])
    slope = (chosen * sigma * (1.0 + pre * (1.0 - sigma))).astype(BF16)
    for i, (k, lo, size) in enumerate(plan):
        grads[e ^ k, :, lo : lo + size] = dot(slope, scratch[i][...], NT)
    moment = jnp.zeros((rows, 1), F32)
    for j in range(n_ev):
        span = slice(j * width, (j + 1) * width)
        moment = moment + jnp.sum(grads[j] * gain[:, span] * mid[:, span], axis=-1, keepdims=True)
    scalars = pack_scalars([outcome[0], outcome[1], moment], rows)
    each = n_ev // n_mp
    cols = DV // n_mp
    for k in range(n_mp):
        for j in range(each):
            outs[k][:, j * width : (j + 1) * width] = grads[(m ^ k) * each + j].astype(BF16)
        outs[k][:, cols:] = scalars


def back_kernel(
    n_mp, n_ev, plan, where_ref, meta_ref, vec_ref, mid_ref, gain_ref, vgain_ref, head_ref,
    qkv_ref, prob_ref, *refs
):
    n = len(plan)
    pay_in, refs = refs[:n_mp], refs[n_mp:]
    pieces, refs = refs[:n], refs[n:]
    outs, refs = refs[:n_mp], refs[n_mp:]
    outcome_ref, refs = refs[0], refs[1:]
    scratch, refs = refs[:n], refs[n:]
    grads, table, sems = refs
    copies = fetch(pieces, scratch, sems)
    e, m = where_ref[0], where_ref[1]
    rows = vec_ref.shape[0]
    cols = DV // n_mp
    total = pay_in[0][...].astype(F32)
    for k in range(1, n_mp):
        total = total + pay_in[k][...].astype(F32)
    packed = total[:, cols:]
    outcome = [unpack_scalar(packed, 0), unpack_scalar(packed, 1)]
    moment = unpack_scalar(packed, 2) * (1.0 / DV)
    lane = lax.broadcasted_iota(jnp.int32, (rows, LANES), 1)
    outcome_ref[...] = jnp.where(lane == 0, outcome[0], outcome[1])
    treated = meta_ref[:, 0:1] > 0.5
    delta = 4096.0 * (jnp.where(treated, outcome[1], outcome[0]) - meta_ref[:, 1:2])
    factor = rms_factor(mid_ref[...])
    at = pl.ds(pl.multiple_of(m * cols, cols), cols)
    mid = mid_ref[:, at]
    head = jnp.where(treated, head_ref[1:2, at], head_ref[0:1, at])
    scaled = total[:, :cols] * gain_ref[:, at]
    grad_mid = delta * (head + factor * (scaled - mid * (factor * factor * moment)))
    grad_c = grad_mid.astype(BF16)
    three = [[], [], []]
    for h in range(cols // VHDIM):
        span = slice(h * VHDIM, (h + 1) * VHDIM)
        prob = prob_ref[h]
        grad_p = dot(grad_c[:, span], qkv_ref[2, :, span], NT)
        grad_s = prob * (grad_p - jnp.sum(grad_p * prob, axis=-1, keepdims=True))
        grad_s = (grad_s * VHDIM ** (-0.5)).astype(BF16)
        three[0].append(dot(grad_s, qkv_ref[1, :, span]).astype(BF16))
        three[1].append(dot(grad_s, qkv_ref[0, :, span], TN).astype(BF16))
        three[2].append(dot(prob.astype(BF16), grad_c[:, span], TN).astype(BF16))
    three = [jnp.concatenate(parts, axis=1) for parts in three]
    for i, (k, lo, size) in enumerate(plan):
        copies[i].wait()
        part = dot(three[0], scratch[i][0, :size, :], NT)
        part = part + dot(three[1], scratch[i][1, :size, :], NT)
        part = part + dot(three[2], scratch[i][2, :size, :], NT)
        grads[e ^ k, :, lo : lo + size] = part
    width = DV // n_ev
    vec = vec_ref[...]
    spread = rms_factor(vec)
    moment = jnp.zeros((rows, 1), F32)
    for j in range(n_ev):
        span = slice(j * width, (j + 1) * width)
        scaled = grads[j] * vgain_ref[:, span]
        moment = moment + jnp.sum(scaled * vec[:, span], axis=-1, keepdims=True)
        if (j + 1) * width <= D:
            table[:, :, span] = (scaled * spread).reshape(n_mp, VPAD, width)

    @pl.when(m * cols < D)
    def _():
        here = pl.ds(pl.multiple_of(m * cols, cols), cols)
        table[:, :, here] = table[:, :, here] + grad_mid.reshape(n_mp, VPAD, cols)

    scalars = pack_scalars([moment], rows).astype(F32)
    table[:, :, D:] = scalars.reshape(n_mp, VPAD, LANES)
    for k in range(n_mp):
        outs[k][...] = table[m ^ k].astype(BF16)


def finish_kernel(n_mp, visits_dev, count_ref, own_ref, *refs):
    pays, out_ref = refs[:n_mp], refs[n_mp]
    total = pays[0][...].astype(F32)
    for k in range(1, n_mp):
        total = total + pays[k][...].astype(F32)
    vec = own_ref[...].astype(F32)
    spread = rms_factor(vec)
    moment = unpack_scalar(total[:, D:], 0) * (1.0 / DV)
    grad = total[:, :D] - vec[:, :D] * (spread * spread * spread * moment)
    row = lax.broadcasted_iota(jnp.int32, (VPAD, 1), 0)
    inverse = jnp.zeros((VPAD, 1), F32)
    for v in range(visits_dev):
        inverse = jnp.where(row == v, 1.0 / count_ref[v].astype(F32), inverse)
    out_ref[...] = (grad * inverse).astype(BF16)


def swap(x, axis, size, k):
    return lax.ppermute(x, axis, [(i, i ^ k) for i in range(size)])


def first_hop(shard, n_ev):
    if n_ev != 8:
        return [shard] + [swap(shard, "events", n_ev, k) for k in range(1, n_ev)]
    return [shard, swap(shard, "events", n_ev, 2), swap(shard, "events", n_ev, 4)]


def halves_kernel(half, low_ref, high_ref, low_out, high_out):
    low_out[...] = low_ref[...]
    high_out[...] = high_ref[:, half:, :] if len(high_ref.shape) == 3 else high_ref[...]


def halves_of(pieces, half):
    tail = pieces[1].shape[-1]
    if pieces[1].ndim == 2:
        low, high = (half, tail), (half, tail)
        block = [pl.BlockSpec(low, lambda i: (0, 0)), pl.BlockSpec(high, lambda i: (1, 0))]
    else:
        lead, rows = pieces[1].shape[:2]
        low, high = (lead, half, tail), (lead, rows - half, tail)
        block = [pl.BlockSpec(low, lambda i: (0, 0, 0)), vmem()]
    outs = [pl.BlockSpec(shape, lambda i, n=len(low): (0,) * n) for shape in (low, high)]
    return pl.pallas_call(
        functools.partial(halves_kernel, half),
        grid=(1,),
        out_shape=[jax.ShapeDtypeStruct(low, BF16), jax.ShapeDtypeStruct(high, BF16)],
        in_specs=block,
        out_specs=outs,
        compiler_params=params(),
        cost_estimate=cost(0),
        name="halves",
    )(pieces[1], pieces[2])


def second_hop(low, high, n_ev):
    return [swap(low, "events", n_ev, 4), swap(high, "events", n_ev, 2)]


def across(pieces, n_ev):
    return [swap(piece, "events", n_ev, 1) for piece in pieces]


def direct_plan(n_ev, width):
    order = range(n_ev) if n_ev != 8 else (0, 2, 4, 6, 1, 3, 5, 7)
    return [(k, 0, width) for k in order]


def hop_plan(n_ev, width):
    if n_ev != 8:
        return direct_plan(n_ev, width)
    half = width // 2
    near = [(0, 0, width), (2, 0, width), (4, 0, width), (6, 0, half), (6, half, half)]
    return near + [(k ^ 1, lo, size) for k, lo, size in near]


def gather_events(block, n_ev):
    if n_ev != 8:
        return jnp.concatenate(
            [block] + [swap(block, "events", n_ev, k) for k in range(1, n_ev)], axis=0
        )
    pair = jnp.concatenate([block, swap(block, "events", n_ev, 1)], axis=0)
    return jnp.concatenate([pair] + [swap(pair, "events", n_ev, k) for k in (2, 4, 6)], axis=0)


def local(
    event_x,
    event_visit,
    visit_count,
    visit_patient,
    treatment,
    outcome_target,
    enc_gain,
    enc_qkv,
    enc_out,
    visit_gain,
    visit_qkv,
    ffn_gain,
    ffn_in,
    ffn_out,
    head_weight,
    head_bias,
):
    n_ev = lax.axis_size("events")
    n_mp = lax.axis_size("mp")
    e = lax.axis_index("events")
    m = lax.axis_index("mp")
    rows_dev = event_x.shape[0]
    visits_dev = visit_count.shape[0]
    per_owner = visits_dev * n_mp
    group = n_mp * VPAD
    cols = DV // n_mp
    hidden = ffn_in.shape[1]
    where = jnp.stack([e, m]).astype(jnp.int32)
    ids = event_visit.reshape(1, rows_dev)

    send = pl.pallas_call(
        functools.partial(pack_kernel, n_ev, per_owner, visits_dev),
        out_shape=jax.ShapeDtypeStruct((rows_dev, D + LANES), BF16),
        in_specs=[smem(), vmem(), vmem()],
        out_specs=vmem(),
        compiler_params=params(),
        cost_estimate=cost(0),
        name="pack",
    )(where, ids, event_x)
    got = lax.all_to_all(
        send.reshape(n_ev, rows_dev // n_ev, D + LANES), "events", split_axis=0, concat_axis=0,
        tiled=True,
    ).reshape(rows_dev, D + LANES)

    ffn_first = first_hop(ffn_in, n_ev)

    head_t = head_weight.T
    width = DV // n_ev
    own_head = lax.dynamic_slice_in_dim(head_t, e * width, width, 1)
    head_hi = own_head.astype(BF16)
    head_mid = (own_head - head_hi.astype(F32)).astype(BF16)
    head_lo = (own_head - head_hi.astype(F32) - head_mid.astype(F32)).astype(BF16)
    heads = jnp.concatenate([head_hi, head_mid, head_lo, jnp.zeros((2, width), BF16)], axis=0)
    qkv_shard = pl.pallas_call(
        fold_kernel,
        out_shape=jax.ShapeDtypeStruct((3, width + FW_ROWS, cols), BF16),
        in_specs=[vmem()] * 3,
        out_specs=vmem(),
        compiler_params=params(),
        cost_estimate=cost(30),
        name="fold",
    )(ffn_out, heads, after(visit_qkv, *ffn_first[1:]))
    qkv_first = [qkv_shard] + first_hop(after(qkv_shard, got), n_ev)[1:]
    qkv_plan = hop_plan(n_ev, width)
    ffn_plan = hop_plan(n_ev, width)
    two_hops = n_ev == 8
    if two_hops:
        ffn_halves = halves_of(ffn_first, width // 2)
        ffn_far = across(ffn_first, n_ev)
        qkv_far = across(qkv_first[:1], n_ev)
        got = after(got, *ffn_far, *ffn_halves, *qkv_far)

    def spread_rows(values, fill):
        values = values.astype(F32).reshape(n_mp, visits_dev)
        return jnp.pad(values, ((0, 0), (0, VPAD - visits_dev)), constant_values=fill).reshape(group)

    patient = spread_rows(visit_patient, -1.0)
    meta = jnp.stack(
        [spread_rows(treatment, 0.0), spread_rows(outcome_target, 0.0), patient], axis=1
    )
    patient_row = patient.reshape(1, group)

    vec = pl.pallas_call(
        functools.partial(encode_kernel, visits_dev),
        out_shape=jax.ShapeDtypeStruct((VPAD, DV), BF16),
        in_specs=[smem(), vmem(), vmem(), hbm(), hbm()],
        out_specs=vmem(),
        scratch_shapes=[
            pltpu.VMEM((D, 2 * D), BF16),
            pltpu.VMEM((D, D), BF16),
            pltpu.VMEM((D, D), BF16),
            pltpu.VMEM((visits_dev * VB, D), BF16),
            pltpu.VMEM((visits_dev * VB, 2 * D), BF16),
            pltpu.VMEM((visits_dev, HEADS, VB), F32),
            pltpu.VMEM((visits_dev, HEADS, D), BF16),
            pltpu.SemaphoreType.DMA((3,)),
        ],
        compiler_params=params(),
        cost_estimate=cost(0),
        name="encode",
    )(visit_count, got, enc_gain.reshape(1, D), enc_qkv, enc_out)

    if two_hops:
        qkv_halves = halves_of([qkv_first[0]] + [after(p, vec) for p in qkv_first[1:]], width // 2)
        vec = after(vec, *qkv_halves)
    vecs = [vec] + [swap(vec, "mp", n_mp, k) for k in range(1, n_mp)]
    if two_hops:
        qkv_second = second_hop(*qkv_halves, n_ev)
        ffn_second = second_hop(*[after(piece, *vecs[1:]) for piece in ffn_halves], n_ev)
        qkv_far += across([after(piece, *vecs[1:]) for piece in qkv_first[1:]], n_ev)
        qkv_pieces = qkv_first + qkv_second + qkv_far + across(qkv_second, n_ev)
    else:
        qkv_pieces = qkv_first
    n_q = len(qkv_plan)
    all_vec, attended, qkv, prob, fw = pl.pallas_call(
        functools.partial(project_kernel, n_mp, n_ev, qkv_plan),
        out_shape=(
            jax.ShapeDtypeStruct((group, DV), F32),
            jax.ShapeDtypeStruct((group, cols), BF16),
            jax.ShapeDtypeStruct((3, group, cols), BF16),
            jax.ShapeDtypeStruct((cols // VHDIM, group, group), F32),
            jax.ShapeDtypeStruct((FW_ROWS, cols), F32),
        ),
        in_specs=[smem()] + [vmem()] * (3 + n_mp) + [hbm()] * n_q,
        out_specs=(vmem(),) * 5,
        scratch_shapes=[pltpu.VMEM(piece.shape, BF16) for piece in qkv_pieces]
        + [
            pltpu.VMEM((n_mp, VPAD, DV), F32),
            pltpu.VMEM((n_ev, group, width), BF16),
            pltpu.SemaphoreType.DMA((n_q,)),
        ],
        compiler_params=params(),
        cost_estimate=cost(0),
        name="project",
    )(where, meta, patient_row, visit_gain.reshape(1, DV), *vecs, *qkv_pieces)

    attns = [attended] + [swap(attended, "mp", n_mp, k) for k in range(1, n_mp)]
    if two_hops:
        ffn_second = [after(piece, *attns[1:]) for piece in ffn_second]
        ffn_pieces = ffn_first + ffn_second + ffn_far + across(ffn_second, n_ev)
    else:
        ffn_pieces = ffn_first
    n_f = len(ffn_plan)
    ffn_outs = pl.pallas_call(
        functools.partial(ffn_kernel, n_mp, n_ev, ffn_plan),
        out_shape=[jax.ShapeDtypeStruct((group, cols + LANES), BF16)] * n_mp
        + [jax.ShapeDtypeStruct((group, DV), F32)],
        in_specs=[smem()] + [vmem()] * 5 + [smem()] + [vmem()] * n_mp + [hbm()] * n_f,
        out_specs=[vmem()] * (n_mp + 1),
        scratch_shapes=[pltpu.VMEM(piece.shape, BF16) for piece in ffn_pieces]
        + [
            pltpu.VMEM((n_mp, group, cols), F32),
            pltpu.VMEM((n_ev, group, width), BF16),
            pltpu.VMEM((n_ev, group, width), F32),
            pltpu.SemaphoreType.DMA((n_f,)),
        ],
        compiler_params=params(),
        cost_estimate=cost(7),
        name="ffn",
    )(where, meta, all_vec, ffn_gain.reshape(1, DV), fw, head_t, head_bias, *attns, *ffn_pieces)
    mid = ffn_outs[n_mp]
    pays = [ffn_outs[0]] + [swap(ffn_outs[k], "mp", n_mp, k) for k in range(1, n_mp)]

    back_outs = pl.pallas_call(
        functools.partial(back_kernel, n_mp, n_ev, qkv_plan),
        out_shape=[jax.ShapeDtypeStruct((VPAD, D + LANES), BF16)] * n_mp
        + [jax.ShapeDtypeStruct((group, LANES), F32)],
        in_specs=[smem()] + [vmem()] * (8 + n_mp) + [hbm()] * n_q,
        out_specs=[vmem()] * (n_mp + 1),
        scratch_shapes=[pltpu.VMEM(piece.shape, BF16) for piece in qkv_pieces]
        + [
            pltpu.VMEM((n_ev, group, width), F32),
            pltpu.VMEM((n_mp, VPAD, D + LANES), F32),
            pltpu.SemaphoreType.DMA((n_q,)),
        ],
        compiler_params=params(),
        cost_estimate=cost(7),
        name="back",
    )(
        where, meta, all_vec, mid, ffn_gain.reshape(1, DV), visit_gain.reshape(1, DV), head_t, qkv,
        prob, *pays, *qkv_pieces,
    )
    outcomes = back_outs[n_mp][:, :2].reshape(n_mp, VPAD, 2)[:, :visits_dev].reshape(per_owner, 2)
    shares = [back_outs[0]] + [swap(back_outs[k], "mp", n_mp, k) for k in range(1, n_mp)]
    visit_grad = pl.pallas_call(
        functools.partial(finish_kernel, n_mp, visits_dev),
        out_shape=jax.ShapeDtypeStruct((VPAD, D), BF16),
        in_specs=[smem()] + [vmem()] * (1 + n_mp),
        out_specs=vmem(),
        compiler_params=params(),
        cost_estimate=cost(0),
        name="finish",
    )(visit_count, vec, *shares)

    table = gather_events(visit_grad, n_ev)
    slot = jnp.arange(n_ev * VPAD, dtype=jnp.int32)
    inner = slot % VPAD
    named = ((slot // VPAD) ^ e) * per_owner + m * visits_dev + inner
    named = jnp.where(inner < visits_dev, named, -2)
    chosen = (event_visit[:, None] == named[None, :]).astype(BF16)
    event_grads = dot(chosen, table).astype(BF16)
    return (outcomes, event_grads)


def solution(mesh):
    in_specs = (
        P(("events", "mp"), None),
        P(("events", "mp")),
        P(("events", "mp")),
        P("events"),
        P("events"),
        P("events"),
        P(),
        P(),
        P(),
        P(),
        P(None, "events", "mp"),
        P(),
        P("events", "mp"),
        P("mp", "events"),
        P(),
        P(),
    )
    out_specs = (P("events", None), P(("events", "mp"), None))
    return jax.shard_map(local, mesh=mesh, in_specs=in_specs, out_specs=out_specs, check_vma=False)
```

```python
import functools

import jax
import jax.numpy as jnp
from jax import lax
from jax.experimental import pallas as pl
from jax.experimental.pallas import tpu as pltpu
from jax.sharding import PartitionSpec as P

D = 1024
HEADS = 16
HDIM = 64
VB = 128
DV = 2048
VHDIM = 128
VPAD = 8
FW_ROWS = 16
SNUG = 48
LANES = 128
EPS = 1e-5
F32 = jnp.float32
BF16 = jnp.bfloat16

NT = (((1,), (1,)), ((), ()))
TN = (((0,), (0,)), ((), ()))
NN = (((1,), (0,)), ((), ()))


def dot(a, b, dims=NN):
    return lax.dot_general(a, b, dims, preferred_element_type=F32)


def vmem():
    return pl.BlockSpec(memory_space=pltpu.VMEM)


def smem():
    return pl.BlockSpec(memory_space=pltpu.SMEM)


def hbm():
    return pl.BlockSpec(memory_space=pltpu.HBM)


def params(mib):
    return pltpu.CompilerParams(vmem_limit_bytes=int(mib * 1024) * 1024)


def cost(micros):
    return pl.CostEstimate(
        flops=int(micros * 1e9) + 1, bytes_accessed=int(micros * 1e6) + 1, transcendentals=0
    )


def after(value, *others):
    return lax.optimization_barrier((value, *others))[0]


def strict_upper(rows):
    a = lax.broadcasted_iota(jnp.int32, (rows, rows), 0)
    b = lax.broadcasted_iota(jnp.int32, (rows, rows), 1)
    return (a < b).astype(BF16)


def pick_rows(position, first, count, rows):
    slots = lax.broadcasted_iota(jnp.int32, (count, rows), 0) + first
    return (slots == position).astype(BF16)


def pack_kernel(senders, per_owner, visits_dev, where_ref, ids_ref, x_hbm, out_ref, x_ref, sem):
    copy = pltpu.make_async_copy(x_hbm, x_ref, sem)
    copy.start()
    rows = x_ref.shape[0]
    cap_rows = rows // senders
    ids = jnp.concatenate([ids_ref[i : i + 1, :] for i in range(ids_ref.shape[0])], axis=1)
    owners = lax.broadcasted_iota(jnp.int32, (senders, rows), 0)
    hot = (ids >= owners * per_owner) & (ids < (owners + 1) * per_owner)
    hot_f = hot.astype(F32)
    before = dot(hot.astype(BF16), strict_upper(rows))
    base = (owners * cap_rows + 1).astype(F32)
    position = (jnp.sum(hot_f * (base + before), axis=0, keepdims=True)).astype(jnp.int32) - 1
    first = (owners * per_owner + where_ref[1] * visits_dev).astype(F32)
    label = jnp.sum(hot_f * (ids.astype(F32) - first + 1.0), axis=0, keepdims=True)
    label = jnp.broadcast_to(label, (LANES, rows)).astype(BF16)
    copy.wait()
    step = rows // 3
    for c in range(3):
        chosen = pick_rows(position, c * step, step, rows)
        out_ref[c * step : (c + 1) * step, :D] = dot(chosen, x_ref[...]).astype(BF16)
        out_ref[c * step : (c + 1) * step, D:] = dot(chosen, label, NT).astype(BF16)


def prep_kernel(visits_dev, patient_ref, treat_ref, target_ref, meta_ref, row_ref):
    rows, lanes = meta_ref.shape
    slot = lax.broadcasted_iota(jnp.int32, (rows, lanes), 0)
    lane = lax.broadcasted_iota(jnp.int32, (rows, lanes), 1)
    place = lax.broadcasted_iota(jnp.int32, (VPAD, rows), 1)
    meta = jnp.where(lane == 2, -1.0, jnp.zeros((rows, lanes), F32))
    line = jnp.full((VPAD, rows), -1.0, F32)
    for g in range(patient_ref.shape[0]):
        at = (g // visits_dev) * VPAD + g % visits_dev
        patient = patient_ref[g].astype(F32)
        here = jnp.where(
            lane == 0, treat_ref[g].astype(F32), jnp.where(lane == 1, target_ref[g], patient)
        )
        meta = jnp.where((slot == at) & (lane < 3), here, meta)
        line = jnp.where(place == at, patient, line)
    meta_ref[...] = meta
    row_ref[...] = line


def fold_kernel(weight_ref, head_ref, qkv_ref, out_ref):
    rows, cols = qkv_ref.shape[1:]
    out_ref[:, :rows, :] = qkv_ref[...]
    folded = dot(head_ref[...], weight_ref[...], NT)
    folded = folded[0:2] + folded[2:4] + folded[4:6]
    one = folded.astype(BF16).astype(F32)
    two = (folded - one).astype(BF16).astype(F32)
    parts = (one, two, folded - one - two)
    chunks = folded.shape[1] // cols
    blank = jnp.zeros((FW_ROWS - 2 * chunks, cols), F32)
    for t in range(3):
        lines = [
            parts[t][j : j + 1, c * cols : (c + 1) * cols] for j in range(2) for c in range(chunks)
        ]
        out_ref[t, rows:, :] = jnp.concatenate(lines + [blank], axis=0).astype(BF16)


def encode_kernel(
    visits_dev,
    count_ref,
    gain_ref,
    got_hbm,
    qkv_ref,
    proj_ref,
    vec_ref,
    got_ref,
    wqk,
    wv,
    wo,
    normed,
    qk,
    pbar,
    ctx,
    sems,
):
    rows = got_ref.shape[0]
    slots = visits_dev * VB
    inputs = [
        pltpu.make_async_copy(got_hbm.at[:, D:], got_ref.at[:, D:], sems.at[3]),
        pltpu.make_async_copy(got_hbm.at[:, :D], got_ref.at[:, :D], sems.at[4]),
    ]
    copies = [
        pltpu.make_async_copy(qkv_ref.at[:, : 2 * D], wqk, sems.at[0]),
        pltpu.make_async_copy(qkv_ref.at[:, 2 * D :], wv, sems.at[1]),
        pltpu.make_async_copy(proj_ref, wo, sems.at[2]),
    ]
    for copy in inputs + copies:
        copy.start()
    inputs[0].wait()
    lane0 = (lax.broadcasted_iota(jnp.int32, (VPAD, LANES), 1) == 0).astype(BF16)
    label = dot(lane0, got_ref[:, D:], NT)[:1]
    visits = lax.broadcasted_iota(jnp.int32, (VPAD, rows), 0)
    hot = label == (visits + 1).astype(F32)
    hot_b = hot.astype(BF16)
    hot_f = hot.astype(F32)
    before = dot(hot_b, strict_upper(rows))
    base = (visits * VB + 1).astype(F32)
    position = (jnp.sum(hot_f * (base + before), axis=0, keepdims=True)).astype(jnp.int32) - 1
    inputs[1].wait()
    sums = dot(hot_b, got_ref[:, :D])
    gain = gain_ref[...]
    step = 2 * VB
    for c in range(slots // step):
        part = dot(pick_rows(position, c * step, step, rows), got_ref[:, :D])
        scale = lax.rsqrt(jnp.mean(part * part, axis=-1, keepdims=True) + EPS)
        normed[c * step : (c + 1) * step, :] = (part * scale * gain).astype(BF16)
    copies[0].wait()
    wide = 512
    for c in range(2 * D // wide):
        cols = slice(c * wide, (c + 1) * wide)
        qk[:, cols] = dot(normed[...], wqk[:, cols]).astype(BF16)

    lanes = lax.broadcasted_iota(jnp.int32, (VB, LANES), 1)
    low = (lanes < HDIM).astype(F32) * HDIM ** (-0.5)
    high = (lanes >= HDIM).astype(F32) * HDIM ** (-0.5)
    key_slot = lax.broadcasted_iota(jnp.int32, (VB, 2 * VB), 0)
    query_lane = lax.broadcasted_iota(jnp.int32, (1, 2 * VB), 1)
    query_slot = jnp.where(query_lane >= VB, query_lane - VB, query_lane)
    rows8 = lax.broadcasted_iota(jnp.int32, (VPAD, 2 * VB), 0)
    lanes8 = lax.broadcasted_iota(jnp.int32, (VPAD, 2 * VB), 1)
    halves = ((lanes8 >= rows8 * VB) & (lanes8 < (rows8 + 1) * VB)).astype(BF16)

    def one_visit(v, carry):
        count = count_ref[v]
        at = pl.ds(pl.multiple_of(v * VB, VB), VB)
        live_key = key_slot < count
        weight = (query_slot < count).astype(F32) / count.astype(F32)
        for p in range(HEADS // 2):
            q = qk[at, p * LANES : (p + 1) * LANES].astype(F32)
            k = qk[at, D + p * LANES : D + (p + 1) * LANES]
            both = jnp.concatenate([(q * low).astype(BF16), (q * high).astype(BF16)], axis=0)
            scores = jnp.where(live_key, dot(k, both, NT), -1e30)
            top = jnp.max(scores, axis=0, keepdims=True)
            grown = jnp.exp(scores - top)
            total = jnp.sum(grown, axis=0, keepdims=True)
            shares = (grown * (weight / total)).astype(BF16)
            pbar[v, 2 * p : 2 * p + 2, :] = dot(halves, shares, NT)[:2]
        ctx[v] = dot(pbar[v].astype(BF16), normed[at, :]).astype(BF16)
        return carry

    lax.fori_loop(0, visits_dev, one_visit, 0)
    copies[1].wait()
    copies[2].wait()
    vals = dot(ctx[...].reshape(visits_dev * HEADS, D), wv[...]).reshape(visits_dev, HEADS, D)
    head_row = lax.broadcasted_iota(jnp.int32, (1, HEADS, D), 1) * HDIM
    col = lax.broadcasted_iota(jnp.int32, (1, HEADS, D), 2)
    own = (col >= head_row) & (col < head_row + HDIM)
    attended = jnp.sum(jnp.where(own, vals, 0.0), axis=1)
    attended = jnp.concatenate([attended, jnp.zeros((VPAD - visits_dev, D), F32)], axis=0)
    head_part = attended.astype(BF16)
    rest = (attended - head_part.astype(F32)).astype(BF16)
    mixed = dot(head_part, wo[...]) + dot(rest, wo[...])
    row = lax.broadcasted_iota(jnp.int32, (VPAD, 1), 0)
    inverse = jnp.zeros((VPAD, 1), F32)
    for v in range(visits_dev):
        inverse = jnp.where(row == v, 1.0 / count_ref[v].astype(F32), inverse)
    mean_input = sums * inverse
    vec_ref[:, :D] = (mean_input + mixed).astype(BF16)
    vec_ref[:, D:] = mean_input.astype(BF16)


def rms_factor(values):
    return lax.rsqrt(jnp.mean(values * values, axis=-1, keepdims=True) + EPS)


def fetch(pieces, scratch, sems, first=0):
    copies = [
        pltpu.make_async_copy(piece, buffer, sems.at[first + i])
        for i, (piece, buffer) in enumerate(zip(pieces, scratch, strict=True))
    ]
    for copy in copies:
        copy.start()
    return copies


def project_kernel(n_mp, n_ev, plan, where_ref, *refs):
    n = len(plan)
    vec_in, (gain_ref, meta_ref, patient_ref), refs = refs[:n_mp], refs[n_mp : n_mp + 3], refs[n_mp + 3 :]
    pieces, refs = refs[:n], refs[n:]
    attended_ref, state, refs = refs[0], refs[1], refs[2:]
    scratch, refs = refs[:n], refs[n:]
    vec, blocks, sems, kept, out_sems = refs
    copies = fetch(pieces, scratch, sems)
    e, m = where_ref[0], where_ref[1]
    cols = attended_ref.shape[1]
    saves = [
        pltpu.make_async_copy(kept.at[:, lo:hi], state.at[:, lo:hi], out_sems.at[i])
        for i, (lo, hi) in enumerate(state_spans(cols))
    ]
    for k in range(n_mp):
        vec[m ^ k] = vec_in[k][...]
    rows = n_mp * VPAD
    full = vec[...].astype(F32).reshape(rows, DV)
    kept[:, :DV] = full
    saves[0].start()
    normed = (full * rms_factor(full) * gain_ref[...]).astype(BF16)
    width = DV // n_ev
    for j in range(n_ev):
        blocks[j] = normed[:, j * width : (j + 1) * width]
    totals = [jnp.zeros((rows, cols), F32) for _ in range(3)]
    fw = jnp.zeros((FW_ROWS, cols), F32)
    for i, (k, lo, size) in enumerate(plan):
        copies[i].wait()
        block = blocks[e ^ k][:, lo : lo + size]
        for t in range(3):
            totals[t] = totals[t] + dot(block, scratch[i][t, :size, :])
            if scratch[i].shape[1] > size:
                fw = fw + scratch[i][t, size:, :].astype(F32)
    parts = [total.astype(BF16) for total in totals]
    for t in range(3):
        kept[:, DV + t * cols : DV + (t + 1) * cols] = parts[t].astype(F32)
    kept[:FW_ROWS, DV + 3 * cols : DV + 4 * cols] = fw
    saves[1].start()
    q_at = lax.broadcasted_iota(jnp.int32, (rows, rows), 0)
    k_at = lax.broadcasted_iota(jnp.int32, (rows, rows), 1)
    allowed = (meta_ref[:, 2:3] == patient_ref[0:1, :]) & (k_at <= q_at)
    for h in range(cols // VHDIM):
        span = slice(h * VHDIM, (h + 1) * VHDIM)
        scores = dot(parts[0][:, span], parts[1][:, span], NT) * VHDIM ** (-0.5)
        scores = jnp.where(allowed, scores, -1e30)
        grown = jnp.exp(scores - jnp.max(scores, axis=-1, keepdims=True))
        prob = grown / jnp.sum(grown, axis=-1, keepdims=True)
        kept[:, DV + 4 * cols + h * rows : DV + 4 * cols + (h + 1) * rows] = prob
        attended_ref[:, span] = dot(prob.astype(BF16), parts[2][:, span]).astype(BF16)
    saves[2].start()
    for save in saves:
        save.wait()


def state_spans(cols):
    return ((0, DV), (DV, DV + 4 * cols), (DV + 4 * cols, DV + 4 * cols + LANES))


def pack_scalars(columns, rows):
    lane = lax.broadcasted_iota(jnp.int32, (rows, LANES), 1)
    spread = jnp.zeros((rows, LANES), F32)
    for c, column in enumerate(columns):
        at = (lane == c) | (lane == 8 + c) | (lane == 16 + c)
        spread = jnp.where(at, column, spread)
    one = spread.astype(BF16).astype(F32)
    two = (spread - one).astype(BF16).astype(F32)
    three = spread - one - two
    return jnp.where(lane < 8, one, jnp.where(lane < 16, two, three)).astype(BF16)


def unpack_scalar(packed, c):
    return packed[:, c : c + 1] + packed[:, 8 + c : 9 + c] + packed[:, 16 + c : 17 + c]


def ffn_kernel(
    n_mp, n_ev, plan, where_ref, bias_ref, gain_ref, meta_ref, head_ref, *refs
):
    n = len(plan)
    attn_in, state, refs = refs[:n_mp], refs[n_mp], refs[n_mp + 1 :]
    pieces, refs = refs[:n], refs[n:]
    outs, mid_ref, refs = refs[:n_mp], refs[n_mp], refs[n_mp + 1 :]
    scratch, refs = refs[:n], refs[n:]
    attn, vec_ref, fw_ref, blocks, grads, sems = refs
    e, m = where_ref[0], where_ref[1]
    cols = DV // n_mp
    fw_at = DV + 3 * cols
    sources = [state.at[:, :DV], state.at[:FW_ROWS, fw_at : fw_at + cols]]
    small = fetch(sources, [vec_ref, fw_ref], sems, n)
    copies = fetch(pieces, scratch, sems)
    for k in range(n_mp):
        attn[m ^ k] = attn_in[k][...]
    for copy in small:
        copy.wait()
    rows = vec_ref.shape[0]
    mid = vec_ref[...] + jnp.concatenate([attn[k] for k in range(n_mp)], axis=1).astype(F32)
    at = pl.ds(pl.multiple_of(m * cols, cols), cols)
    factor = rms_factor(mid)
    mid_ref[:, :cols] = vec_ref[:, at] + attn[m].astype(F32)
    mid_ref[:, cols:] = jnp.broadcast_to(factor, (rows, LANES))
    gain = gain_ref[...]
    normed = (mid * factor * gain).astype(BF16)
    width = DV // n_ev
    for j in range(n_ev):
        blocks[j] = normed[:, j * width : (j + 1) * width]
    hidden = scratch[0].shape[1]
    pre = jnp.zeros((rows, hidden), F32)
    chunks = hidden // fw_ref.shape[1]
    fw = [
        jnp.concatenate([fw_ref[j * chunks + c : j * chunks + c + 1, :] for c in range(chunks)], axis=1)
        for j in range(2)
    ]
    for i, (k, lo, size) in enumerate(plan):
        copies[i].wait()
        pre = pre + dot(blocks[e ^ k][:, lo : lo + size], scratch[i][...])
    sigma = 1.0 / (1.0 + jnp.exp(-pre))
    act = (pre * sigma).astype(BF16).astype(F32)
    first = (m == 0).astype(F32)
    outcome = []
    for j in range(2):
        base = jnp.sum(mid * head_ref[j : j + 1, :], axis=-1, keepdims=True) + bias_ref[j]
        outcome.append(jnp.sum(act * fw[j], axis=-1, keepdims=True) + first * base)
    chosen = jnp.where(meta_ref[:, 0:1] > 0.5, fw[1], fw[0])
    slope = (chosen * sigma * (1.0 + pre * (1.0 - sigma))).astype(BF16)
    for i, (k, lo, size) in enumerate(plan):
        grads[e ^ k, :, lo : lo + size] = dot(slope, scratch[i][...], NT)
    moment = jnp.zeros((rows, 1), F32)
    for j in range(n_ev):
        span = slice(j * width, (j + 1) * width)
        moment = moment + jnp.sum(grads[j] * gain[:, span] * mid[:, span], axis=-1, keepdims=True)
    scalars = pack_scalars([outcome[0], outcome[1], moment], rows)
    each = n_ev // n_mp
    for k in range(n_mp):
        for j in range(each):
            outs[k][:, j * width : (j + 1) * width] = grads[(m ^ k) * each + j].astype(BF16)
        outs[k][:, cols:] = scalars


def back_kernel(
    n_mp, n_ev, plan, where_ref, mid_ref, meta_ref, gain_ref, vgain_ref, head_ref, *refs
):
    n = len(plan)
    pay_in, state, refs = refs[:n_mp], refs[n_mp], refs[n_mp + 1 :]
    pieces, refs = refs[:n], refs[n:]
    outs, outcome_ref, coef_ref, refs = refs[:n_mp], refs[n_mp], refs[n_mp + 1], refs[n_mp + 2 :]
    scratch, refs = refs[:n], refs[n:]
    kept, grads, table, sems = refs
    (stored,) = fetch([state], [kept], sems, n)
    copies = fetch(pieces, scratch, sems)
    e, m = where_ref[0], where_ref[1]
    rows = mid_ref.shape[0]
    cols = DV // n_mp
    total = pay_in[0][...].astype(F32)
    for k in range(1, n_mp):
        total = total + pay_in[k][...].astype(F32)
    packed = total[:, cols:]
    outcome = [unpack_scalar(packed, 0), unpack_scalar(packed, 1)]
    moment = unpack_scalar(packed, 2) * (1.0 / DV)
    lane = lax.broadcasted_iota(jnp.int32, (rows, LANES), 1)
    outcome_ref[...] = jnp.where(lane == 0, outcome[0], outcome[1])
    treated = meta_ref[:, 0:1] > 0.5
    delta = 4096.0 * (jnp.where(treated, outcome[1], outcome[0]) - meta_ref[:, 1:2])
    factor = mid_ref[:, cols : cols + 1]
    at = pl.ds(pl.multiple_of(m * cols, cols), cols)
    mid = mid_ref[:, :cols]
    head = jnp.where(treated, head_ref[1:2, at], head_ref[0:1, at])
    scaled = total[:, :cols] * gain_ref[:, at]
    grad_mid = delta * (head + factor * (scaled - mid * (factor * factor * moment)))
    grad_c = grad_mid.astype(BF16)
    stored.wait()
    queries, keys, values = (
        kept[:, DV + t * cols : DV + (t + 1) * cols].astype(BF16) for t in range(3)
    )
    three = [[], [], []]
    for h in range(cols // VHDIM):
        span = slice(h * VHDIM, (h + 1) * VHDIM)
        prob = kept[:, DV + 4 * cols + h * rows : DV + 4 * cols + (h + 1) * rows]
        grad_p = dot(grad_c[:, span], values[:, span], NT)
        grad_s = prob * (grad_p - jnp.sum(grad_p * prob, axis=-1, keepdims=True))
        grad_s = (grad_s * VHDIM ** (-0.5)).astype(BF16)
        three[0].append(dot(grad_s, keys[:, span]).astype(BF16))
        three[1].append(dot(grad_s, queries[:, span], TN).astype(BF16))
        three[2].append(dot(prob.astype(BF16), grad_c[:, span], TN).astype(BF16))
    three = [jnp.concatenate(parts, axis=1) for parts in three]
    for i, (k, lo, size) in enumerate(plan):
        copies[i].wait()
        part = dot(three[0], scratch[i][0, :size, :], NT)
        part = part + dot(three[1], scratch[i][1, :size, :], NT)
        part = part + dot(three[2], scratch[i][2, :size, :], NT)
        grads[e ^ k, :, lo : lo + size] = part
    width = DV // n_ev
    vec = kept[:, :DV]
    spread = rms_factor(vec)
    moment = jnp.zeros((rows, 1), F32)
    for j in range(n_ev):
        span = slice(j * width, (j + 1) * width)
        scaled = grads[j] * vgain_ref[:, span]
        moment = moment + jnp.sum(scaled * vec[:, span], axis=-1, keepdims=True)
        if (j + 1) * width <= D:
            table[:, :, span] = (scaled * spread).reshape(n_mp, VPAD, width)

    @pl.when(m * cols < D)
    def _():
        here = pl.ds(pl.multiple_of(m * cols, cols), cols)
        table[:, :, here] = table[:, :, here] + grad_mid.reshape(n_mp, VPAD, cols)

    scalars = pack_scalars([moment], rows).astype(F32)
    table[:, :, D:] = scalars.reshape(n_mp, VPAD, LANES)
    for k in range(n_mp):
        outs[k][...] = table[m ^ k].astype(BF16)
    table[:, :, :D] = (vec[:, :D] * (spread * spread * spread * (1.0 / DV))).reshape(n_mp, VPAD, D)
    coef_ref[...] = table[m][:, :D]


def finish_kernel(n_mp, visits_dev, count_ref, coef_ref, *refs):
    pays, out_ref = refs[:n_mp], refs[n_mp]
    total = pays[0][...].astype(F32)
    for k in range(1, n_mp):
        total = total + pays[k][...].astype(F32)
    grad = total[:, :D] - coef_ref[...] * unpack_scalar(total[:, D:], 0)
    row = lax.broadcasted_iota(jnp.int32, (VPAD, 1), 0)
    inverse = jnp.zeros((VPAD, 1), F32)
    for v in range(visits_dev):
        inverse = jnp.where(row == v, 1.0 / count_ref[v].astype(F32), inverse)
    out_ref[...] = (grad * inverse).astype(BF16).astype(F32)


def spread_kernel(n_ev, pick, *refs):
    tables, out, rows_ref, out_sems = refs[:n_ev], *refs[n_ev:]
    table = jnp.concatenate([each[...] for each in tables], axis=0).astype(BF16)
    rows = rows_ref.shape[0]
    step = rows // 3
    saves = []
    for c in range(3):
        span = slice(c * step, (c + 1) * step)
        rows_ref[span, :] = dot(pick[span, :], table).astype(BF16)
        saves.append(pltpu.make_async_copy(rows_ref.at[span, :], out.at[span, :], out_sems.at[c]))
        saves[c].start()
    for save in saves:
        save.wait()


def swap(x, axis, size, k):
    return lax.ppermute(x, axis, [(i, i ^ k) for i in range(size)])


def first_hop(shard, n_ev):
    if n_ev != 8:
        return [shard] + [swap(shard, "events", n_ev, k) for k in range(1, n_ev)]
    return [shard, swap(shard, "events", n_ev, 2), swap(shard, "events", n_ev, 4)]


def halves_kernel(low_ref, high_ref, low_out, high_out):
    low_out[...] = low_ref[...]
    high_out[...] = high_ref[...]


def halves_of(pieces, half):
    cols = pieces[1].shape[1]
    shape = jax.ShapeDtypeStruct((half, cols), BF16)
    block = pl.BlockSpec((half, cols), lambda i: (0, 0))
    return pl.pallas_call(
        halves_kernel,
        grid=(1,),
        out_shape=[shape, shape],
        in_specs=[block, pl.BlockSpec((half, cols), lambda i: (1, 0))],
        out_specs=[block, block],
        compiler_params=params(SNUG),
        cost_estimate=cost(0),
        name="halves",
    )(pieces[1], pieces[2])


def split_kernel(half, low_ref, high_ref, low_out, high_out, low, high, sems):
    rows = high_ref.shape[1]
    sources = [low_ref.at[:, :half, :], high_ref.at[:, half:rows, :]]
    copies = fetch(sources, [low, high], sems)
    saves = []
    for i, (buffer, out) in enumerate(((low, low_out), (high, high_out))):
        copies[i].wait()
        saves += fetch([buffer], [out], sems, 2 + i)
    for save in saves:
        save.wait()


def split_of(pieces, half):
    lead, rows, cols = pieces[1].shape
    return pl.pallas_call(
        functools.partial(split_kernel, half),
        out_shape=[
            jax.ShapeDtypeStruct((lead, half, cols), BF16),
            jax.ShapeDtypeStruct((lead, rows - half, cols), BF16),
        ],
        in_specs=[hbm()] * 2,
        out_specs=[hbm()] * 2,
        scratch_shapes=[
            pltpu.VMEM((lead, half, cols), BF16),
            pltpu.VMEM((lead, rows - half, cols), BF16),
            pltpu.SemaphoreType.DMA((4,)),
        ],
        compiler_params=params(SNUG),
        cost_estimate=cost(0),
        name="split",
    )(pieces[1], pieces[2])


def second_hop(low, high, n_ev):
    return [swap(low, "events", n_ev, 4), swap(high, "events", n_ev, 2)]


def across(pieces, n_ev):
    return [swap(piece, "events", n_ev, 1) for piece in pieces]


def direct_plan(n_ev, width):
    order = range(n_ev) if n_ev != 8 else (0, 2, 4, 6, 1, 3, 5, 7)
    return [(k, 0, width) for k in order]


def hop_plan(n_ev, width):
    if n_ev != 8:
        return direct_plan(n_ev, width)
    half = width // 2
    near = [(0, 0, width), (2, 0, width), (4, 0, width), (6, 0, half), (6, half, half)]
    return near + [(k ^ 1, lo, size) for k, lo, size in near]


def event_order(n_ev):
    return list(range(n_ev)) if n_ev != 8 else [0, 2, 4, 6, 1, 3, 5, 7]


def gather_events(block, n_ev):
    if n_ev != 8:
        return [block] + [swap(block, "events", n_ev, k) for k in range(1, n_ev)]
    near = [block] + [swap(block, "events", n_ev, k) for k in (2, 4, 6)]
    return near + across(near, n_ev)


def local(
    event_x,
    event_visit,
    visit_count,
    visit_patient,
    treatment,
    outcome_target,
    enc_gain,
    enc_qkv,
    enc_out,
    visit_gain,
    visit_qkv,
    ffn_gain,
    ffn_in,
    ffn_out,
    head_weight,
    head_bias,
):
    n_ev = lax.axis_size("events")
    n_mp = lax.axis_size("mp")
    e = lax.axis_index("events")
    m = lax.axis_index("mp")
    rows_dev = event_x.shape[0]
    visits_dev = visit_count.shape[0]
    per_owner = visits_dev * n_mp
    group = n_mp * VPAD
    cols = DV // n_mp
    hidden = ffn_in.shape[1]
    where = jnp.stack([e, m]).astype(jnp.int32)
    ids = event_visit.reshape(rows_dev // LANES, LANES)

    send = pl.pallas_call(
        functools.partial(pack_kernel, n_ev, per_owner, visits_dev),
        out_shape=jax.ShapeDtypeStruct((rows_dev, D + LANES), BF16),
        in_specs=[smem(), vmem(), hbm()],
        out_specs=vmem(),
        scratch_shapes=[pltpu.VMEM((rows_dev, D), BF16), pltpu.SemaphoreType.DMA],
        compiler_params=params(12),
        cost_estimate=cost(0),
        name="pack",
    )(where, ids, event_x)
    got = lax.all_to_all(
        send.reshape(n_ev, rows_dev // n_ev, D + LANES), "events", split_axis=0, concat_axis=0,
        tiled=True,
    ).reshape(rows_dev, D + LANES)

    ffn_first = first_hop(ffn_in, n_ev)

    head_t = head_weight.T
    width = DV // n_ev
    own_head = lax.dynamic_slice_in_dim(head_t, e * width, width, 1)
    head_hi = own_head.astype(BF16)
    head_mid = (own_head - head_hi.astype(F32)).astype(BF16)
    head_lo = (own_head - head_hi.astype(F32) - head_mid.astype(F32)).astype(BF16)
    heads = jnp.concatenate([head_hi, head_mid, head_lo, jnp.zeros((2, width), BF16)], axis=0)
    meta, patient_row = pl.pallas_call(
        functools.partial(prep_kernel, visits_dev),
        out_shape=[
            jax.ShapeDtypeStruct((group, LANES), F32),
            jax.ShapeDtypeStruct((VPAD, group), F32),
        ],
        in_specs=[smem()] * 3,
        out_specs=[vmem()] * 2,
        compiler_params=params(4),
        cost_estimate=cost(0),
        name="prep",
    )(visit_patient, treatment, outcome_target)
    two_hops = n_ev == 8
    inner = jnp.arange(VPAD, dtype=jnp.int32)
    named = (jnp.array(event_order(n_ev), jnp.int32) ^ e)[:, None] * per_owner
    named = jnp.where(inner < visits_dev, named + m * visits_dev + inner[None, :], -2).reshape(-1)
    chosen = (event_visit[:, None] == named[None, :]).astype(BF16)
    ready = [meta, patient_row, head_t, chosen]
    if two_hops:
        ffn_halves = halves_of(ffn_first, width // 2)
        ready += ffn_halves
    qkv_shard = pl.pallas_call(
        fold_kernel,
        out_shape=jax.ShapeDtypeStruct((3, width + FW_ROWS, cols), BF16),
        in_specs=[vmem()] * 3,
        out_specs=vmem(),
        compiler_params=params(SNUG),
        cost_estimate=cost(30),
        name="fold",
    )(ffn_out, heads, after(visit_qkv, *ffn_first[1:], *ready))
    qkv_first = [qkv_shard] + first_hop(after(qkv_shard, got), n_ev)[1:]
    qkv_plan = hop_plan(n_ev, width)
    ffn_plan = hop_plan(n_ev, width)
    if two_hops:
        ffn_far = across(ffn_first, n_ev)
        qkv_far = across(qkv_first[:1], n_ev)
        got = after(got, *ffn_far, *qkv_far)

    vec = pl.pallas_call(
        functools.partial(encode_kernel, visits_dev),
        out_shape=jax.ShapeDtypeStruct((VPAD, DV), BF16),
        in_specs=[smem(), vmem(), hbm(), hbm(), hbm()],
        out_specs=vmem(),
        scratch_shapes=[
            pltpu.VMEM((rows_dev, D + LANES), BF16),
            pltpu.VMEM((D, 2 * D), BF16),
            pltpu.VMEM((D, D), BF16),
            pltpu.VMEM((D, D), BF16),
            pltpu.VMEM((visits_dev * VB, D), BF16),
            pltpu.VMEM((visits_dev * VB, 2 * D), BF16),
            pltpu.VMEM((visits_dev, HEADS, VB), F32),
            pltpu.VMEM((visits_dev, HEADS, D), BF16),
            pltpu.SemaphoreType.DMA((5,)),
        ],
        compiler_params=params(SNUG),
        cost_estimate=cost(0),
        name="encode",
    )(visit_count, enc_gain.reshape(1, D), got, enc_qkv, enc_out)

    if two_hops:
        qkv_halves = split_of([qkv_first[0]] + [after(p, vec) for p in qkv_first[1:]], width // 2)
        vec = after(vec, *qkv_halves)
    vecs = [vec] + [swap(vec, "mp", n_mp, k) for k in range(1, n_mp)]
    if two_hops:
        qkv_second = second_hop(*qkv_halves, n_ev)
        ffn_second = second_hop(*[after(piece, *vecs[1:]) for piece in ffn_halves], n_ev)
        qkv_far += across([after(piece, *vecs[1:]) for piece in qkv_first[1:]], n_ev)
        qkv_pieces = qkv_first + qkv_second + qkv_far + across(qkv_second, n_ev)
    else:
        qkv_pieces = qkv_first
    n_q = len(qkv_plan)
    vgain = visit_gain.reshape(1, DV)
    state_shape = (group, state_spans(cols)[2][1])
    attended, state = pl.pallas_call(
        functools.partial(project_kernel, n_mp, n_ev, qkv_plan),
        out_shape=[
            jax.ShapeDtypeStruct((group, cols), BF16),
            jax.ShapeDtypeStruct(state_shape, F32),
        ],
        in_specs=[smem()] + [vmem()] * (n_mp + 3) + [hbm()] * n_q,
        out_specs=[vmem(), hbm()],
        scratch_shapes=[pltpu.VMEM(piece.shape, BF16) for piece in qkv_pieces]
        + [
            pltpu.VMEM((n_mp, VPAD, DV), BF16),
            pltpu.VMEM((n_ev, group, width), BF16),
            pltpu.SemaphoreType.DMA((n_q,)),
            pltpu.VMEM(state_shape, F32),
            pltpu.SemaphoreType.DMA((3,)),
        ],
        compiler_params=params(SNUG),
        cost_estimate=cost(0),
        name="project",
    )(where, *vecs, vgain, meta, patient_row, *qkv_pieces)

    attns = [attended] + [swap(attended, "mp", n_mp, k) for k in range(1, n_mp)]
    if two_hops:
        ffn_second = [after(piece, *attns[1:]) for piece in ffn_second]
        ffn_pieces = ffn_first + ffn_second + ffn_far + across(ffn_second, n_ev)
    else:
        ffn_pieces = ffn_first
    n_f = len(ffn_plan)
    fgain = ffn_gain.reshape(1, DV)
    ffn_outs = pl.pallas_call(
        functools.partial(ffn_kernel, n_mp, n_ev, ffn_plan),
        out_shape=[jax.ShapeDtypeStruct((group, cols + LANES), BF16)] * n_mp
        + [jax.ShapeDtypeStruct((group, cols + LANES), F32)],
        in_specs=[smem()] * 2 + [vmem()] * (3 + n_mp) + [hbm()] * (1 + n_f),
        out_specs=[vmem()] * (n_mp + 1),
        scratch_shapes=[pltpu.VMEM(piece.shape, BF16) for piece in ffn_pieces]
        + [
            pltpu.VMEM((n_mp, group, cols), BF16),
            pltpu.VMEM((group, DV), F32),
            pltpu.VMEM((FW_ROWS, cols), F32),
            pltpu.VMEM((n_ev, group, width), BF16),
            pltpu.VMEM((n_ev, group, width), F32),
            pltpu.SemaphoreType.DMA((n_f + 2,)),
        ],
        compiler_params=params(SNUG),
        cost_estimate=cost(0),
        name="ffn",
    )(where, head_bias, fgain, meta, head_t, *attns, state, *ffn_pieces)
    mid = ffn_outs[n_mp]
    pays = [ffn_outs[0]] + [swap(ffn_outs[k], "mp", n_mp, k) for k in range(1, n_mp)]

    back_outs = pl.pallas_call(
        functools.partial(back_kernel, n_mp, n_ev, qkv_plan),
        out_shape=[jax.ShapeDtypeStruct((VPAD, D + LANES), BF16)] * n_mp
        + [jax.ShapeDtypeStruct((group, LANES), F32), jax.ShapeDtypeStruct((VPAD, D), F32)],
        in_specs=[smem()] + [vmem()] * (5 + n_mp) + [hbm()] * (1 + n_q),
        out_specs=[vmem()] * (n_mp + 2),
        scratch_shapes=[pltpu.VMEM(piece.shape, BF16) for piece in qkv_pieces]
        + [
            pltpu.VMEM(state_shape, F32),
            pltpu.VMEM((n_ev, group, width), F32),
            pltpu.VMEM((n_mp, VPAD, D + LANES), F32),
            pltpu.SemaphoreType.DMA((n_q + 1,)),
        ],
        compiler_params=params(SNUG),
        cost_estimate=cost(0),
        name="back",
    )(where, mid, meta, fgain, vgain, head_t, *pays, state, *qkv_pieces)
    outcomes = back_outs[n_mp][:, :2].reshape(n_mp, VPAD, 2)[:, :visits_dev].reshape(per_owner, 2)
    shares = [back_outs[0]] + [swap(back_outs[k], "mp", n_mp, k) for k in range(1, n_mp)]
    visit_grad = pl.pallas_call(
        functools.partial(finish_kernel, n_mp, visits_dev),
        out_shape=jax.ShapeDtypeStruct((VPAD, D), F32),
        in_specs=[smem()] + [vmem()] * (1 + n_mp),
        out_specs=vmem(),
        compiler_params=params(4),
        cost_estimate=cost(0),
        name="finish",
    )(visit_count, after(back_outs[n_mp + 1], outcomes), *shares)

    tables = gather_events(visit_grad, n_ev)
    event_grads = pl.pallas_call(
        functools.partial(spread_kernel, n_ev),
        out_shape=jax.ShapeDtypeStruct((rows_dev, D), BF16),
        in_specs=[vmem()] * (n_ev + 1),
        out_specs=hbm(),
        scratch_shapes=[
            pltpu.VMEM((rows_dev, D), BF16),
            pltpu.SemaphoreType.DMA((3,)),
        ],
        compiler_params=params(8),
        cost_estimate=cost(0),
        name="spread",
    )(chosen, *tables)
    return (outcomes, event_grads)


def solution(mesh):
    in_specs = (
        P(("events", "mp"), None),
        P(("events", "mp")),
        P(("events", "mp")),
        P("events"),
        P("events"),
        P("events"),
        P(),
        P(),
        P(),
        P(),
        P(None, "events", "mp"),
        P(),
        P("events", "mp"),
        P("mp", "events"),
        P(),
        P(),
    )
    out_specs = (P("events", None), P(("events", "mp"), None))
    return jax.shard_map(local, mesh=mesh, in_specs=in_specs, out_specs=out_specs, check_vma=False)
```

```python
import functools

import jax
import jax.numpy as jnp
from jax import lax
from jax.experimental import pallas as pl
from jax.experimental.pallas import tpu as pltpu
from jax.sharding import PartitionSpec as P

D = 1024
HEADS = 16
HDIM = 64
VB = 128
DV = 2048
VHDIM = 128
VPAD = 8
FW_ROWS = 16
SNUG = 48
LANES = 128
EPS = 1e-5
F32 = jnp.float32
BF16 = jnp.bfloat16

NT = (((1,), (1,)), ((), ()))
TN = (((0,), (0,)), ((), ()))
NN = (((1,), (0,)), ((), ()))


def dot(a, b, dims=NN):
    return lax.dot_general(a, b, dims, preferred_element_type=F32)


def vmem():
    return pl.BlockSpec(memory_space=pltpu.VMEM)


def smem():
    return pl.BlockSpec(memory_space=pltpu.SMEM)


def hbm():
    return pl.BlockSpec(memory_space=pltpu.HBM)


def params(mib):
    return pltpu.CompilerParams(vmem_limit_bytes=int(mib * 1024) * 1024)


def cost(micros):
    return pl.CostEstimate(
        flops=int(micros * 1e9) + 1, bytes_accessed=int(micros * 1e6) + 1, transcendentals=0
    )


def after(value, *others):
    return lax.optimization_barrier((value, *others))[0]


def strict_upper(rows):
    a = lax.broadcasted_iota(jnp.int32, (rows, rows), 0)
    b = lax.broadcasted_iota(jnp.int32, (rows, rows), 1)
    return (a < b).astype(BF16)


def pick_rows(position, first, count, rows):
    slots = lax.broadcasted_iota(jnp.int32, (count, rows), 0) + first
    return (slots == position).astype(BF16)


def pack_kernel(senders, per_owner, visits_dev, where_ref, ids_ref, x_hbm, out_ref, x_ref, sem):
    copy = pltpu.make_async_copy(x_hbm, x_ref, sem)
    copy.start()
    rows = x_ref.shape[0]
    cap_rows = rows // senders
    ids = jnp.concatenate([ids_ref[i : i + 1, :] for i in range(ids_ref.shape[0])], axis=1)
    owners = lax.broadcasted_iota(jnp.int32, (senders, rows), 0)
    hot = (ids >= owners * per_owner) & (ids < (owners + 1) * per_owner)
    hot_f = hot.astype(F32)
    before = dot(hot.astype(BF16), strict_upper(rows))
    base = (owners * cap_rows + 1).astype(F32)
    position = (jnp.sum(hot_f * (base + before), axis=0, keepdims=True)).astype(jnp.int32) - 1
    first = (owners * per_owner + where_ref[1] * visits_dev).astype(F32)
    label = jnp.sum(hot_f * (ids.astype(F32) - first + 1.0), axis=0, keepdims=True)
    label = jnp.broadcast_to(label, (LANES, rows)).astype(BF16)
    copy.wait()
    step = rows // 3
    for c in range(3):
        chosen = pick_rows(position, c * step, step, rows)
        out_ref[c * step : (c + 1) * step, :D] = dot(chosen, x_ref[...]).astype(BF16)
        out_ref[c * step : (c + 1) * step, D:] = dot(chosen, label, NT).astype(BF16)


def prep_kernel(visits_dev, patient_ref, treat_ref, target_ref, meta_ref, row_ref):
    rows, lanes = meta_ref.shape
    slot = lax.broadcasted_iota(jnp.int32, (rows, lanes), 0)
    lane = lax.broadcasted_iota(jnp.int32, (rows, lanes), 1)
    place = lax.broadcasted_iota(jnp.int32, (VPAD, rows), 1)
    meta = jnp.where(lane == 2, -1.0, jnp.zeros((rows, lanes), F32))
    line = jnp.full((VPAD, rows), -1.0, F32)
    for g in range(patient_ref.shape[0]):
        at = (g // visits_dev) * VPAD + g % visits_dev
        patient = patient_ref[g].astype(F32)
        here = jnp.where(
            lane == 0, treat_ref[g].astype(F32), jnp.where(lane == 1, target_ref[g], patient)
        )
        meta = jnp.where((slot == at) & (lane < 3), here, meta)
        line = jnp.where(place == at, patient, line)
    meta_ref[...] = meta
    row_ref[...] = line


def fold_kernel(weight_ref, head_ref, ffn_ref, out_ref):
    rows = ffn_ref.shape[0]
    out_ref[:rows, :] = ffn_ref[...]
    folded = dot(head_ref[...], weight_ref[...], NT)
    folded = folded[0:2] + folded[2:4] + folded[4:6]
    one = folded.astype(BF16).astype(F32)
    two = (folded - one).astype(BF16).astype(F32)
    three = folded - one - two
    blank = jnp.zeros((FW_ROWS - 6, folded.shape[1]), F32)
    out_ref[rows:, :] = jnp.concatenate([one, two, three, blank], axis=0).astype(BF16)


def encode_kernel(
    visits_dev,
    count_ref,
    gain_ref,
    got_hbm,
    qkv_ref,
    proj_ref,
    vec_ref,
    got_ref,
    wqk,
    wv,
    wo,
    normed,
    qk,
    pbar,
    ctx,
    sems,
):
    rows = got_ref.shape[0]
    slots = visits_dev * VB
    inputs = [
        pltpu.make_async_copy(got_hbm.at[:, D:], got_ref.at[:, D:], sems.at[3]),
        pltpu.make_async_copy(got_hbm.at[:, :D], got_ref.at[:, :D], sems.at[4]),
    ]
    copies = [
        pltpu.make_async_copy(qkv_ref.at[:, : 2 * D], wqk, sems.at[0]),
        pltpu.make_async_copy(qkv_ref.at[:, 2 * D :], wv, sems.at[1]),
        pltpu.make_async_copy(proj_ref, wo, sems.at[2]),
    ]
    for copy in inputs + copies:
        copy.start()
    inputs[0].wait()
    lane0 = (lax.broadcasted_iota(jnp.int32, (VPAD, LANES), 1) == 0).astype(BF16)
    label = dot(lane0, got_ref[:, D:], NT)[:1]
    visits = lax.broadcasted_iota(jnp.int32, (VPAD, rows), 0)
    hot = label == (visits + 1).astype(F32)
    hot_b = hot.astype(BF16)
    hot_f = hot.astype(F32)
    before = dot(hot_b, strict_upper(rows))
    base = (visits * VB + 1).astype(F32)
    position = (jnp.sum(hot_f * (base + before), axis=0, keepdims=True)).astype(jnp.int32) - 1
    inputs[1].wait()
    sums = dot(hot_b, got_ref[:, :D])
    gain = gain_ref[...]
    step = 2 * VB
    for c in range(slots // step):
        part = dot(pick_rows(position, c * step, step, rows), got_ref[:, :D])
        scale = lax.rsqrt(jnp.mean(part * part, axis=-1, keepdims=True) + EPS)
        normed[c * step : (c + 1) * step, :] = (part * scale * gain).astype(BF16)
    copies[0].wait()
    wide = 512
    for c in range(2 * D // wide):
        cols = slice(c * wide, (c + 1) * wide)
        qk[:, cols] = dot(normed[...], wqk[:, cols]).astype(BF16)

    lanes = lax.broadcasted_iota(jnp.int32, (VB, LANES), 1)
    low = (lanes < HDIM).astype(F32) * HDIM ** (-0.5)
    high = (lanes >= HDIM).astype(F32) * HDIM ** (-0.5)
    key_slot = lax.broadcasted_iota(jnp.int32, (VB, 2 * VB), 0)
    query_lane = lax.broadcasted_iota(jnp.int32, (1, 2 * VB), 1)
    query_slot = jnp.where(query_lane >= VB, query_lane - VB, query_lane)
    rows8 = lax.broadcasted_iota(jnp.int32, (VPAD, 2 * VB), 0)
    lanes8 = lax.broadcasted_iota(jnp.int32, (VPAD, 2 * VB), 1)
    halves = ((lanes8 >= rows8 * VB) & (lanes8 < (rows8 + 1) * VB)).astype(BF16)

    def one_visit(v, carry):
        count = count_ref[v]
        at = pl.ds(pl.multiple_of(v * VB, VB), VB)
        live_key = key_slot < count
        weight = (query_slot < count).astype(F32) / count.astype(F32)
        for p in range(HEADS // 2):
            q = qk[at, p * LANES : (p + 1) * LANES].astype(F32)
            k = qk[at, D + p * LANES : D + (p + 1) * LANES]
            both = jnp.concatenate([(q * low).astype(BF16), (q * high).astype(BF16)], axis=0)
            scores = jnp.where(live_key, dot(k, both, NT), -1e30)
            top = jnp.max(scores, axis=0, keepdims=True)
            grown = jnp.exp(scores - top)
            total = jnp.sum(grown, axis=0, keepdims=True)
            shares = (grown * (weight / total)).astype(BF16)
            pbar[v, 2 * p : 2 * p + 2, :] = dot(halves, shares, NT)[:2]
        ctx[v] = dot(pbar[v].astype(BF16), normed[at, :]).astype(BF16)
        return carry

    lax.fori_loop(0, visits_dev, one_visit, 0)
    copies[1].wait()
    copies[2].wait()
    vals = dot(ctx[...].reshape(visits_dev * HEADS, D), wv[...]).reshape(visits_dev, HEADS, D)
    head_row = lax.broadcasted_iota(jnp.int32, (1, HEADS, D), 1) * HDIM
    col = lax.broadcasted_iota(jnp.int32, (1, HEADS, D), 2)
    own = (col >= head_row) & (col < head_row + HDIM)
    attended = jnp.sum(jnp.where(own, vals, 0.0), axis=1)
    attended = jnp.concatenate([attended, jnp.zeros((VPAD - visits_dev, D), F32)], axis=0)
    head_part = attended.astype(BF16)
    rest = (attended - head_part.astype(F32)).astype(BF16)
    mixed = dot(head_part, wo[...]) + dot(rest, wo[...])
    row = lax.broadcasted_iota(jnp.int32, (VPAD, 1), 0)
    inverse = jnp.zeros((VPAD, 1), F32)
    for v in range(visits_dev):
        inverse = jnp.where(row == v, 1.0 / count_ref[v].astype(F32), inverse)
    mean_input = sums * inverse
    vec_ref[:, :D] = (mean_input + mixed).astype(BF16)
    vec_ref[:, D:] = mean_input.astype(BF16)


def rms_factor(values):
    return lax.rsqrt(jnp.mean(values * values, axis=-1, keepdims=True) + EPS)


def fetch(pieces, scratch, sems, first=0):
    copies = [
        pltpu.make_async_copy(piece, buffer, sems.at[first + i])
        for i, (piece, buffer) in enumerate(zip(pieces, scratch, strict=True))
    ]
    for copy in copies:
        copy.start()
    return copies


def project_kernel(n_mp, n_ev, plan, where_ref, *refs):
    n = len(plan)
    vec_in, (gain_ref, meta_ref, patient_ref), refs = refs[:n_mp], refs[n_mp : n_mp + 3], refs[n_mp + 3 :]
    pieces, refs = refs[:n], refs[n:]
    attended_ref, state, refs = refs[0], refs[1], refs[2:]
    scratch, refs = refs[:n], refs[n:]
    vec, blocks, sems, kept, out_sems = refs
    copies = fetch(pieces, scratch, sems)
    e, m = where_ref[0], where_ref[1]
    cols = attended_ref.shape[1]
    saves = [
        pltpu.make_async_copy(kept.at[:, lo:hi], state.at[:, lo:hi], out_sems.at[i])
        for i, (lo, hi) in enumerate(state_spans(cols))
    ]
    for k in range(n_mp):
        vec[m ^ k] = vec_in[k][...]
    rows = n_mp * VPAD
    full = vec[...].astype(F32).reshape(rows, DV)
    kept[:, :DV] = full
    saves[0].start()
    normed = (full * rms_factor(full) * gain_ref[...]).astype(BF16)
    width = DV // n_ev
    for j in range(n_ev):
        blocks[j] = normed[:, j * width : (j + 1) * width]
    totals = [jnp.zeros((rows, cols), F32) for _ in range(3)]
    for i, (k, lo, size) in enumerate(plan):
        copies[i].wait()
        block = blocks[e ^ k][:, lo : lo + size]
        for t in range(3):
            totals[t] = totals[t] + dot(block, scratch[i][t, :size, :])
    parts = [total.astype(BF16) for total in totals]
    for t in range(3):
        kept[:, DV + t * cols : DV + (t + 1) * cols] = parts[t].astype(F32)
    saves[1].start()
    q_at = lax.broadcasted_iota(jnp.int32, (rows, rows), 0)
    k_at = lax.broadcasted_iota(jnp.int32, (rows, rows), 1)
    allowed = (meta_ref[:, 2:3] == patient_ref[0:1, :]) & (k_at <= q_at)
    for h in range(cols // VHDIM):
        span = slice(h * VHDIM, (h + 1) * VHDIM)
        scores = dot(parts[0][:, span], parts[1][:, span], NT) * VHDIM ** (-0.5)
        scores = jnp.where(allowed, scores, -1e30)
        grown = jnp.exp(scores - jnp.max(scores, axis=-1, keepdims=True))
        prob = grown / jnp.sum(grown, axis=-1, keepdims=True)
        kept[:, DV + 3 * cols + h * rows : DV + 3 * cols + (h + 1) * rows] = prob
        attended_ref[:, span] = dot(prob.astype(BF16), parts[2][:, span]).astype(BF16)
    saves[2].start()
    for save in saves:
        save.wait()


def state_spans(cols):
    return ((0, DV), (DV, DV + 3 * cols), (DV + 3 * cols, DV + 3 * cols + LANES))


def pack_scalars(columns, rows):
    lane = lax.broadcasted_iota(jnp.int32, (rows, LANES), 1)
    spread = jnp.zeros((rows, LANES), F32)
    for c, column in enumerate(columns):
        at = (lane == c) | (lane == 8 + c) | (lane == 16 + c)
        spread = jnp.where(at, column, spread)
    one = spread.astype(BF16).astype(F32)
    two = (spread - one).astype(BF16).astype(F32)
    three = spread - one - two
    return jnp.where(lane < 8, one, jnp.where(lane < 16, two, three)).astype(BF16)


def unpack_scalar(packed, c):
    return packed[:, c : c + 1] + packed[:, 8 + c : 9 + c] + packed[:, 16 + c : 17 + c]


def ffn_kernel(
    n_mp, n_ev, plan, where_ref, bias_ref, gain_ref, meta_ref, head_ref, *refs
):
    n = len(plan)
    attn_in, state, refs = refs[:n_mp], refs[n_mp], refs[n_mp + 1 :]
    pieces, refs = refs[:n], refs[n:]
    outs, mid_ref, refs = refs[:n_mp], refs[n_mp], refs[n_mp + 1 :]
    scratch, refs = refs[:n], refs[n:]
    attn, vec_ref, blocks, grads, sems = refs
    e, m = where_ref[0], where_ref[1]
    cols = DV // n_mp
    small = fetch([state.at[:, :DV]], [vec_ref], sems, n)
    copies = fetch(pieces, scratch, sems)
    for k in range(n_mp):
        attn[m ^ k] = attn_in[k][...]
    for copy in small:
        copy.wait()
    rows = vec_ref.shape[0]
    mid = vec_ref[...] + jnp.concatenate([attn[k] for k in range(n_mp)], axis=1).astype(F32)
    at = pl.ds(pl.multiple_of(m * cols, cols), cols)
    factor = rms_factor(mid)
    mid_ref[:, :cols] = vec_ref[:, at] + attn[m].astype(F32)
    mid_ref[:, cols:] = jnp.broadcast_to(factor, (rows, LANES))
    gain = gain_ref[...]
    normed = (mid * factor * gain).astype(BF16)
    width = DV // n_ev
    for j in range(n_ev):
        blocks[j] = normed[:, j * width : (j + 1) * width]
    hidden = scratch[0].shape[1]
    pre = jnp.zeros((rows, hidden), F32)
    fw = jnp.zeros((2, hidden), F32)
    for i, (k, lo, size) in enumerate(plan):
        copies[i].wait()
        pre = pre + dot(blocks[e ^ k][:, lo : lo + size], scratch[i][:size, :])
        if scratch[i].shape[0] > size:
            parts = scratch[i][size : size + FW_ROWS, :].astype(F32)
            fw = fw + (parts[0:2] + parts[2:4] + parts[4:6])
    sigma = 1.0 / (1.0 + jnp.exp(-pre))
    act = (pre * sigma).astype(BF16).astype(F32)
    first = (m == 0).astype(F32)
    outcome = []
    for j in range(2):
        base = jnp.sum(mid * head_ref[j : j + 1, :], axis=-1, keepdims=True) + bias_ref[j]
        outcome.append(jnp.sum(act * fw[j : j + 1, :], axis=-1, keepdims=True) + first * base)
    chosen = jnp.where(meta_ref[:, 0:1] > 0.5, fw[1:2, :], fw[0:1, :])
    slope = (chosen * sigma * (1.0 + pre * (1.0 - sigma))).astype(BF16)
    for i, (k, lo, size) in enumerate(plan):
        grads[e ^ k, :, lo : lo + size] = dot(slope, scratch[i][:size, :], NT)
    moment = jnp.zeros((rows, 1), F32)
    for j in range(n_ev):
        span = slice(j * width, (j + 1) * width)
        moment = moment + jnp.sum(grads[j] * gain[:, span] * mid[:, span], axis=-1, keepdims=True)
    scalars = pack_scalars([outcome[0], outcome[1], moment], rows)
    each = n_ev // n_mp
    for k in range(n_mp):
        for j in range(each):
            outs[k][:, j * width : (j + 1) * width] = grads[(m ^ k) * each + j].astype(BF16)
        outs[k][:, cols:] = scalars


def back_kernel(
    n_mp, n_ev, plan, where_ref, mid_ref, meta_ref, gain_ref, vgain_ref, head_ref, *refs
):
    n = len(plan)
    pay_in, state, refs = refs[:n_mp], refs[n_mp], refs[n_mp + 1 :]
    pieces, refs = refs[:n], refs[n:]
    outs, outcome_ref, coef_ref, refs = refs[:n_mp], refs[n_mp], refs[n_mp + 1], refs[n_mp + 2 :]
    scratch, refs = refs[:n], refs[n:]
    kept, grads, table, sems = refs
    (stored,) = fetch([state], [kept], sems, n)
    copies = fetch(pieces, scratch, sems)
    e, m = where_ref[0], where_ref[1]
    rows = mid_ref.shape[0]
    cols = DV // n_mp
    total = pay_in[0][...].astype(F32)
    for k in range(1, n_mp):
        total = total + pay_in[k][...].astype(F32)
    packed = total[:, cols:]
    outcome = [unpack_scalar(packed, 0), unpack_scalar(packed, 1)]
    moment = unpack_scalar(packed, 2) * (1.0 / DV)
    lane = lax.broadcasted_iota(jnp.int32, (rows, LANES), 1)
    outcome_ref[...] = jnp.where(lane == 0, outcome[0], outcome[1])
    treated = meta_ref[:, 0:1] > 0.5
    delta = 4096.0 * (jnp.where(treated, outcome[1], outcome[0]) - meta_ref[:, 1:2])
    factor = mid_ref[:, cols : cols + 1]
    at = pl.ds(pl.multiple_of(m * cols, cols), cols)
    mid = mid_ref[:, :cols]
    head = jnp.where(treated, head_ref[1:2, at], head_ref[0:1, at])
    scaled = total[:, :cols] * gain_ref[:, at]
    grad_mid = delta * (head + factor * (scaled - mid * (factor * factor * moment)))
    grad_c = grad_mid.astype(BF16)
    stored.wait()
    queries, keys, values = (
        kept[:, DV + t * cols : DV + (t + 1) * cols].astype(BF16) for t in range(3)
    )
    three = [[], [], []]
    for h in range(cols // VHDIM):
        span = slice(h * VHDIM, (h + 1) * VHDIM)
        prob = kept[:, DV + 3 * cols + h * rows : DV + 3 * cols + (h + 1) * rows]
        grad_p = dot(grad_c[:, span], values[:, span], NT)
        grad_s = prob * (grad_p - jnp.sum(grad_p * prob, axis=-1, keepdims=True))
        grad_s = (grad_s * VHDIM ** (-0.5)).astype(BF16)
        three[0].append(dot(grad_s, keys[:, span]).astype(BF16))
        three[1].append(dot(grad_s, queries[:, span], TN).astype(BF16))
        three[2].append(dot(prob.astype(BF16), grad_c[:, span], TN).astype(BF16))
    three = [jnp.concatenate(parts, axis=1) for parts in three]
    for i, (k, lo, size) in enumerate(plan):
        copies[i].wait()
        part = dot(three[0], scratch[i][0, :size, :], NT)
        part = part + dot(three[1], scratch[i][1, :size, :], NT)
        part = part + dot(three[2], scratch[i][2, :size, :], NT)
        grads[e ^ k, :, lo : lo + size] = part
    width = DV // n_ev
    vec = kept[:, :DV]
    spread = rms_factor(vec)
    moment = jnp.zeros((rows, 1), F32)
    for j in range(n_ev):
        span = slice(j * width, (j + 1) * width)
        scaled = grads[j] * vgain_ref[:, span]
        moment = moment + jnp.sum(scaled * vec[:, span], axis=-1, keepdims=True)
        if (j + 1) * width <= D:
            table[:, :, span] = (scaled * spread).reshape(n_mp, VPAD, width)

    @pl.when(m * cols < D)
    def _():
        here = pl.ds(pl.multiple_of(m * cols, cols), cols)
        table[:, :, here] = table[:, :, here] + grad_mid.reshape(n_mp, VPAD, cols)

    scalars = pack_scalars([moment], rows).astype(F32)
    table[:, :, D:] = scalars.reshape(n_mp, VPAD, LANES)
    for k in range(n_mp):
        outs[k][...] = table[m ^ k].astype(BF16)
    table[:, :, :D] = (vec[:, :D] * (spread * spread * spread * (1.0 / DV))).reshape(n_mp, VPAD, D)
    coef_ref[...] = table[m][:, :D]


def finish_kernel(n_mp, visits_dev, count_ref, coef_ref, *refs):
    pays, out_ref = refs[:n_mp], refs[n_mp]
    total = pays[0][...].astype(F32)
    for k in range(1, n_mp):
        total = total + pays[k][...].astype(F32)
    grad = total[:, :D] - coef_ref[...] * unpack_scalar(total[:, D:], 0)
    row = lax.broadcasted_iota(jnp.int32, (VPAD, 1), 0)
    inverse = jnp.zeros((VPAD, 1), F32)
    for v in range(visits_dev):
        inverse = jnp.where(row == v, 1.0 / count_ref[v].astype(F32), inverse)
    out_ref[...] = (grad * inverse).astype(BF16).astype(F32)


def spread_kernel(n_ev, pick, *refs):
    tables, out, rows_ref, out_sems = refs[:n_ev], *refs[n_ev:]
    table = jnp.concatenate([each[...] for each in tables], axis=0).astype(BF16)
    rows = rows_ref.shape[0]
    step = rows // 3
    saves = []
    for c in range(3):
        span = slice(c * step, (c + 1) * step)
        rows_ref[span, :] = dot(pick[span, :], table).astype(BF16)
        saves.append(pltpu.make_async_copy(rows_ref.at[span, :], out.at[span, :], out_sems.at[c]))
        saves[c].start()
    for save in saves:
        save.wait()


def swap(x, axis, size, k):
    return lax.ppermute(x, axis, [(i, i ^ k) for i in range(size)])


def first_hop(shard, n_ev):
    if n_ev != 8:
        return [shard] + [swap(shard, "events", n_ev, k) for k in range(1, n_ev)]
    return [shard, swap(shard, "events", n_ev, 2), swap(shard, "events", n_ev, 4)]


def halves_kernel(low_ref, high_ref, low_out, high_out):
    half = low_out.shape[0]
    low_out[...] = low_ref[...]
    high_out[...] = high_ref[half:, :]


def halves_of(pieces, half):
    rows, cols = pieces[1].shape
    low = pl.BlockSpec((half, cols), lambda i: (0, 0))
    return pl.pallas_call(
        halves_kernel,
        grid=(1,),
        out_shape=[
            jax.ShapeDtypeStruct((half, cols), BF16),
            jax.ShapeDtypeStruct((rows - half, cols), BF16),
        ],
        in_specs=[low, vmem()],
        out_specs=[low, vmem()],
        compiler_params=params(SNUG),
        cost_estimate=cost(0),
        name="halves",
    )(pieces[1], pieces[2])


def split_kernel(half, low_ref, high_ref, low_out, high_out, low, high, sems):
    rows = high_ref.shape[1]
    sources = [low_ref.at[:, :half, :], high_ref.at[:, half:rows, :]]
    copies = fetch(sources, [low, high], sems)
    saves = []
    for i, (buffer, out) in enumerate(((low, low_out), (high, high_out))):
        copies[i].wait()
        saves += fetch([buffer], [out], sems, 2 + i)
    for save in saves:
        save.wait()


def split_of(pieces, half):
    lead, rows, cols = pieces[1].shape
    return pl.pallas_call(
        functools.partial(split_kernel, half),
        out_shape=[
            jax.ShapeDtypeStruct((lead, half, cols), BF16),
            jax.ShapeDtypeStruct((lead, rows - half, cols), BF16),
        ],
        in_specs=[hbm()] * 2,
        out_specs=[hbm()] * 2,
        scratch_shapes=[
            pltpu.VMEM((lead, half, cols), BF16),
            pltpu.VMEM((lead, rows - half, cols), BF16),
            pltpu.SemaphoreType.DMA((4,)),
        ],
        compiler_params=params(SNUG),
        cost_estimate=cost(0),
        name="split",
    )(pieces[1], pieces[2])


def second_hop(low, high, n_ev):
    return [swap(low, "events", n_ev, 4), swap(high, "events", n_ev, 2)]


def across(pieces, n_ev):
    return [swap(piece, "events", n_ev, 1) for piece in pieces]


def direct_plan(n_ev, width):
    order = range(n_ev) if n_ev != 8 else (0, 2, 4, 6, 1, 3, 5, 7)
    return [(k, 0, width) for k in order]


def hop_plan(n_ev, width):
    if n_ev != 8:
        return direct_plan(n_ev, width)
    half = width // 2
    near = [(0, 0, width), (2, 0, width), (4, 0, width), (6, 0, half), (6, half, half)]
    return near + [(k ^ 1, lo, size) for k, lo, size in near]


def event_order(n_ev):
    return list(range(n_ev)) if n_ev != 8 else [0, 2, 4, 6, 1, 3, 5, 7]


def gather_events(block, n_ev):
    if n_ev != 8:
        return [block] + [swap(block, "events", n_ev, k) for k in range(1, n_ev)]
    near = [block] + [swap(block, "events", n_ev, k) for k in (2, 4, 6)]
    return near + across(near, n_ev)


def local(
    event_x,
    event_visit,
    visit_count,
    visit_patient,
    treatment,
    outcome_target,
    enc_gain,
    enc_qkv,
    enc_out,
    visit_gain,
    visit_qkv,
    ffn_gain,
    ffn_in,
    ffn_out,
    head_weight,
    head_bias,
):
    n_ev = lax.axis_size("events")
    n_mp = lax.axis_size("mp")
    e = lax.axis_index("events")
    m = lax.axis_index("mp")
    rows_dev = event_x.shape[0]
    visits_dev = visit_count.shape[0]
    per_owner = visits_dev * n_mp
    group = n_mp * VPAD
    cols = DV // n_mp
    hidden = ffn_in.shape[1]
    where = jnp.stack([e, m]).astype(jnp.int32)
    ids = event_visit.reshape(rows_dev // LANES, LANES)

    send = pl.pallas_call(
        functools.partial(pack_kernel, n_ev, per_owner, visits_dev),
        out_shape=jax.ShapeDtypeStruct((rows_dev, D + LANES), BF16),
        in_specs=[smem(), vmem(), hbm()],
        out_specs=vmem(),
        scratch_shapes=[pltpu.VMEM((rows_dev, D), BF16), pltpu.SemaphoreType.DMA],
        compiler_params=params(12),
        cost_estimate=cost(0),
        name="pack",
    )(where, ids, event_x)
    got = lax.all_to_all(
        send.reshape(n_ev, rows_dev // n_ev, D + LANES), "events", split_axis=0, concat_axis=0,
        tiled=True,
    ).reshape(rows_dev, D + LANES)

    qkv_first = first_hop(visit_qkv, n_ev)

    head_t = head_weight.T
    width = DV // n_ev
    own_head = lax.dynamic_slice_in_dim(head_t, e * width, width, 1)
    head_hi = own_head.astype(BF16)
    head_mid = (own_head - head_hi.astype(F32)).astype(BF16)
    head_lo = (own_head - head_hi.astype(F32) - head_mid.astype(F32)).astype(BF16)
    heads = jnp.concatenate([head_hi, head_mid, head_lo, jnp.zeros((2, width), BF16)], axis=0)
    meta, patient_row = pl.pallas_call(
        functools.partial(prep_kernel, visits_dev),
        out_shape=[
            jax.ShapeDtypeStruct((group, LANES), F32),
            jax.ShapeDtypeStruct((VPAD, group), F32),
        ],
        in_specs=[smem()] * 3,
        out_specs=[vmem()] * 2,
        compiler_params=params(4),
        cost_estimate=cost(0),
        name="prep",
    )(visit_patient, treatment, outcome_target)
    two_hops = n_ev == 8
    inner = jnp.arange(VPAD, dtype=jnp.int32)
    named = (jnp.array(event_order(n_ev), jnp.int32) ^ e)[:, None] * per_owner
    named = jnp.where(inner < visits_dev, named + m * visits_dev + inner[None, :], -2).reshape(-1)
    chosen = (event_visit[:, None] == named[None, :]).astype(BF16)
    ready = [meta, patient_row, head_t, chosen]
    if two_hops:
        qkv_halves = split_of(qkv_first, width // 2)
        qkv_far = across(qkv_first, n_ev)
        ready += [*qkv_halves, *qkv_far]
    ffn_shard = pl.pallas_call(
        fold_kernel,
        out_shape=jax.ShapeDtypeStruct((width + FW_ROWS, hidden), BF16),
        in_specs=[vmem()] * 3,
        out_specs=vmem(),
        compiler_params=params(SNUG),
        cost_estimate=cost(30),
        name="fold",
    )(ffn_out, heads, after(ffn_in, *ready))
    qkv_plan = hop_plan(n_ev, width)
    ffn_plan = hop_plan(n_ev, width)
    gate = [got]
    if two_hops:
        qkv_second = second_hop(*qkv_halves, n_ev)
        qkv_far += across(qkv_second, n_ev)
        ffn_far = across([ffn_shard], n_ev)
        gate += qkv_second
    ffn_first = [ffn_shard] + first_hop(after(ffn_shard, *gate), n_ev)[1:]
    if two_hops:
        got = after(got, *ffn_far, *qkv_far)
    vec = pl.pallas_call(
        functools.partial(encode_kernel, visits_dev),
        out_shape=jax.ShapeDtypeStruct((VPAD, DV), BF16),
        in_specs=[smem(), vmem(), hbm(), hbm(), hbm()],
        out_specs=vmem(),
        scratch_shapes=[
            pltpu.VMEM((rows_dev, D + LANES), BF16),
            pltpu.VMEM((D, 2 * D), BF16),
            pltpu.VMEM((D, D), BF16),
            pltpu.VMEM((D, D), BF16),
            pltpu.VMEM((visits_dev * VB, D), BF16),
            pltpu.VMEM((visits_dev * VB, 2 * D), BF16),
            pltpu.VMEM((visits_dev, HEADS, VB), F32),
            pltpu.VMEM((visits_dev, HEADS, D), BF16),
            pltpu.SemaphoreType.DMA((5,)),
        ],
        compiler_params=params(53),
        cost_estimate=cost(0),
        name="encode",
    )(visit_count, enc_gain.reshape(1, D), got, enc_qkv, enc_out)

    vecs = [vec] + [swap(vec, "mp", n_mp, k) for k in range(1, n_mp)]
    if two_hops:
        qkv_pieces = qkv_first + qkv_second + qkv_far
        ffn_next = [ffn_first[0]] + [after(piece, *vecs[1:]) for piece in ffn_first[1:]]
        ffn_second = second_hop(*halves_of(ffn_next, width // 2), n_ev)
        ffn_far += across(ffn_next[1:], n_ev)
        vecs[0] = after(vec, *ffn_far[1:])
    else:
        qkv_pieces = qkv_first
    n_q = len(qkv_plan)
    vgain = visit_gain.reshape(1, DV)
    state_shape = (group, state_spans(cols)[2][1])
    attended, state = pl.pallas_call(
        functools.partial(project_kernel, n_mp, n_ev, qkv_plan),
        out_shape=[
            jax.ShapeDtypeStruct((group, cols), BF16),
            jax.ShapeDtypeStruct(state_shape, F32),
        ],
        in_specs=[smem()] + [vmem()] * (n_mp + 3) + [hbm()] * n_q,
        out_specs=[vmem(), hbm()],
        scratch_shapes=[pltpu.VMEM(piece.shape, BF16) for piece in qkv_pieces]
        + [
            pltpu.VMEM((n_mp, VPAD, DV), BF16),
            pltpu.VMEM((n_ev, group, width), BF16),
            pltpu.SemaphoreType.DMA((n_q,)),
            pltpu.VMEM(state_shape, F32),
            pltpu.SemaphoreType.DMA((3,)),
        ],
        compiler_params=params(SNUG),
        cost_estimate=cost(0),
        name="project",
    )(where, *vecs, vgain, meta, patient_row, *qkv_pieces)

    attns = [attended] + [swap(attended, "mp", n_mp, k) for k in range(1, n_mp)]
    if two_hops:
        ffn_second = [after(piece, *attns[1:]) for piece in ffn_second]
        ffn_pieces = ffn_first + ffn_second + ffn_far + across(ffn_second, n_ev)
    else:
        ffn_pieces = ffn_first
    n_f = len(ffn_plan)
    fgain = ffn_gain.reshape(1, DV)
    ffn_outs = pl.pallas_call(
        functools.partial(ffn_kernel, n_mp, n_ev, ffn_plan),
        out_shape=[jax.ShapeDtypeStruct((group, cols + LANES), BF16)] * n_mp
        + [jax.ShapeDtypeStruct((group, cols + LANES), F32)],
        in_specs=[smem()] * 2 + [vmem()] * (3 + n_mp) + [hbm()] * (1 + n_f),
        out_specs=[vmem()] * (n_mp + 1),
        scratch_shapes=[pltpu.VMEM(piece.shape, BF16) for piece in ffn_pieces]
        + [
            pltpu.VMEM((n_mp, group, cols), BF16),
            pltpu.VMEM((group, DV), F32),
            pltpu.VMEM((n_ev, group, width), BF16),
            pltpu.VMEM((n_ev, group, width), F32),
            pltpu.SemaphoreType.DMA((n_f + 1,)),
        ],
        compiler_params=params(SNUG),
        cost_estimate=cost(0),
        name="ffn",
    )(where, head_bias, fgain, meta, head_t, *attns, state, *ffn_pieces)
    mid = ffn_outs[n_mp]
    pays = [ffn_outs[0]] + [swap(ffn_outs[k], "mp", n_mp, k) for k in range(1, n_mp)]

    back_outs = pl.pallas_call(
        functools.partial(back_kernel, n_mp, n_ev, qkv_plan),
        out_shape=[jax.ShapeDtypeStruct((VPAD, D + LANES), BF16)] * n_mp
        + [jax.ShapeDtypeStruct((group, LANES), F32), jax.ShapeDtypeStruct((VPAD, D), F32)],
        in_specs=[smem()] + [vmem()] * (5 + n_mp) + [hbm()] * (1 + n_q),
        out_specs=[vmem()] * (n_mp + 2),
        scratch_shapes=[pltpu.VMEM(piece.shape, BF16) for piece in qkv_pieces]
        + [
            pltpu.VMEM(state_shape, F32),
            pltpu.VMEM((n_ev, group, width), F32),
            pltpu.VMEM((n_mp, VPAD, D + LANES), F32),
            pltpu.SemaphoreType.DMA((n_q + 1,)),
        ],
        compiler_params=params(SNUG),
        cost_estimate=cost(0),
        name="back",
    )(where, mid, meta, fgain, vgain, head_t, *pays, state, *qkv_pieces)
    outcomes = back_outs[n_mp][:, :2].reshape(n_mp, VPAD, 2)[:, :visits_dev].reshape(per_owner, 2)
    shares = [back_outs[0]] + [swap(back_outs[k], "mp", n_mp, k) for k in range(1, n_mp)]
    visit_grad = pl.pallas_call(
        functools.partial(finish_kernel, n_mp, visits_dev),
        out_shape=jax.ShapeDtypeStruct((VPAD, D), F32),
        in_specs=[smem()] + [vmem()] * (1 + n_mp),
        out_specs=vmem(),
        compiler_params=params(4),
        cost_estimate=cost(0),
        name="finish",
    )(visit_count, after(back_outs[n_mp + 1], outcomes), *shares)

    tables = gather_events(visit_grad, n_ev)
    event_grads = pl.pallas_call(
        functools.partial(spread_kernel, n_ev),
        out_shape=jax.ShapeDtypeStruct((rows_dev, D), BF16),
        in_specs=[vmem()] * (n_ev + 1),
        out_specs=hbm(),
        scratch_shapes=[
            pltpu.VMEM((rows_dev, D), BF16),
            pltpu.SemaphoreType.DMA((3,)),
        ],
        compiler_params=params(8),
        cost_estimate=cost(0),
        name="spread",
    )(chosen, *tables)
    return (outcomes, event_grads)


def solution(mesh):
    in_specs = (
        P(("events", "mp"), None),
        P(("events", "mp")),
        P(("events", "mp")),
        P("events"),
        P("events"),
        P("events"),
        P(),
        P(),
        P(),
        P(),
        P(None, "events", "mp"),
        P(),
        P("events", "mp"),
        P("mp", "events"),
        P(),
        P(),
    )
    out_specs = (P("events", None), P(("events", "mp"), None))
    return jax.shard_map(local, mesh=mesh, in_specs=in_specs, out_specs=out_specs, check_vma=False)
```

```python
import functools

import jax
import jax.numpy as jnp
from jax import lax
from jax.experimental import pallas as pl
from jax.experimental.pallas import tpu as pltpu
from jax.sharding import PartitionSpec as P

D = 1024
HEADS = 16
HDIM = 64
VB = 128
DV = 2048
VHDIM = 128
VPAD = 8
FW_ROWS = 16
SNUG = 48
LANES = 128
EPS = 1e-5
F32 = jnp.float32
BF16 = jnp.bfloat16

NT = (((1,), (1,)), ((), ()))
TN = (((0,), (0,)), ((), ()))
NN = (((1,), (0,)), ((), ()))


def dot(a, b, dims=NN):
    return lax.dot_general(a, b, dims, preferred_element_type=F32)


def vmem():
    return pl.BlockSpec(memory_space=pltpu.VMEM)


def smem():
    return pl.BlockSpec(memory_space=pltpu.SMEM)


def hbm():
    return pl.BlockSpec(memory_space=pltpu.HBM)


def params(mib):
    return pltpu.CompilerParams(vmem_limit_bytes=int(mib * 1024) * 1024)


def cost(micros):
    return pl.CostEstimate(
        flops=int(micros * 1e9) + 1, bytes_accessed=int(micros * 1e6) + 1, transcendentals=0
    )


def after(value, *others):
    return lax.optimization_barrier((value, *others))[0]


def rank_before(hot):
    classes, rows = hot.shape
    tiles = [hot[:, c : c + LANES] for c in range(0, rows, LANES)]
    a = lax.broadcasted_iota(jnp.int32, (LANES, LANES), 0)
    b = lax.broadcasted_iota(jnp.int32, (LANES, LANES), 1)
    stacked = jnp.concatenate(tiles, axis=0)
    inside = dot(stacked.astype(BF16), (a < b).astype(BF16))
    sizes = jnp.sum(stacked, axis=1, keepdims=True)
    offset, ranks = jnp.zeros((classes, 1), F32), []
    for t in range(len(tiles)):
        span = slice(t * classes, (t + 1) * classes)
        ranks.append(inside[span] + offset)
        offset = offset + sizes[span]
    return jnp.concatenate(ranks, axis=1)


def pick_rows(position, first, count, rows):
    slots = lax.broadcasted_iota(jnp.int32, (count, rows), 0) + first
    return (slots == position).astype(BF16)


def pack_kernel(senders, per_owner, visits_dev, where_ref, ids_ref, x_hbm, out_ref, x_ref, sem):
    copy = pltpu.make_async_copy(x_hbm, x_ref, sem)
    copy.start()
    rows = x_ref.shape[0]
    cap_rows = rows // senders
    ids = jnp.concatenate([ids_ref[i : i + 1, :] for i in range(ids_ref.shape[0])], axis=1)
    owners = lax.broadcasted_iota(jnp.int32, (senders, rows), 0)
    hot = (ids >= owners * per_owner) & (ids < (owners + 1) * per_owner)
    hot_f = hot.astype(F32)
    before = rank_before(hot_f)
    base = (owners * cap_rows + 1).astype(F32)
    position = (jnp.sum(hot_f * (base + before), axis=0, keepdims=True)).astype(jnp.int32) - 1
    first = (owners * per_owner + where_ref[1] * visits_dev).astype(F32)
    label = jnp.sum(hot_f * (ids.astype(F32) - first + 1.0), axis=0, keepdims=True)
    label = jnp.broadcast_to(label, (LANES, rows)).astype(BF16)
    copy.wait()
    step = rows // 3
    for c in range(3):
        chosen = pick_rows(position, c * step, step, rows)
        out_ref[c * step : (c + 1) * step, :D] = dot(chosen, x_ref[...]).astype(BF16)
        out_ref[c * step : (c + 1) * step, D:] = dot(chosen, label, NT).astype(BF16)


def prep_kernel(visits_dev, patient_ref, treat_ref, target_ref, meta_ref, row_ref):
    rows, lanes = meta_ref.shape
    slot = lax.broadcasted_iota(jnp.int32, (rows, lanes), 0)
    lane = lax.broadcasted_iota(jnp.int32, (rows, lanes), 1)
    place = lax.broadcasted_iota(jnp.int32, (VPAD, rows), 1)
    meta = jnp.where(lane == 2, -1.0, jnp.zeros((rows, lanes), F32))
    line = jnp.full((VPAD, rows), -1.0, F32)
    for g in range(patient_ref.shape[0]):
        at = (g // visits_dev) * VPAD + g % visits_dev
        patient = patient_ref[g].astype(F32)
        here = jnp.where(
            lane == 0, treat_ref[g].astype(F32), jnp.where(lane == 1, target_ref[g], patient)
        )
        meta = jnp.where((slot == at) & (lane < 3), here, meta)
        line = jnp.where(place == at, patient, line)
    meta_ref[...] = meta
    row_ref[...] = line


def fold_kernel(weight_ref, head_ref, ffn_ref, out_ref):
    rows = ffn_ref.shape[0]
    out_ref[:rows, :] = ffn_ref[...]
    folded = dot(head_ref[...], weight_ref[...], NT)
    folded = folded[0:2] + folded[2:4] + folded[4:6]
    one = folded.astype(BF16).astype(F32)
    two = (folded - one).astype(BF16).astype(F32)
    three = folded - one - two
    blank = jnp.zeros((FW_ROWS - 6, folded.shape[1]), F32)
    out_ref[rows:, :] = jnp.concatenate([one, two, three, blank], axis=0).astype(BF16)


def encode_kernel(
    visits_dev,
    count_ref,
    gain_ref,
    got_hbm,
    qkv_ref,
    proj_ref,
    vec_ref,
    got_ref,
    wqk,
    wv,
    wo,
    normed,
    qk,
    pbar,
    ctx,
    sems,
):
    rows = got_ref.shape[0]
    slots = visits_dev * VB
    inputs = [
        pltpu.make_async_copy(got_hbm.at[:, D:], got_ref.at[:, D:], sems.at[3]),
        pltpu.make_async_copy(got_hbm.at[:, :D], got_ref.at[:, :D], sems.at[4]),
    ]
    copies = [
        pltpu.make_async_copy(qkv_ref.at[:, : 2 * D], wqk, sems.at[0]),
        pltpu.make_async_copy(qkv_ref.at[:, 2 * D :], wv, sems.at[1]),
        pltpu.make_async_copy(proj_ref, wo, sems.at[2]),
    ]
    for copy in inputs + copies:
        copy.start()
    inputs[0].wait()
    lane0 = (lax.broadcasted_iota(jnp.int32, (VPAD, LANES), 1) == 0).astype(BF16)
    label = dot(lane0, got_ref[:, D:], NT)[:1]
    visits = lax.broadcasted_iota(jnp.int32, (VPAD, rows), 0)
    hot = label == (visits + 1).astype(F32)
    hot_b = hot.astype(BF16)
    hot_f = hot.astype(F32)
    before = rank_before(hot_f)
    base = (visits * VB + 1).astype(F32)
    position = (jnp.sum(hot_f * (base + before), axis=0, keepdims=True)).astype(jnp.int32) - 1
    inputs[1].wait()
    sums = dot(hot_b, got_ref[:, :D])
    gain = gain_ref[...]
    step = 2 * VB
    for c in range(slots // step):
        part = dot(pick_rows(position, c * step, step, rows), got_ref[:, :D])
        scale = lax.rsqrt(jnp.mean(part * part, axis=-1, keepdims=True) + EPS)
        normed[c * step : (c + 1) * step, :] = (part * scale * gain).astype(BF16)
    copies[0].wait()
    wide = 512
    for c in range(2 * D // wide):
        cols = slice(c * wide, (c + 1) * wide)
        qk[:, cols] = dot(normed[...], wqk[:, cols]).astype(BF16)

    lanes = lax.broadcasted_iota(jnp.int32, (VB, LANES), 1)
    low = (lanes < HDIM).astype(F32) * HDIM ** (-0.5)
    high = (lanes >= HDIM).astype(F32) * HDIM ** (-0.5)
    key_slot = lax.broadcasted_iota(jnp.int32, (VB, 2 * VB), 0)
    query_lane = lax.broadcasted_iota(jnp.int32, (1, 2 * VB), 1)
    query_slot = jnp.where(query_lane >= VB, query_lane - VB, query_lane)
    rows8 = lax.broadcasted_iota(jnp.int32, (VPAD, 2 * VB), 0)
    lanes8 = lax.broadcasted_iota(jnp.int32, (VPAD, 2 * VB), 1)
    halves = ((lanes8 >= rows8 * VB) & (lanes8 < (rows8 + 1) * VB)).astype(BF16)

    def one_visit(v, carry):
        count = count_ref[v]
        at = slice(v * VB, (v + 1) * VB)
        live_key = key_slot < count
        weight = (query_slot < count).astype(F32) / count.astype(F32)
        for p in range(HEADS // 2):
            q = qk[at, p * LANES : (p + 1) * LANES].astype(F32)
            k = qk[at, D + p * LANES : D + (p + 1) * LANES]
            both = jnp.concatenate([(q * low).astype(BF16), (q * high).astype(BF16)], axis=0)
            scores = jnp.where(live_key, dot(k, both, NT), -1e30)
            top = jnp.max(scores, axis=0, keepdims=True)
            grown = jnp.exp(scores - top)
            total = jnp.sum(grown, axis=0, keepdims=True)
            shares = (grown * (weight / total)).astype(BF16)
            pbar[v, 2 * p : 2 * p + 2, :] = dot(halves, shares, NT)[:2]
        ctx[v] = dot(pbar[v].astype(BF16), normed[at, :]).astype(BF16)
        return carry

    for v in range(visits_dev):
        one_visit(v, 0)
    copies[1].wait()
    copies[2].wait()
    vals = dot(ctx[...].reshape(visits_dev * HEADS, D), wv[...]).reshape(visits_dev, HEADS, D)
    head_row = lax.broadcasted_iota(jnp.int32, (1, HEADS, D), 1) * HDIM
    col = lax.broadcasted_iota(jnp.int32, (1, HEADS, D), 2)
    own = (col >= head_row) & (col < head_row + HDIM)
    attended = jnp.sum(jnp.where(own, vals, 0.0), axis=1)
    attended = jnp.concatenate([attended, jnp.zeros((VPAD - visits_dev, D), F32)], axis=0)
    head_part = attended.astype(BF16)
    rest = (attended - head_part.astype(F32)).astype(BF16)
    mixed = dot(head_part, wo[...]) + dot(rest, wo[...])
    row = lax.broadcasted_iota(jnp.int32, (VPAD, 1), 0)
    inverse = jnp.zeros((VPAD, 1), F32)
    for v in range(visits_dev):
        inverse = jnp.where(row == v, 1.0 / count_ref[v].astype(F32), inverse)
    mean_input = sums * inverse
    vec_ref[:, :D] = (mean_input + mixed).astype(BF16)
    vec_ref[:, D:] = mean_input.astype(BF16)


def rms_factor(values):
    return lax.rsqrt(jnp.mean(values * values, axis=-1, keepdims=True) + EPS)


def fetch(pieces, scratch, sems, first=0):
    copies = [
        pltpu.make_async_copy(piece, buffer, sems.at[first + i])
        for i, (piece, buffer) in enumerate(zip(pieces, scratch, strict=True))
    ]
    for copy in copies:
        copy.start()
    return copies


def project_kernel(n_mp, n_ev, plan, where_ref, *refs):
    n = len(plan)
    vec_in, (gain_ref, meta_ref, patient_ref), refs = refs[:n_mp], refs[n_mp : n_mp + 3], refs[n_mp + 3 :]
    pieces, refs = refs[:n], refs[n:]
    attended_ref, state, refs = refs[0], refs[1], refs[2:]
    scratch, refs = refs[:n], refs[n:]
    vec, blocks, sems, kept, out_sems = refs
    copies = fetch(pieces, scratch, sems)
    e, m = where_ref[0], where_ref[1]
    cols = attended_ref.shape[1]
    saves = [
        pltpu.make_async_copy(kept.at[:, lo:hi], state.at[:, lo:hi], out_sems.at[i])
        for i, (lo, hi) in enumerate(state_spans(cols))
    ]
    for k in range(n_mp):
        vec[m ^ k] = vec_in[k][...]
    rows = n_mp * VPAD
    full = vec[...].astype(F32).reshape(rows, DV)
    kept[:, :DV] = full
    saves[0].start()
    normed = (full * rms_factor(full) * gain_ref[...]).astype(BF16)
    width = DV // n_ev
    for j in range(n_ev):
        blocks[j] = normed[:, j * width : (j + 1) * width]
    totals = [jnp.zeros((rows, cols), F32) for _ in range(3)]
    for i, (k, lo, size) in enumerate(plan):
        copies[i].wait()
        block = blocks[e ^ k][:, lo : lo + size]
        for t in range(3):
            totals[t] = totals[t] + dot(block, scratch[i][t, :size, :])
    parts = [total.astype(BF16) for total in totals]
    for t in range(3):
        kept[:, DV + t * cols : DV + (t + 1) * cols] = parts[t].astype(F32)
    saves[1].start()
    q_at = lax.broadcasted_iota(jnp.int32, (rows, rows), 0)
    k_at = lax.broadcasted_iota(jnp.int32, (rows, rows), 1)
    allowed = (meta_ref[:, 2:3] == patient_ref[0:1, :]) & (k_at <= q_at)
    for h in range(cols // VHDIM):
        span = slice(h * VHDIM, (h + 1) * VHDIM)
        scores = dot(parts[0][:, span], parts[1][:, span], NT) * VHDIM ** (-0.5)
        scores = jnp.where(allowed, scores, -1e30)
        grown = jnp.exp(scores - jnp.max(scores, axis=-1, keepdims=True))
        prob = grown / jnp.sum(grown, axis=-1, keepdims=True)
        kept[:, DV + 3 * cols + h * rows : DV + 3 * cols + (h + 1) * rows] = prob
        attended_ref[:, span] = dot(prob.astype(BF16), parts[2][:, span]).astype(BF16)
    saves[2].start()
    for save in saves:
        save.wait()


def state_spans(cols):
    return ((0, DV), (DV, DV + 3 * cols), (DV + 3 * cols, DV + 3 * cols + LANES))


def pack_scalars(columns, rows):
    lane = lax.broadcasted_iota(jnp.int32, (rows, LANES), 1)
    spread = jnp.zeros((rows, LANES), F32)
    for c, column in enumerate(columns):
        at = (lane == c) | (lane == 8 + c) | (lane == 16 + c)
        spread = jnp.where(at, column, spread)
    one = spread.astype(BF16).astype(F32)
    two = (spread - one).astype(BF16).astype(F32)
    three = spread - one - two
    return jnp.where(lane < 8, one, jnp.where(lane < 16, two, three)).astype(BF16)


def unpack_scalar(packed, c):
    return packed[:, c : c + 1] + packed[:, 8 + c : 9 + c] + packed[:, 16 + c : 17 + c]


def ffn_kernel(
    n_mp, n_ev, plan, where_ref, bias_ref, gain_ref, meta_ref, head_ref, *refs
):
    n = len(plan)
    attn_in, state, refs = refs[:n_mp], refs[n_mp], refs[n_mp + 1 :]
    pieces, refs = refs[:n], refs[n:]
    outs, mid_ref, refs = refs[:n_mp], refs[n_mp], refs[n_mp + 1 :]
    scratch, refs = refs[:n], refs[n:]
    attn, vec_ref, blocks, grads, sems = refs
    e, m = where_ref[0], where_ref[1]
    cols = DV // n_mp
    small = fetch([state.at[:, :DV]], [vec_ref], sems, n)
    copies = fetch(pieces, scratch, sems)
    for k in range(n_mp):
        attn[m ^ k] = attn_in[k][...]
    for copy in small:
        copy.wait()
    rows = vec_ref.shape[0]
    mid = vec_ref[...] + jnp.concatenate([attn[k] for k in range(n_mp)], axis=1).astype(F32)
    at = pl.ds(pl.multiple_of(m * cols, cols), cols)
    factor = rms_factor(mid)
    mid_ref[:, :cols] = vec_ref[:, at] + attn[m].astype(F32)
    mid_ref[:, cols:] = jnp.broadcast_to(factor, (rows, LANES))
    gain = gain_ref[...]
    normed = (mid * factor * gain).astype(BF16)
    width = DV // n_ev
    for j in range(n_ev):
        blocks[j] = normed[:, j * width : (j + 1) * width]
    hidden = scratch[0].shape[1]
    pre = jnp.zeros((rows, hidden), F32)
    fw = jnp.zeros((2, hidden), F32)
    for i, (k, lo, size) in enumerate(plan):
        copies[i].wait()
        pre = pre + dot(blocks[e ^ k][:, lo : lo + size], scratch[i][:size, :])
        if scratch[i].shape[0] > size:
            parts = scratch[i][size : size + FW_ROWS, :].astype(F32)
            fw = fw + (parts[0:2] + parts[2:4] + parts[4:6])
    sigma = 1.0 / (1.0 + jnp.exp(-pre))
    act = (pre * sigma).astype(BF16).astype(F32)
    first = (m == 0).astype(F32)
    outcome = []
    for j in range(2):
        base = jnp.sum(mid * head_ref[j : j + 1, :], axis=-1, keepdims=True) + bias_ref[j]
        outcome.append(jnp.sum(act * fw[j : j + 1, :], axis=-1, keepdims=True) + first * base)
    chosen = jnp.where(meta_ref[:, 0:1] > 0.5, fw[1:2, :], fw[0:1, :])
    slope = (chosen * sigma * (1.0 + pre * (1.0 - sigma))).astype(BF16)
    moment = jnp.sum(slope.astype(F32) * pre, axis=-1, keepdims=True) / factor
    for i, (k, lo, size) in enumerate(plan):
        grads[e ^ k, :, lo : lo + size] = dot(slope, scratch[i][:size, :], NT)
    scalars = pack_scalars([outcome[0], outcome[1], moment], rows)
    each = n_ev // n_mp
    for k in range(n_mp):
        for j in range(each):
            outs[k][:, j * width : (j + 1) * width] = grads[(m ^ k) * each + j].astype(BF16)
        outs[k][:, cols:] = scalars


def back_kernel(
    n_mp, n_ev, plan, where_ref, mid_ref, meta_ref, gain_ref, vgain_ref, head_ref, *refs
):
    n = len(plan)
    pay_in, state, refs = refs[:n_mp], refs[n_mp], refs[n_mp + 1 :]
    pieces, refs = refs[:n], refs[n:]
    outs, outcome_ref, coef_ref, refs = refs[:n_mp], refs[n_mp], refs[n_mp + 1], refs[n_mp + 2 :]
    scratch, refs = refs[:n], refs[n:]
    kept, grads, table, sems = refs
    (stored,) = fetch([state], [kept], sems, n)
    copies = fetch(pieces, scratch, sems)
    e, m = where_ref[0], where_ref[1]
    rows = mid_ref.shape[0]
    cols = DV // n_mp
    total = pay_in[0][...].astype(F32)
    for k in range(1, n_mp):
        total = total + pay_in[k][...].astype(F32)
    packed = total[:, cols:]
    outcome = [unpack_scalar(packed, 0), unpack_scalar(packed, 1)]
    moment = unpack_scalar(packed, 2) * (1.0 / DV)
    lane = lax.broadcasted_iota(jnp.int32, (rows, LANES), 1)
    outcome_ref[...] = jnp.where(lane == 0, outcome[0], outcome[1])
    treated = meta_ref[:, 0:1] > 0.5
    delta = 4096.0 * (jnp.where(treated, outcome[1], outcome[0]) - meta_ref[:, 1:2])
    factor = mid_ref[:, cols : cols + 1]
    at = pl.ds(pl.multiple_of(m * cols, cols), cols)
    mid = mid_ref[:, :cols]
    head = jnp.where(treated, head_ref[1:2, at], head_ref[0:1, at])
    scaled = total[:, :cols] * gain_ref[:, at]
    grad_mid = delta * (head + factor * (scaled - mid * (factor * factor * moment)))
    grad_c = grad_mid.astype(BF16)
    stored.wait()
    queries, keys, values = (
        kept[:, DV + t * cols : DV + (t + 1) * cols].astype(BF16) for t in range(3)
    )
    three = [[], [], []]
    for h in range(cols // VHDIM):
        span = slice(h * VHDIM, (h + 1) * VHDIM)
        prob = kept[:, DV + 3 * cols + h * rows : DV + 3 * cols + (h + 1) * rows]
        grad_p = dot(grad_c[:, span], values[:, span], NT)
        grad_s = prob * (grad_p - jnp.sum(grad_p * prob, axis=-1, keepdims=True))
        grad_s = (grad_s * VHDIM ** (-0.5)).astype(BF16)
        three[0].append(dot(grad_s, keys[:, span]).astype(BF16))
        three[1].append(dot(grad_s, queries[:, span], TN).astype(BF16))
        three[2].append(dot(prob.astype(BF16), grad_c[:, span], TN).astype(BF16))
    three = [jnp.concatenate(parts, axis=1) for parts in three]
    for i, (k, lo, size) in enumerate(plan):
        copies[i].wait()
        part = dot(three[0], scratch[i][0, :size, :], NT)
        part = part + dot(three[1], scratch[i][1, :size, :], NT)
        part = part + dot(three[2], scratch[i][2, :size, :], NT)
        grads[e ^ k, :, lo : lo + size] = part
    width = DV // n_ev
    vec = kept[:, :DV]
    spread = rms_factor(vec)
    moment = jnp.zeros((rows, 1), F32)
    for t in range(3):
        forward = kept[:, DV + t * cols : DV + (t + 1) * cols]
        moment = moment + jnp.sum(three[t].astype(F32) * forward, axis=-1, keepdims=True)
    moment = moment / spread
    for j in range(D // width):
        span = slice(j * width, (j + 1) * width)
        scaled = grads[j] * vgain_ref[:, span]
        table[:, :, span] = (scaled * spread).reshape(n_mp, VPAD, width)

    @pl.when(m * cols < D)
    def _():
        here = pl.ds(pl.multiple_of(m * cols, cols), cols)
        table[:, :, here] = table[:, :, here] + grad_mid.reshape(n_mp, VPAD, cols)

    scalars = pack_scalars([moment], rows).astype(F32)
    table[:, :, D:] = scalars.reshape(n_mp, VPAD, LANES)
    for k in range(n_mp):
        outs[k][...] = table[m ^ k].astype(BF16)
    table[:, :, :D] = (vec[:, :D] * (spread * spread * spread * (1.0 / DV))).reshape(n_mp, VPAD, D)
    coef_ref[...] = table[m][:, :D]


def finish_kernel(n_mp, visits_dev, count_ref, coef_ref, *refs):
    pays, out_ref = refs[:n_mp], refs[n_mp]
    total = pays[0][...].astype(F32)
    for k in range(1, n_mp):
        total = total + pays[k][...].astype(F32)
    grad = total[:, :D] - coef_ref[...] * unpack_scalar(total[:, D:], 0)
    row = lax.broadcasted_iota(jnp.int32, (VPAD, 1), 0)
    inverse = jnp.zeros((VPAD, 1), F32)
    for v in range(visits_dev):
        inverse = jnp.where(row == v, 1.0 / count_ref[v].astype(F32), inverse)
    out_ref[...] = (grad * inverse).astype(BF16).astype(F32)


def spread_kernel(n_ev, pick, *refs):
    tables, out, rows_ref, out_sems = refs[:n_ev], *refs[n_ev:]
    table = jnp.concatenate([each[...] for each in tables], axis=0).astype(BF16)
    rows = rows_ref.shape[0]
    step = rows // 3
    saves = []
    for c in range(3):
        span = slice(c * step, (c + 1) * step)
        rows_ref[span, :] = dot(pick[span, :], table).astype(BF16)
        saves.append(pltpu.make_async_copy(rows_ref.at[span, :], out.at[span, :], out_sems.at[c]))
        saves[c].start()
    for save in saves:
        save.wait()


def swap(x, axis, size, k):
    return lax.ppermute(x, axis, [(i, i ^ k) for i in range(size)])


def first_hop(shard, n_ev):
    if n_ev != 8:
        return [shard] + [swap(shard, "events", n_ev, k) for k in range(1, n_ev)]
    return [shard, swap(shard, "events", n_ev, 2), swap(shard, "events", n_ev, 4)]


def halves_kernel(low_ref, high_ref, low_out, high_out):
    half = low_out.shape[0]
    low_out[...] = low_ref[...]
    high_out[...] = high_ref[half:, :]


def halves_of(pieces, half):
    rows, cols = pieces[1].shape
    low = pl.BlockSpec((half, cols), lambda i: (0, 0))
    return pl.pallas_call(
        halves_kernel,
        grid=(1,),
        out_shape=[
            jax.ShapeDtypeStruct((half, cols), BF16),
            jax.ShapeDtypeStruct((rows - half, cols), BF16),
        ],
        in_specs=[low, vmem()],
        out_specs=[low, vmem()],
        compiler_params=params(SNUG),
        cost_estimate=cost(0),
        name="halves",
    )(pieces[1], pieces[2])


def split_kernel(half, low_ref, high_ref, low_out, high_out, low, high, sems):
    rows = high_ref.shape[1]
    sources = [low_ref.at[:, :half, :], high_ref.at[:, half:rows, :]]
    copies = fetch(sources, [low, high], sems)
    saves = []
    for i, (buffer, out) in enumerate(((low, low_out), (high, high_out))):
        copies[i].wait()
        saves += fetch([buffer], [out], sems, 2 + i)
    for save in saves:
        save.wait()


def split_of(pieces, half):
    lead, rows, cols = pieces[1].shape
    return pl.pallas_call(
        functools.partial(split_kernel, half),
        out_shape=[
            jax.ShapeDtypeStruct((lead, half, cols), BF16),
            jax.ShapeDtypeStruct((lead, rows - half, cols), BF16),
        ],
        in_specs=[hbm()] * 2,
        out_specs=[hbm()] * 2,
        scratch_shapes=[
            pltpu.VMEM((lead, half, cols), BF16),
            pltpu.VMEM((lead, rows - half, cols), BF16),
            pltpu.SemaphoreType.DMA((4,)),
        ],
        compiler_params=params(SNUG),
        cost_estimate=cost(0),
        name="split",
    )(pieces[1], pieces[2])


def second_hop(low, high, n_ev):
    return [swap(low, "events", n_ev, 4), swap(high, "events", n_ev, 2)]


def across(pieces, n_ev):
    return [swap(piece, "events", n_ev, 1) for piece in pieces]


def direct_plan(n_ev, width):
    order = range(n_ev) if n_ev != 8 else (0, 2, 4, 6, 1, 3, 5, 7)
    return [(k, 0, width) for k in order]


def hop_plan(n_ev, width):
    if n_ev != 8:
        return direct_plan(n_ev, width)
    half = width // 2
    near = [(0, 0, width), (2, 0, width), (4, 0, width), (6, 0, half), (6, half, half)]
    return near + [(k ^ 1, lo, size) for k, lo, size in near]


def event_order(n_ev):
    return list(range(n_ev)) if n_ev != 8 else [0, 2, 4, 6, 1, 3, 5, 7]


def gather_events(block, n_ev):
    if n_ev != 8:
        return [block] + [swap(block, "events", n_ev, k) for k in range(1, n_ev)]
    near = [block] + [swap(block, "events", n_ev, k) for k in (2, 4, 6)]
    return near + across(near, n_ev)


def local(
    event_x,
    event_visit,
    visit_count,
    visit_patient,
    treatment,
    outcome_target,
    enc_gain,
    enc_qkv,
    enc_out,
    visit_gain,
    visit_qkv,
    ffn_gain,
    ffn_in,
    ffn_out,
    head_weight,
    head_bias,
):
    n_ev = lax.axis_size("events")
    n_mp = lax.axis_size("mp")
    e = lax.axis_index("events")
    m = lax.axis_index("mp")
    rows_dev = event_x.shape[0]
    visits_dev = visit_count.shape[0]
    per_owner = visits_dev * n_mp
    group = n_mp * VPAD
    cols = DV // n_mp
    hidden = ffn_in.shape[1]
    where = jnp.stack([e, m]).astype(jnp.int32)
    ids = event_visit.reshape(rows_dev // LANES, LANES)

    send = pl.pallas_call(
        functools.partial(pack_kernel, n_ev, per_owner, visits_dev),
        out_shape=jax.ShapeDtypeStruct((rows_dev, D + LANES), BF16),
        in_specs=[smem(), vmem(), hbm()],
        out_specs=vmem(),
        scratch_shapes=[pltpu.VMEM((rows_dev, D), BF16), pltpu.SemaphoreType.DMA],
        compiler_params=params(12),
        cost_estimate=cost(0),
        name="pack",
    )(where, ids, event_x)
    got = lax.all_to_all(
        send.reshape(n_ev, rows_dev // n_ev, D + LANES), "events", split_axis=0, concat_axis=0,
        tiled=True,
    ).reshape(rows_dev, D + LANES)

    qkv_first = first_hop(visit_qkv, n_ev)

    head_t = head_weight.T
    width = DV // n_ev
    own_head = lax.dynamic_slice_in_dim(head_t, e * width, width, 1)
    head_hi = own_head.astype(BF16)
    head_mid = (own_head - head_hi.astype(F32)).astype(BF16)
    head_lo = (own_head - head_hi.astype(F32) - head_mid.astype(F32)).astype(BF16)
    heads = jnp.concatenate([head_hi, head_mid, head_lo, jnp.zeros((2, width), BF16)], axis=0)
    meta, patient_row = pl.pallas_call(
        functools.partial(prep_kernel, visits_dev),
        out_shape=[
            jax.ShapeDtypeStruct((group, LANES), F32),
            jax.ShapeDtypeStruct((VPAD, group), F32),
        ],
        in_specs=[smem()] * 3,
        out_specs=[vmem()] * 2,
        compiler_params=params(4),
        cost_estimate=cost(0),
        name="prep",
    )(visit_patient, treatment, outcome_target)
    two_hops = n_ev == 8
    inner = jnp.arange(VPAD, dtype=jnp.int32)
    named = (jnp.array(event_order(n_ev), jnp.int32) ^ e)[:, None] * per_owner
    named = jnp.where(inner < visits_dev, named + m * visits_dev + inner[None, :], -2).reshape(-1)
    chosen = (event_visit[:, None] == named[None, :]).astype(BF16)
    ready = [meta, patient_row, head_t, chosen]
    if two_hops:
        qkv_halves = split_of(qkv_first, width // 2)
        qkv_far = across(qkv_first, n_ev)
        ready += [*qkv_halves, *qkv_far]
    ffn_shard = pl.pallas_call(
        fold_kernel,
        out_shape=jax.ShapeDtypeStruct((width + FW_ROWS, hidden), BF16),
        in_specs=[vmem()] * 3,
        out_specs=vmem(),
        compiler_params=params(SNUG),
        cost_estimate=cost(30),
        name="fold",
    )(ffn_out, heads, after(ffn_in, *ready))
    qkv_plan = hop_plan(n_ev, width)
    ffn_plan = hop_plan(n_ev, width)
    gate = [got]
    if two_hops:
        qkv_second = second_hop(*qkv_halves, n_ev)
        qkv_far += across(qkv_second, n_ev)
        ffn_far = across([ffn_shard], n_ev)
        gate += qkv_second
    ffn_first = [ffn_shard] + first_hop(after(ffn_shard, *gate), n_ev)[1:]
    if two_hops:
        got = after(got, *ffn_far, *qkv_far)
    vec = pl.pallas_call(
        functools.partial(encode_kernel, visits_dev),
        out_shape=jax.ShapeDtypeStruct((VPAD, DV), BF16),
        in_specs=[smem(), vmem(), hbm(), hbm(), hbm()],
        out_specs=vmem(),
        scratch_shapes=[
            pltpu.VMEM((rows_dev, D + LANES), BF16),
            pltpu.VMEM((D, 2 * D), BF16),
            pltpu.VMEM((D, D), BF16),
            pltpu.VMEM((D, D), BF16),
            pltpu.VMEM((visits_dev * VB, D), BF16),
            pltpu.VMEM((visits_dev * VB, 2 * D), BF16),
            pltpu.VMEM((visits_dev, HEADS, VB), F32),
            pltpu.VMEM((visits_dev, HEADS, D), BF16),
            pltpu.SemaphoreType.DMA((5,)),
        ],
        compiler_params=params(53),
        cost_estimate=cost(0),
        name="encode",
    )(visit_count, enc_gain.reshape(1, D), got, enc_qkv, enc_out)

    vecs = [vec] + [swap(vec, "mp", n_mp, k) for k in range(1, n_mp)]
    if two_hops:
        qkv_pieces = qkv_first + qkv_second + qkv_far
        ffn_next = [ffn_first[0]] + [after(piece, *vecs[1:]) for piece in ffn_first[1:]]
        ffn_second = second_hop(*halves_of(ffn_next, width // 2), n_ev)
        ffn_far += across(ffn_next[1:], n_ev)
        vecs[0] = after(vec, *ffn_far[1:])
    else:
        qkv_pieces = qkv_first
    n_q = len(qkv_plan)
    vgain = visit_gain.reshape(1, DV)
    state_shape = (group, state_spans(cols)[2][1])
    attended, state = pl.pallas_call(
        functools.partial(project_kernel, n_mp, n_ev, qkv_plan),
        out_shape=[
            jax.ShapeDtypeStruct((group, cols), BF16),
            jax.ShapeDtypeStruct(state_shape, F32),
        ],
        in_specs=[smem()] + [vmem()] * (n_mp + 3) + [hbm()] * n_q,
        out_specs=[vmem(), hbm()],
        scratch_shapes=[pltpu.VMEM(piece.shape, BF16) for piece in qkv_pieces]
        + [
            pltpu.VMEM((n_mp, VPAD, DV), BF16),
            pltpu.VMEM((n_ev, group, width), BF16),
            pltpu.SemaphoreType.DMA((n_q,)),
            pltpu.VMEM(state_shape, F32),
            pltpu.SemaphoreType.DMA((3,)),
        ],
        compiler_params=params(SNUG),
        cost_estimate=cost(0),
        name="project",
    )(where, *vecs, vgain, meta, patient_row, *qkv_pieces)

    attns = [attended] + [swap(attended, "mp", n_mp, k) for k in range(1, n_mp)]
    if two_hops:
        ffn_second = [after(piece, *attns[1:]) for piece in ffn_second]
        ffn_pieces = ffn_first + ffn_second + ffn_far + across(ffn_second, n_ev)
    else:
        ffn_pieces = ffn_first
    n_f = len(ffn_plan)
    fgain = ffn_gain.reshape(1, DV)
    ffn_outs = pl.pallas_call(
        functools.partial(ffn_kernel, n_mp, n_ev, ffn_plan),
        out_shape=[jax.ShapeDtypeStruct((group, cols + LANES), BF16)] * n_mp
        + [jax.ShapeDtypeStruct((group, cols + LANES), F32)],
        in_specs=[smem()] * 2 + [vmem()] * (3 + n_mp) + [hbm()] * (1 + n_f),
        out_specs=[vmem()] * (n_mp + 1),
        scratch_shapes=[pltpu.VMEM(piece.shape, BF16) for piece in ffn_pieces]
        + [
            pltpu.VMEM((n_mp, group, cols), BF16),
            pltpu.VMEM((group, DV), F32),
            pltpu.VMEM((n_ev, group, width), BF16),
            pltpu.VMEM((n_ev, group, width), F32),
            pltpu.SemaphoreType.DMA((n_f + 1,)),
        ],
        compiler_params=params(SNUG),
        cost_estimate=cost(0),
        name="ffn",
    )(where, head_bias, fgain, meta, head_t, *attns, state, *ffn_pieces)
    mid = ffn_outs[n_mp]
    pays = [ffn_outs[0]] + [swap(ffn_outs[k], "mp", n_mp, k) for k in range(1, n_mp)]

    back_outs = pl.pallas_call(
        functools.partial(back_kernel, n_mp, n_ev, qkv_plan),
        out_shape=[jax.ShapeDtypeStruct((VPAD, D + LANES), BF16)] * n_mp
        + [jax.ShapeDtypeStruct((group, LANES), F32), jax.ShapeDtypeStruct((VPAD, D), F32)],
        in_specs=[smem()] + [vmem()] * (5 + n_mp) + [hbm()] * (1 + n_q),
        out_specs=[vmem()] * (n_mp + 2),
        scratch_shapes=[pltpu.VMEM(piece.shape, BF16) for piece in qkv_pieces]
        + [
            pltpu.VMEM(state_shape, F32),
            pltpu.VMEM((n_ev, group, width), F32),
            pltpu.VMEM((n_mp, VPAD, D + LANES), F32),
            pltpu.SemaphoreType.DMA((n_q + 1,)),
        ],
        compiler_params=params(SNUG),
        cost_estimate=cost(0),
        name="back",
    )(where, mid, meta, fgain, vgain, head_t, *pays, state, *qkv_pieces)
    outcomes = back_outs[n_mp][:, :2].reshape(n_mp, VPAD, 2)[:, :visits_dev].reshape(per_owner, 2)
    shares = [back_outs[0]] + [swap(back_outs[k], "mp", n_mp, k) for k in range(1, n_mp)]
    visit_grad = pl.pallas_call(
        functools.partial(finish_kernel, n_mp, visits_dev),
        out_shape=jax.ShapeDtypeStruct((VPAD, D), F32),
        in_specs=[smem()] + [vmem()] * (1 + n_mp),
        out_specs=vmem(),
        compiler_params=params(4),
        cost_estimate=cost(0),
        name="finish",
    )(visit_count, after(back_outs[n_mp + 1], outcomes), *shares)

    tables = gather_events(visit_grad, n_ev)
    event_grads = pl.pallas_call(
        functools.partial(spread_kernel, n_ev),
        out_shape=jax.ShapeDtypeStruct((rows_dev, D), BF16),
        in_specs=[vmem()] * (n_ev + 1),
        out_specs=hbm(),
        scratch_shapes=[
            pltpu.VMEM((rows_dev, D), BF16),
            pltpu.SemaphoreType.DMA((3,)),
        ],
        compiler_params=params(8),
        cost_estimate=cost(0),
        name="spread",
    )(chosen, *tables)
    return (outcomes, event_grads)


def solution(mesh):
    in_specs = (
        P(("events", "mp"), None),
        P(("events", "mp")),
        P(("events", "mp")),
        P("events"),
        P("events"),
        P("events"),
        P(),
        P(),
        P(),
        P(),
        P(None, "events", "mp"),
        P(),
        P("events", "mp"),
        P("mp", "events"),
        P(),
        P(),
    )
    out_specs = (P("events", None), P(("events", "mp"), None))
    return jax.shard_map(local, mesh=mesh, in_specs=in_specs, out_specs=out_specs, check_vma=False)
```

```python
import functools

import jax
import jax.numpy as jnp
from jax import lax
from jax.experimental import pallas as pl
from jax.experimental.pallas import tpu as pltpu
from jax.sharding import PartitionSpec as P

D = 1024
HEADS = 16
HDIM = 64
VB = 128
DV = 2048
VHDIM = 128
VPAD = 8
FW_ROWS = 16
SNUG = 48
LANES = 128
EPS = 1e-5
F32 = jnp.float32
BF16 = jnp.bfloat16

NT = (((1,), (1,)), ((), ()))
TN = (((0,), (0,)), ((), ()))
NN = (((1,), (0,)), ((), ()))


def dot(a, b, dims=NN):
    return lax.dot_general(a, b, dims, preferred_element_type=F32)


def vmem():
    return pl.BlockSpec(memory_space=pltpu.VMEM)


def smem():
    return pl.BlockSpec(memory_space=pltpu.SMEM)


def hbm():
    return pl.BlockSpec(memory_space=pltpu.HBM)


def params(mib):
    return pltpu.CompilerParams(vmem_limit_bytes=int(mib * 1024) * 1024)


def cost(micros):
    return pl.CostEstimate(
        flops=int(micros * 1e9) + 1, bytes_accessed=int(micros * 1e6) + 1, transcendentals=0
    )


def after(value, *others):
    return lax.optimization_barrier((value, *others))[0]


def rank_before(hot):
    classes, rows = hot.shape
    tiles = [hot[:, c : c + LANES] for c in range(0, rows, LANES)]
    a = lax.broadcasted_iota(jnp.int32, (LANES, LANES), 0)
    b = lax.broadcasted_iota(jnp.int32, (LANES, LANES), 1)
    stacked = jnp.concatenate(tiles, axis=0)
    inside = dot(stacked.astype(BF16), (a < b).astype(BF16))
    sizes = jnp.sum(stacked, axis=1, keepdims=True)
    offset, ranks = jnp.zeros((classes, 1), F32), []
    for t in range(len(tiles)):
        span = slice(t * classes, (t + 1) * classes)
        ranks.append(inside[span] + offset)
        offset = offset + sizes[span]
    return jnp.concatenate(ranks, axis=1)


def pick_rows(position, first, count, rows):
    slots = lax.broadcasted_iota(jnp.int32, (count, rows), 0) + first
    return (slots == position).astype(BF16)


def pack_kernel(senders, per_owner, visits_dev, where_ref, ids_ref, x_hbm, out_ref, x_ref, sem):
    copy = pltpu.make_async_copy(x_hbm, x_ref, sem)
    copy.start()
    rows = x_ref.shape[0]
    cap_rows = rows // senders
    ids = jnp.concatenate([ids_ref[i : i + 1, :] for i in range(ids_ref.shape[0])], axis=1)
    owners = lax.broadcasted_iota(jnp.int32, (senders, rows), 0)
    hot = (ids >= owners * per_owner) & (ids < (owners + 1) * per_owner)
    hot_f = hot.astype(F32)
    before = rank_before(hot_f)
    base = (owners * cap_rows + 1).astype(F32)
    position = (jnp.sum(hot_f * (base + before), axis=0, keepdims=True)).astype(jnp.int32) - 1
    first = (owners * per_owner + where_ref[1] * visits_dev).astype(F32)
    label = jnp.sum(hot_f * (ids.astype(F32) - first + 1.0), axis=0, keepdims=True)
    label = jnp.broadcast_to(label, (LANES, rows)).astype(BF16)
    copy.wait()
    step = rows // 3
    for c in range(3):
        chosen = pick_rows(position, c * step, step, rows)
        out_ref[c * step : (c + 1) * step, :D] = dot(chosen, x_ref[...]).astype(BF16)
        out_ref[c * step : (c + 1) * step, D:] = dot(chosen, label, NT).astype(BF16)


def prep_kernel(visits_dev, patient_ref, treat_ref, target_ref, meta_ref, row_ref):
    rows, lanes = meta_ref.shape
    slot = lax.broadcasted_iota(jnp.int32, (rows, lanes), 0)
    lane = lax.broadcasted_iota(jnp.int32, (rows, lanes), 1)
    place = lax.broadcasted_iota(jnp.int32, (VPAD, rows), 1)
    meta = jnp.where(lane == 2, -1.0, jnp.zeros((rows, lanes), F32))
    line = jnp.full((VPAD, rows), -1.0, F32)
    for g in range(patient_ref.shape[0]):
        at = (g // visits_dev) * VPAD + g % visits_dev
        patient = patient_ref[g].astype(F32)
        here = jnp.where(
            lane == 0, treat_ref[g].astype(F32), jnp.where(lane == 1, target_ref[g], patient)
        )
        meta = jnp.where((slot == at) & (lane < 3), here, meta)
        line = jnp.where(place == at, patient, line)
    meta_ref[...] = meta
    row_ref[...] = line


def fold_kernel(weight_ref, head_ref, ffn_ref, out_ref):
    rows = ffn_ref.shape[0]
    out_ref[:rows, :] = ffn_ref[...]
    folded = dot(head_ref[...], weight_ref[...], NT)
    folded = folded[0:2] + folded[2:4] + folded[4:6]
    one = folded.astype(BF16).astype(F32)
    two = (folded - one).astype(BF16).astype(F32)
    three = folded - one - two
    blank = jnp.zeros((FW_ROWS - 6, folded.shape[1]), F32)
    out_ref[rows:, :] = jnp.concatenate([one, two, three, blank], axis=0).astype(BF16)


def encode_kernel(
    visits_dev,
    count_ref,
    gain_ref,
    got_hbm,
    qkv_ref,
    proj_ref,
    vec_ref,
    got_ref,
    wqk,
    wv,
    wo,
    normed,
    qk,
    pbar,
    ctx,
    sems,
):
    rows = got_ref.shape[0]
    slots = visits_dev * VB
    inputs = [
        pltpu.make_async_copy(got_hbm.at[:, D:], got_ref.at[:, D:], sems.at[3]),
        pltpu.make_async_copy(got_hbm.at[:, :D], got_ref.at[:, :D], sems.at[4]),
    ]
    copies = [
        pltpu.make_async_copy(qkv_ref.at[:, : 2 * D], wqk, sems.at[0]),
        pltpu.make_async_copy(qkv_ref.at[:, 2 * D :], wv, sems.at[1]),
        pltpu.make_async_copy(proj_ref, wo, sems.at[2]),
    ]
    for copy in inputs + copies:
        copy.start()
    inputs[0].wait()
    lane0 = (lax.broadcasted_iota(jnp.int32, (VPAD, LANES), 1) == 0).astype(BF16)
    label = dot(lane0, got_ref[:, D:], NT)[:1]
    visits = lax.broadcasted_iota(jnp.int32, (VPAD, rows), 0)
    hot = label == (visits + 1).astype(F32)
    hot_b = hot.astype(BF16)
    hot_f = hot.astype(F32)
    before = rank_before(hot_f)
    base = (visits * VB + 1).astype(F32)
    position = (jnp.sum(hot_f * (base + before), axis=0, keepdims=True)).astype(jnp.int32) - 1
    inputs[1].wait()
    sums = dot(hot_b, got_ref[:, :D])
    gain = gain_ref[...]
    step = 2 * VB
    for c in range(slots // step):
        part = dot(pick_rows(position, c * step, step, rows), got_ref[:, :D])
        scale = lax.rsqrt(jnp.mean(part * part, axis=-1, keepdims=True) + EPS)
        normed[c * step : (c + 1) * step, :] = (part * scale * gain).astype(BF16)
    copies[0].wait()
    wide = 512
    for c in range(2 * D // wide):
        cols = slice(c * wide, (c + 1) * wide)
        qk[:, cols] = dot(normed[...], wqk[:, cols]).astype(BF16)

    lanes = lax.broadcasted_iota(jnp.int32, (VB, LANES), 1)
    low = (lanes < HDIM).astype(F32) * HDIM ** (-0.5)
    high = (lanes >= HDIM).astype(F32) * HDIM ** (-0.5)
    key_slot = lax.broadcasted_iota(jnp.int32, (VB, 2 * VB), 0)
    query_lane = lax.broadcasted_iota(jnp.int32, (1, 2 * VB), 1)
    query_slot = jnp.where(query_lane >= VB, query_lane - VB, query_lane)
    rows8 = lax.broadcasted_iota(jnp.int32, (VPAD, 2 * VB), 0)
    lanes8 = lax.broadcasted_iota(jnp.int32, (VPAD, 2 * VB), 1)
    halves = ((lanes8 >= rows8 * VB) & (lanes8 < (rows8 + 1) * VB)).astype(BF16)

    def one_visit(v, carry):
        count = count_ref[v]
        at = slice(v * VB, (v + 1) * VB)
        live_key = key_slot < count
        weight = (query_slot < count).astype(F32) / count.astype(F32)
        for p in range(HEADS // 2):
            q = qk[at, p * LANES : (p + 1) * LANES].astype(F32)
            k = qk[at, D + p * LANES : D + (p + 1) * LANES]
            both = jnp.concatenate([(q * low).astype(BF16), (q * high).astype(BF16)], axis=0)
            scores = jnp.where(live_key, dot(k, both, NT), -1e30)
            top = jnp.max(scores, axis=0, keepdims=True)
            grown = jnp.exp(scores - top)
            total = jnp.sum(grown, axis=0, keepdims=True)
            shares = (grown * (weight / total)).astype(BF16)
            pbar[v, 2 * p : 2 * p + 2, :] = dot(halves, shares, NT)[:2]
        ctx[v] = dot(pbar[v].astype(BF16), normed[at, :]).astype(BF16)
        return carry

    for v in range(visits_dev):
        one_visit(v, 0)
    copies[1].wait()
    copies[2].wait()
    vals = dot(ctx[...].reshape(visits_dev * HEADS, D), wv[...]).reshape(visits_dev, HEADS, D)
    head_row = lax.broadcasted_iota(jnp.int32, (1, HEADS, D), 1) * HDIM
    col = lax.broadcasted_iota(jnp.int32, (1, HEADS, D), 2)
    own = (col >= head_row) & (col < head_row + HDIM)
    attended = jnp.sum(jnp.where(own, vals, 0.0), axis=1)
    attended = jnp.concatenate([attended, jnp.zeros((VPAD - visits_dev, D), F32)], axis=0)
    head_part = attended.astype(BF16)
    rest = (attended - head_part.astype(F32)).astype(BF16)
    mixed = dot(head_part, wo[...]) + dot(rest, wo[...])
    row = lax.broadcasted_iota(jnp.int32, (VPAD, 1), 0)
    inverse = jnp.zeros((VPAD, 1), F32)
    for v in range(visits_dev):
        inverse = jnp.where(row == v, 1.0 / count_ref[v].astype(F32), inverse)
    mean_input = sums * inverse
    vec_ref[:, :D] = (mean_input + mixed).astype(BF16)
    vec_ref[:, D:] = mean_input.astype(BF16)


def rms_factor(values):
    return lax.rsqrt(jnp.mean(values * values, axis=-1, keepdims=True) + EPS)


def fetch(pieces, scratch, sems, first=0):
    copies = [
        pltpu.make_async_copy(piece, buffer, sems.at[first + i])
        for i, (piece, buffer) in enumerate(zip(pieces, scratch, strict=True))
    ]
    for copy in copies:
        copy.start()
    return copies


def fetch_parts(pieces, plan, scratch, sems):
    copies = []
    for (_, parts), buffer in zip(plan, scratch, strict=True):
        group = []
        for i, first, rows in parts:
            span = slice(first, first + rows)
            place = buffer.at[:, span, :] if len(buffer.shape) == 3 else buffer.at[span, :]
            group.append(pltpu.make_async_copy(pieces[i], place, sems.at[i]))
            group[-1].start()
        copies.append(group)
    return copies


def project_kernel(n_mp, n_ev, plan, where_ref, *refs):
    n, groups = sum(len(parts) for _, parts in plan), len(plan)
    vec_in, (gain_ref, meta_ref, patient_ref), refs = refs[:n_mp], refs[n_mp : n_mp + 3], refs[n_mp + 3 :]
    pieces, refs = refs[:n], refs[n:]
    attended_ref, state, refs = refs[0], refs[1], refs[2:]
    scratch, refs = refs[:groups], refs[groups:]
    vec, blocks, sems, kept, out_sems = refs
    copies = fetch_parts(pieces, plan, scratch, sems)
    e, m = where_ref[0], where_ref[1]
    cols = attended_ref.shape[1]
    saves = [
        pltpu.make_async_copy(kept.at[:, lo:hi], state.at[:, lo:hi], out_sems.at[i])
        for i, (lo, hi) in enumerate(state_spans(cols))
    ]
    for k in range(n_mp):
        vec[m ^ k] = vec_in[k][...]
    rows = n_mp * VPAD
    full = vec[...].astype(F32).reshape(rows, DV)
    kept[:, :DV] = full
    saves[0].start()
    normed = (full * rms_factor(full) * gain_ref[...]).astype(BF16)
    width = DV // n_ev
    for j in range(n_ev):
        blocks[j] = normed[:, j * width : (j + 1) * width]
    totals = [jnp.zeros((rows, cols), F32) for _ in range(3)]
    for i, (k, _) in enumerate(plan):
        for copy in copies[i]:
            copy.wait()
        block = blocks[e ^ k]
        for t in range(3):
            totals[t] = totals[t] + dot(block, scratch[i][t])
    parts = [total.astype(BF16) for total in totals]
    for t in range(3):
        kept[:, DV + t * cols : DV + (t + 1) * cols] = parts[t].astype(F32)
    saves[1].start()
    q_at = lax.broadcasted_iota(jnp.int32, (rows, rows), 0)
    k_at = lax.broadcasted_iota(jnp.int32, (rows, rows), 1)
    allowed = (meta_ref[:, 2:3] == patient_ref[0:1, :]) & (k_at <= q_at)
    for h in range(cols // VHDIM):
        span = slice(h * VHDIM, (h + 1) * VHDIM)
        scores = dot(parts[0][:, span], parts[1][:, span], NT) * VHDIM ** (-0.5)
        scores = jnp.where(allowed, scores, -1e30)
        grown = jnp.exp(scores - jnp.max(scores, axis=-1, keepdims=True))
        prob = grown / jnp.sum(grown, axis=-1, keepdims=True)
        kept[:, DV + 3 * cols + h * rows : DV + 3 * cols + (h + 1) * rows] = prob
        attended_ref[:, span] = dot(prob.astype(BF16), parts[2][:, span]).astype(BF16)
    saves[2].start()
    for save in saves:
        save.wait()


def state_spans(cols):
    return ((0, DV), (DV, DV + 3 * cols), (DV + 3 * cols, DV + 3 * cols + LANES))


def pack_scalars(columns, rows):
    lane = lax.broadcasted_iota(jnp.int32, (rows, LANES), 1)
    spread = jnp.zeros((rows, LANES), F32)
    for c, column in enumerate(columns):
        at = (lane == c) | (lane == 8 + c) | (lane == 16 + c)
        spread = jnp.where(at, column, spread)
    one = spread.astype(BF16).astype(F32)
    two = (spread - one).astype(BF16).astype(F32)
    three = spread - one - two
    return jnp.where(lane < 8, one, jnp.where(lane < 16, two, three)).astype(BF16)


def unpack_scalar(packed, c):
    return packed[:, c : c + 1] + packed[:, 8 + c : 9 + c] + packed[:, 16 + c : 17 + c]


def ffn_kernel(
    n_mp, n_ev, plan, where_ref, bias_ref, gain_ref, meta_ref, head_ref, *refs
):
    n, groups = sum(len(parts) for _, parts in plan), len(plan)
    attn_in, state, refs = refs[:n_mp], refs[n_mp], refs[n_mp + 1 :]
    pieces, refs = refs[:n], refs[n:]
    outs, mid_ref, refs = refs[:n_mp], refs[n_mp], refs[n_mp + 1 :]
    scratch, refs = refs[:groups], refs[groups:]
    attn, vec_ref, blocks, grads, sems = refs
    e, m = where_ref[0], where_ref[1]
    cols = DV // n_mp
    small = fetch([state.at[:, :DV]], [vec_ref], sems, n)
    copies = fetch_parts(pieces, plan, scratch, sems)
    for k in range(n_mp):
        attn[m ^ k] = attn_in[k][...]
    for copy in small:
        copy.wait()
    rows = vec_ref.shape[0]
    mid = vec_ref[...] + jnp.concatenate([attn[k] for k in range(n_mp)], axis=1).astype(F32)
    at = pl.ds(pl.multiple_of(m * cols, cols), cols)
    factor = rms_factor(mid)
    mid_ref[:, :cols] = vec_ref[:, at] + attn[m].astype(F32)
    mid_ref[:, cols:] = jnp.broadcast_to(factor, (rows, LANES))
    gain = gain_ref[...]
    normed = (mid * factor * gain).astype(BF16)
    width = DV // n_ev
    for j in range(n_ev):
        blocks[j] = normed[:, j * width : (j + 1) * width]
    hidden = scratch[0].shape[1]
    pre = jnp.zeros((rows, hidden), F32)
    fw = jnp.zeros((2, hidden), F32)
    for i, (k, _) in enumerate(plan):
        for copy in copies[i]:
            copy.wait()
        pre = pre + dot(blocks[e ^ k], scratch[i][:width, :])
        parts = scratch[i][width : width + FW_ROWS, :].astype(F32)
        fw = fw + (parts[0:2] + parts[2:4] + parts[4:6])
    sigma = 1.0 / (1.0 + jnp.exp(-pre))
    act = (pre * sigma).astype(BF16).astype(F32)
    first = (m == 0).astype(F32)
    outcome = []
    for j in range(2):
        base = jnp.sum(mid * head_ref[j : j + 1, :], axis=-1, keepdims=True) + bias_ref[j]
        outcome.append(jnp.sum(act * fw[j : j + 1, :], axis=-1, keepdims=True) + first * base)
    chosen = jnp.where(meta_ref[:, 0:1] > 0.5, fw[1:2, :], fw[0:1, :])
    slope = (chosen * sigma * (1.0 + pre * (1.0 - sigma))).astype(BF16)
    moment = jnp.sum(slope.astype(F32) * pre, axis=-1, keepdims=True) / factor
    for i, (k, _) in enumerate(plan):
        grads[e ^ k] = dot(slope, scratch[i][:width, :], NT)
    scalars = pack_scalars([outcome[0], outcome[1], moment], rows)
    each = n_ev // n_mp
    for k in range(n_mp):
        for j in range(each):
            outs[k][:, j * width : (j + 1) * width] = grads[(m ^ k) * each + j].astype(BF16)
        outs[k][:, cols:] = scalars


def back_kernel(
    n_mp, n_ev, plan, where_ref, mid_ref, meta_ref, gain_ref, vgain_ref, head_ref, *refs
):
    n, groups = sum(len(parts) for _, parts in plan), len(plan)
    pay_in, state, refs = refs[:n_mp], refs[n_mp], refs[n_mp + 1 :]
    pieces, refs = refs[:n], refs[n:]
    outs, outcome_ref, coef_ref, refs = refs[:n_mp], refs[n_mp], refs[n_mp + 1], refs[n_mp + 2 :]
    scratch, refs = refs[:groups], refs[groups:]
    kept, grads, table, sems = refs
    (stored,) = fetch([state], [kept], sems, n)
    copies = fetch_parts(pieces, plan, scratch, sems)
    e, m = where_ref[0], where_ref[1]
    rows = mid_ref.shape[0]
    cols = DV // n_mp
    total = pay_in[0][...].astype(F32)
    for k in range(1, n_mp):
        total = total + pay_in[k][...].astype(F32)
    packed = total[:, cols:]
    outcome = [unpack_scalar(packed, 0), unpack_scalar(packed, 1)]
    moment = unpack_scalar(packed, 2) * (1.0 / DV)
    lane = lax.broadcasted_iota(jnp.int32, (rows, LANES), 1)
    outcome_ref[...] = jnp.where(lane == 0, outcome[0], outcome[1])
    treated = meta_ref[:, 0:1] > 0.5
    delta = 4096.0 * (jnp.where(treated, outcome[1], outcome[0]) - meta_ref[:, 1:2])
    factor = mid_ref[:, cols : cols + 1]
    at = pl.ds(pl.multiple_of(m * cols, cols), cols)
    mid = mid_ref[:, :cols]
    head = jnp.where(treated, head_ref[1:2, at], head_ref[0:1, at])
    scaled = total[:, :cols] * gain_ref[:, at]
    grad_mid = delta * (head + factor * (scaled - mid * (factor * factor * moment)))
    grad_c = grad_mid.astype(BF16)
    stored.wait()
    queries, keys, values = (
        kept[:, DV + t * cols : DV + (t + 1) * cols].astype(BF16) for t in range(3)
    )
    three = [[], [], []]
    for h in range(cols // VHDIM):
        span = slice(h * VHDIM, (h + 1) * VHDIM)
        prob = kept[:, DV + 3 * cols + h * rows : DV + 3 * cols + (h + 1) * rows]
        grad_p = dot(grad_c[:, span], values[:, span], NT)
        grad_s = prob * (grad_p - jnp.sum(grad_p * prob, axis=-1, keepdims=True))
        grad_s = (grad_s * VHDIM ** (-0.5)).astype(BF16)
        three[0].append(dot(grad_s, keys[:, span]).astype(BF16))
        three[1].append(dot(grad_s, queries[:, span], TN).astype(BF16))
        three[2].append(dot(prob.astype(BF16), grad_c[:, span], TN).astype(BF16))
    three = [jnp.concatenate(parts, axis=1) for parts in three]
    for i, (k, _) in enumerate(plan):
        for copy in copies[i]:
            copy.wait()
        part = dot(three[0], scratch[i][0], NT)
        part = part + dot(three[1], scratch[i][1], NT)
        part = part + dot(three[2], scratch[i][2], NT)
        grads[e ^ k] = part
    width = DV // n_ev
    vec = kept[:, :DV]
    spread = rms_factor(vec)
    moment = jnp.zeros((rows, 1), F32)
    for t in range(3):
        forward = kept[:, DV + t * cols : DV + (t + 1) * cols]
        moment = moment + jnp.sum(three[t].astype(F32) * forward, axis=-1, keepdims=True)
    moment = moment / spread
    for j in range(D // width):
        span = slice(j * width, (j + 1) * width)
        scaled = grads[j] * vgain_ref[:, span]
        table[:, :, span] = (scaled * spread).reshape(n_mp, VPAD, width)

    @pl.when(m * cols < D)
    def _():
        here = pl.ds(pl.multiple_of(m * cols, cols), cols)
        table[:, :, here] = table[:, :, here] + grad_mid.reshape(n_mp, VPAD, cols)

    scalars = pack_scalars([moment], rows).astype(F32)
    table[:, :, D:] = scalars.reshape(n_mp, VPAD, LANES)
    for k in range(n_mp):
        outs[k][...] = table[m ^ k].astype(BF16)
    table[:, :, :D] = (vec[:, :D] * (spread * spread * spread * (1.0 / DV))).reshape(n_mp, VPAD, D)
    coef_ref[...] = table[m][:, :D]


def finish_kernel(n_mp, visits_dev, count_ref, coef_ref, *refs):
    pays, out_ref = refs[:n_mp], refs[n_mp]
    total = pays[0][...].astype(F32)
    for k in range(1, n_mp):
        total = total + pays[k][...].astype(F32)
    grad = total[:, :D] - coef_ref[...] * unpack_scalar(total[:, D:], 0)
    row = lax.broadcasted_iota(jnp.int32, (VPAD, 1), 0)
    inverse = jnp.zeros((VPAD, 1), F32)
    for v in range(visits_dev):
        inverse = jnp.where(row == v, 1.0 / count_ref[v].astype(F32), inverse)
    out_ref[...] = (grad * inverse).astype(BF16).astype(F32)


def spread_kernel(n_ev, pick, *refs):
    tables, out, rows_ref, out_sems = refs[:n_ev], *refs[n_ev:]
    table = jnp.concatenate([each[...] for each in tables], axis=0).astype(BF16)
    rows = rows_ref.shape[0]
    step = rows // 3
    saves = []
    for c in range(3):
        span = slice(c * step, (c + 1) * step)
        rows_ref[span, :] = dot(pick[span, :], table).astype(BF16)
        saves.append(pltpu.make_async_copy(rows_ref.at[span, :], out.at[span, :], out_sems.at[c]))
        saves[c].start()
    for save in saves:
        save.wait()


def swap(x, axis, size, k):
    return lax.ppermute(x, axis, [(i, i ^ k) for i in range(size)])


def first_hop(shard, n_ev):
    if n_ev != 8:
        return [shard] + [swap(shard, "events", n_ev, k) for k in range(1, n_ev)]
    return [shard, swap(shard, "events", n_ev, 2), swap(shard, "events", n_ev, 4)]


def halves_kernel(low_ref, high_ref, low_out, high_out):
    half = low_out.shape[0]
    low_out[...] = low_ref[...]
    high_out[...] = high_ref[half:, :]


def halves_of(pieces, half):
    rows, cols = pieces[1].shape
    low = pl.BlockSpec((half, cols), lambda i: (0, 0))
    return pl.pallas_call(
        halves_kernel,
        grid=(1,),
        out_shape=[
            jax.ShapeDtypeStruct((half, cols), BF16),
            jax.ShapeDtypeStruct((rows - half, cols), BF16),
        ],
        in_specs=[low, vmem()],
        out_specs=[low, vmem()],
        compiler_params=params(SNUG),
        cost_estimate=cost(0),
        name="halves",
    )(pieces[1], pieces[2])


def split_kernel(half, low_ref, high_ref, low_out, high_out, low, high, sems):
    rows = high_ref.shape[1]
    sources = [low_ref.at[:, :half, :], high_ref.at[:, half:rows, :]]
    copies = fetch(sources, [low, high], sems)
    saves = []
    for i, (buffer, out) in enumerate(((low, low_out), (high, high_out))):
        copies[i].wait()
        saves += fetch([buffer], [out], sems, 2 + i)
    for save in saves:
        save.wait()


def split_of(pieces, half):
    lead, rows, cols = pieces[1].shape
    return pl.pallas_call(
        functools.partial(split_kernel, half),
        out_shape=[
            jax.ShapeDtypeStruct((lead, half, cols), BF16),
            jax.ShapeDtypeStruct((lead, rows - half, cols), BF16),
        ],
        in_specs=[hbm()] * 2,
        out_specs=[hbm()] * 2,
        scratch_shapes=[
            pltpu.VMEM((lead, half, cols), BF16),
            pltpu.VMEM((lead, rows - half, cols), BF16),
            pltpu.SemaphoreType.DMA((4,)),
        ],
        compiler_params=params(SNUG),
        cost_estimate=cost(0),
        name="split",
    )(pieces[1], pieces[2])


def second_hop(low, high, n_ev):
    return [swap(low, "events", n_ev, 4), swap(high, "events", n_ev, 2)]


def across(pieces, n_ev):
    return [swap(piece, "events", n_ev, 1) for piece in pieces]


def hop_places(n_ev, width):
    if n_ev != 8:
        return [(k, 0) for k in range(n_ev)]
    near = [(0, 0), (2, 0), (4, 0), (6, 0), (6, width // 2)]
    return near + [(k ^ 1, first) for k, first in near]


def grouped(places, pieces, row_axis):
    plan = {}
    for i, (k, first) in enumerate(places):
        plan.setdefault(k, []).append((i, first, pieces[i].shape[row_axis]))
    return list(plan.items())


def room(plan, piece, row_axis):
    shapes = []
    for _, parts in plan:
        shape = list(piece.shape)
        shape[row_axis] = max(first + rows for _, first, rows in parts)
        shapes.append(pltpu.VMEM(tuple(shape), BF16))
    return shapes


def event_order(n_ev):
    return list(range(n_ev)) if n_ev != 8 else [0, 2, 4, 6, 1, 3, 5, 7]


def gather_events(block, n_ev):
    if n_ev != 8:
        return [block] + [swap(block, "events", n_ev, k) for k in range(1, n_ev)]
    near = [block] + [swap(block, "events", n_ev, k) for k in (2, 4, 6)]
    return near + across(near, n_ev)


def local(
    event_x,
    event_visit,
    visit_count,
    visit_patient,
    treatment,
    outcome_target,
    enc_gain,
    enc_qkv,
    enc_out,
    visit_gain,
    visit_qkv,
    ffn_gain,
    ffn_in,
    ffn_out,
    head_weight,
    head_bias,
):
    n_ev = lax.axis_size("events")
    n_mp = lax.axis_size("mp")
    e = lax.axis_index("events")
    m = lax.axis_index("mp")
    rows_dev = event_x.shape[0]
    visits_dev = visit_count.shape[0]
    per_owner = visits_dev * n_mp
    group = n_mp * VPAD
    cols = DV // n_mp
    hidden = ffn_in.shape[1]
    where = jnp.stack([e, m]).astype(jnp.int32)
    ids = event_visit.reshape(rows_dev // LANES, LANES)

    send = pl.pallas_call(
        functools.partial(pack_kernel, n_ev, per_owner, visits_dev),
        out_shape=jax.ShapeDtypeStruct((rows_dev, D + LANES), BF16),
        in_specs=[smem(), vmem(), hbm()],
        out_specs=vmem(),
        scratch_shapes=[pltpu.VMEM((rows_dev, D), BF16), pltpu.SemaphoreType.DMA],
        compiler_params=params(12),
        cost_estimate=cost(0),
        name="pack",
    )(where, ids, event_x)
    got = lax.all_to_all(
        send.reshape(n_ev, rows_dev // n_ev, D + LANES), "events", split_axis=0, concat_axis=0,
        tiled=True,
    ).reshape(rows_dev, D + LANES)

    qkv_first = first_hop(visit_qkv, n_ev)

    head_t = head_weight.T
    width = DV // n_ev
    own_head = lax.dynamic_slice_in_dim(head_t, e * width, width, 1)
    head_hi = own_head.astype(BF16)
    head_mid = (own_head - head_hi.astype(F32)).astype(BF16)
    head_lo = (own_head - head_hi.astype(F32) - head_mid.astype(F32)).astype(BF16)
    heads = jnp.concatenate([head_hi, head_mid, head_lo, jnp.zeros((2, width), BF16)], axis=0)
    meta, patient_row = pl.pallas_call(
        functools.partial(prep_kernel, visits_dev),
        out_shape=[
            jax.ShapeDtypeStruct((group, LANES), F32),
            jax.ShapeDtypeStruct((VPAD, group), F32),
        ],
        in_specs=[smem()] * 3,
        out_specs=[vmem()] * 2,
        compiler_params=params(4),
        cost_estimate=cost(0),
        name="prep",
    )(visit_patient, treatment, outcome_target)
    two_hops = n_ev == 8
    inner = jnp.arange(VPAD, dtype=jnp.int32)
    named = (jnp.array(event_order(n_ev), jnp.int32) ^ e)[:, None] * per_owner
    named = jnp.where(inner < visits_dev, named + m * visits_dev + inner[None, :], -2).reshape(-1)
    chosen = (event_visit[:, None] == named[None, :]).astype(BF16)
    ready = [meta, patient_row, head_t, chosen]
    if two_hops:
        qkv_halves = split_of(qkv_first, width // 2)
        qkv_far = across(qkv_first, n_ev)
        ready += [*qkv_halves, *qkv_far]
    ffn_shard = pl.pallas_call(
        fold_kernel,
        out_shape=jax.ShapeDtypeStruct((width + FW_ROWS, hidden), BF16),
        in_specs=[vmem()] * 3,
        out_specs=vmem(),
        compiler_params=params(SNUG),
        cost_estimate=cost(30),
        name="fold",
    )(ffn_out, heads, after(ffn_in, *ready))
    gate = [got]
    if two_hops:
        qkv_second = second_hop(*qkv_halves, n_ev)
        qkv_far += across(qkv_second, n_ev)
        ffn_far = across([ffn_shard], n_ev)
        gate += qkv_second
    ffn_first = [ffn_shard] + first_hop(after(ffn_shard, *gate), n_ev)[1:]
    if two_hops:
        got = after(got, *ffn_far, *qkv_far)
    vec = pl.pallas_call(
        functools.partial(encode_kernel, visits_dev),
        out_shape=jax.ShapeDtypeStruct((VPAD, DV), BF16),
        in_specs=[smem(), vmem(), hbm(), hbm(), hbm()],
        out_specs=vmem(),
        scratch_shapes=[
            pltpu.VMEM((rows_dev, D + LANES), BF16),
            pltpu.VMEM((D, 2 * D), BF16),
            pltpu.VMEM((D, D), BF16),
            pltpu.VMEM((D, D), BF16),
            pltpu.VMEM((visits_dev * VB, D), BF16),
            pltpu.VMEM((visits_dev * VB, 2 * D), BF16),
            pltpu.VMEM((visits_dev, HEADS, VB), F32),
            pltpu.VMEM((visits_dev, HEADS, D), BF16),
            pltpu.SemaphoreType.DMA((5,)),
        ],
        compiler_params=params(53),
        cost_estimate=cost(0),
        name="encode",
    )(visit_count, enc_gain.reshape(1, D), got, enc_qkv, enc_out)

    vecs = [vec] + [swap(vec, "mp", n_mp, k) for k in range(1, n_mp)]
    if two_hops:
        qkv_pieces = qkv_first + qkv_second + qkv_far
        ffn_next = [ffn_first[0]] + [after(piece, *vecs[1:]) for piece in ffn_first[1:]]
        ffn_second = second_hop(*halves_of(ffn_next, width // 2), n_ev)
        ffn_far += across(ffn_next[1:], n_ev)
        vecs[0] = after(vec, *ffn_far[1:])
    else:
        qkv_pieces = qkv_first
    n_q = len(qkv_pieces)
    qkv_plan = grouped(hop_places(n_ev, width), qkv_pieces, 1)
    vgain = visit_gain.reshape(1, DV)
    state_shape = (group, state_spans(cols)[2][1])
    attended, state = pl.pallas_call(
        functools.partial(project_kernel, n_mp, n_ev, qkv_plan),
        out_shape=[
            jax.ShapeDtypeStruct((group, cols), BF16),
            jax.ShapeDtypeStruct(state_shape, F32),
        ],
        in_specs=[smem()] + [vmem()] * (n_mp + 3) + [hbm()] * n_q,
        out_specs=[vmem(), hbm()],
        scratch_shapes=room(qkv_plan, visit_qkv, 1)
        + [
            pltpu.VMEM((n_mp, VPAD, DV), BF16),
            pltpu.VMEM((n_ev, group, width), BF16),
            pltpu.SemaphoreType.DMA((n_q,)),
            pltpu.VMEM(state_shape, F32),
            pltpu.SemaphoreType.DMA((3,)),
        ],
        compiler_params=params(SNUG),
        cost_estimate=cost(0),
        name="project",
    )(where, *vecs, vgain, meta, patient_row, *qkv_pieces)

    attns = [attended] + [swap(attended, "mp", n_mp, k) for k in range(1, n_mp)]
    if two_hops:
        ffn_second = [after(piece, *attns[1:]) for piece in ffn_second]
        ffn_pieces = ffn_first + ffn_second + ffn_far + across(ffn_second, n_ev)
    else:
        ffn_pieces = ffn_first
    n_f = len(ffn_pieces)
    ffn_plan = grouped(hop_places(n_ev, width), ffn_pieces, 0)
    fgain = ffn_gain.reshape(1, DV)
    ffn_outs = pl.pallas_call(
        functools.partial(ffn_kernel, n_mp, n_ev, ffn_plan),
        out_shape=[jax.ShapeDtypeStruct((group, cols + LANES), BF16)] * n_mp
        + [jax.ShapeDtypeStruct((group, cols + LANES), F32)],
        in_specs=[smem()] * 2 + [vmem()] * (3 + n_mp) + [hbm()] * (1 + n_f),
        out_specs=[vmem()] * (n_mp + 1),
        scratch_shapes=room(ffn_plan, ffn_shard, 0)
        + [
            pltpu.VMEM((n_mp, group, cols), BF16),
            pltpu.VMEM((group, DV), F32),
            pltpu.VMEM((n_ev, group, width), BF16),
            pltpu.VMEM((n_ev, group, width), F32),
            pltpu.SemaphoreType.DMA((n_f + 1,)),
        ],
        compiler_params=params(SNUG),
        cost_estimate=cost(0),
        name="ffn",
    )(where, head_bias, fgain, meta, head_t, *attns, state, *ffn_pieces)
    mid = ffn_outs[n_mp]
    pays = [ffn_outs[0]] + [swap(ffn_outs[k], "mp", n_mp, k) for k in range(1, n_mp)]

    back_outs = pl.pallas_call(
        functools.partial(back_kernel, n_mp, n_ev, qkv_plan),
        out_shape=[jax.ShapeDtypeStruct((VPAD, D + LANES), BF16)] * n_mp
        + [jax.ShapeDtypeStruct((group, LANES), F32), jax.ShapeDtypeStruct((VPAD, D), F32)],
        in_specs=[smem()] + [vmem()] * (5 + n_mp) + [hbm()] * (1 + n_q),
        out_specs=[vmem()] * (n_mp + 2),
        scratch_shapes=room(qkv_plan, visit_qkv, 1)
        + [
            pltpu.VMEM(state_shape, F32),
            pltpu.VMEM((n_ev, group, width), F32),
            pltpu.VMEM((n_mp, VPAD, D + LANES), F32),
            pltpu.SemaphoreType.DMA((n_q + 1,)),
        ],
        compiler_params=params(SNUG),
        cost_estimate=cost(0),
        name="back",
    )(where, mid, meta, fgain, vgain, head_t, *pays, state, *qkv_pieces)
    outcomes = back_outs[n_mp][:, :2].reshape(n_mp, VPAD, 2)[:, :visits_dev].reshape(per_owner, 2)
    shares = [back_outs[0]] + [swap(back_outs[k], "mp", n_mp, k) for k in range(1, n_mp)]
    visit_grad = pl.pallas_call(
        functools.partial(finish_kernel, n_mp, visits_dev),
        out_shape=jax.ShapeDtypeStruct((VPAD, D), F32),
        in_specs=[smem()] + [vmem()] * (1 + n_mp),
        out_specs=vmem(),
        compiler_params=params(4),
        cost_estimate=cost(0),
        name="finish",
    )(visit_count, after(back_outs[n_mp + 1], outcomes), *shares)

    tables = gather_events(visit_grad, n_ev)
    event_grads = pl.pallas_call(
        functools.partial(spread_kernel, n_ev),
        out_shape=jax.ShapeDtypeStruct((rows_dev, D), BF16),
        in_specs=[vmem()] * (n_ev + 1),
        out_specs=hbm(),
        scratch_shapes=[
            pltpu.VMEM((rows_dev, D), BF16),
            pltpu.SemaphoreType.DMA((3,)),
        ],
        compiler_params=params(8),
        cost_estimate=cost(0),
        name="spread",
    )(chosen, *tables)
    return (outcomes, event_grads)


def solution(mesh):
    in_specs = (
        P(("events", "mp"), None),
        P(("events", "mp")),
        P(("events", "mp")),
        P("events"),
        P("events"),
        P("events"),
        P(),
        P(),
        P(),
        P(),
        P(None, "events", "mp"),
        P(),
        P("events", "mp"),
        P("mp", "events"),
        P(),
        P(),
    )
    out_specs = (P("events", None), P(("events", "mp"), None))
    return jax.shard_map(local, mesh=mesh, in_specs=in_specs, out_specs=out_specs, check_vma=False)
```

```python
import functools

import jax
import jax.numpy as jnp
from jax import lax
from jax.experimental import pallas as pl
from jax.experimental.pallas import tpu as pltpu
from jax.sharding import PartitionSpec as P

D = 1024
HEADS = 16
HDIM = 64
VB = 128
DV = 2048
VHDIM = 128
VPAD = 8
FW_ROWS = 16
SNUG = 48
LANES = 128
EPS = 1e-5
F32 = jnp.float32
BF16 = jnp.bfloat16

NT = (((1,), (1,)), ((), ()))
TN = (((0,), (0,)), ((), ()))
NN = (((1,), (0,)), ((), ()))


def dot(a, b, dims=NN):
    return lax.dot_general(a, b, dims, preferred_element_type=F32)


def vmem():
    return pl.BlockSpec(memory_space=pltpu.VMEM)


def smem():
    return pl.BlockSpec(memory_space=pltpu.SMEM)


def hbm():
    return pl.BlockSpec(memory_space=pltpu.HBM)


def params(mib):
    return pltpu.CompilerParams(vmem_limit_bytes=int(mib * 1024) * 1024)


def cost(micros):
    return pl.CostEstimate(
        flops=int(micros * 1e9) + 1, bytes_accessed=int(micros * 1e6) + 1, transcendentals=0
    )


def after(value, *others):
    return lax.optimization_barrier((value, *others))[0]


def rank_before(hot):
    classes, rows = hot.shape
    tiles = [hot[:, c : c + LANES] for c in range(0, rows, LANES)]
    a = lax.broadcasted_iota(jnp.int32, (LANES, LANES), 0)
    b = lax.broadcasted_iota(jnp.int32, (LANES, LANES), 1)
    stacked = jnp.concatenate(tiles, axis=0)
    inside = dot(stacked.astype(BF16), (a < b).astype(BF16))
    sizes = jnp.sum(stacked, axis=1, keepdims=True)
    offset, ranks = jnp.zeros((classes, 1), F32), []
    for t in range(len(tiles)):
        span = slice(t * classes, (t + 1) * classes)
        ranks.append(inside[span] + offset)
        offset = offset + sizes[span]
    return jnp.concatenate(ranks, axis=1)


def pick_rows(position, first, count, rows):
    slots = lax.broadcasted_iota(jnp.int32, (count, rows), 0) + first
    return (slots == position).astype(BF16)


def pack_kernel(senders, per_owner, visits_dev, where_ref, ids_ref, x_hbm, out_ref, x_ref, sem):
    copy = pltpu.make_async_copy(x_hbm, x_ref, sem)
    copy.start()
    rows = x_ref.shape[0]
    cap_rows = rows // senders
    ids = jnp.concatenate([ids_ref[i : i + 1, :] for i in range(ids_ref.shape[0])], axis=1)
    owners = lax.broadcasted_iota(jnp.int32, (senders, rows), 0)
    hot = (ids >= owners * per_owner) & (ids < (owners + 1) * per_owner)
    hot_f = hot.astype(F32)
    before = rank_before(hot_f)
    base = (owners * cap_rows + 1).astype(F32)
    position = (jnp.sum(hot_f * (base + before), axis=0, keepdims=True)).astype(jnp.int32) - 1
    first = (owners * per_owner + where_ref[1] * visits_dev).astype(F32)
    label = jnp.sum(hot_f * (ids.astype(F32) - first + 1.0), axis=0, keepdims=True)
    label = jnp.broadcast_to(label, (LANES, rows)).astype(BF16)
    copy.wait()
    step = rows // 3
    for c in range(3):
        chosen = pick_rows(position, c * step, step, rows)
        out_ref[c * step : (c + 1) * step, :D] = dot(chosen, x_ref[...]).astype(BF16)
        out_ref[c * step : (c + 1) * step, D:] = dot(chosen, label, NT).astype(BF16)


def prep_kernel(visits_dev, patient_ref, treat_ref, target_ref, meta_ref, row_ref):
    rows, lanes = meta_ref.shape
    slot = lax.broadcasted_iota(jnp.int32, (rows, lanes), 0)
    lane = lax.broadcasted_iota(jnp.int32, (rows, lanes), 1)
    place = lax.broadcasted_iota(jnp.int32, (VPAD, rows), 1)
    meta = jnp.where(lane == 2, -1.0, jnp.zeros((rows, lanes), F32))
    line = jnp.full((VPAD, rows), -1.0, F32)
    for g in range(patient_ref.shape[0]):
        at = (g // visits_dev) * VPAD + g % visits_dev
        patient = patient_ref[g].astype(F32)
        here = jnp.where(
            lane == 0, treat_ref[g].astype(F32), jnp.where(lane == 1, target_ref[g], patient)
        )
        meta = jnp.where((slot == at) & (lane < 3), here, meta)
        line = jnp.where(place == at, patient, line)
    meta_ref[...] = meta
    row_ref[...] = line


def fold_kernel(weight_ref, head_ref, ffn_ref, out_ref):
    rows = ffn_ref.shape[0]
    out_ref[:rows, :] = ffn_ref[...]
    folded = dot(head_ref[...], weight_ref[...], NT)
    folded = folded[0:2] + folded[2:4] + folded[4:6]
    one = folded.astype(BF16).astype(F32)
    two = (folded - one).astype(BF16).astype(F32)
    three = folded - one - two
    blank = jnp.zeros((FW_ROWS - 6, folded.shape[1]), F32)
    out_ref[rows:, :] = jnp.concatenate([one, two, three, blank], axis=0).astype(BF16)


def encode_kernel(
    visits_dev,
    gain_ref,
    got_hbm,
    qkv_ref,
    proj_ref,
    vec_ref,
    got_ref,
    wqk,
    wv,
    wo,
    normed,
    qk,
    pbar,
    ctx,
    sems,
):
    rows = got_ref.shape[0]
    slots = visits_dev * VB
    inputs = [
        pltpu.make_async_copy(got_hbm.at[:, D:], got_ref.at[:, D:], sems.at[3]),
        pltpu.make_async_copy(got_hbm.at[:, :D], got_ref.at[:, :D], sems.at[4]),
    ]
    copies = [
        pltpu.make_async_copy(qkv_ref.at[:, : 2 * D], wqk, sems.at[0]),
        pltpu.make_async_copy(qkv_ref.at[:, 2 * D :], wv, sems.at[1]),
        pltpu.make_async_copy(proj_ref, wo, sems.at[2]),
    ]
    for copy in inputs + copies:
        copy.start()
    inputs[0].wait()
    lane0 = (lax.broadcasted_iota(jnp.int32, (VPAD, LANES), 1) == 0).astype(BF16)
    label = dot(lane0, got_ref[:, D:], NT)[:1]
    visits = lax.broadcasted_iota(jnp.int32, (VPAD, rows), 0)
    hot = label == (visits + 1).astype(F32)
    hot_b = hot.astype(BF16)
    hot_f = hot.astype(F32)
    before = rank_before(hot_f)
    counts = jnp.maximum(jnp.sum(hot_f, axis=1, keepdims=True), 1.0)
    base = (visits * VB + 1).astype(F32)
    position = (jnp.sum(hot_f * (base + before), axis=0, keepdims=True)).astype(jnp.int32) - 1
    inputs[1].wait()
    sums = dot(hot_b, got_ref[:, :D])
    gain = gain_ref[...]
    step = 2 * VB
    for c in range(slots // step):
        part = dot(pick_rows(position, c * step, step, rows), got_ref[:, :D])
        scale = lax.rsqrt(jnp.mean(part * part, axis=-1, keepdims=True) + EPS)
        normed[c * step : (c + 1) * step, :] = (part * scale * gain).astype(BF16)
    copies[0].wait()
    wide = 512
    for c in range(2 * D // wide):
        cols = slice(c * wide, (c + 1) * wide)
        qk[:, cols] = dot(normed[...], wqk[:, cols]).astype(BF16)

    lanes = lax.broadcasted_iota(jnp.int32, (VB, LANES), 1)
    low = (lanes < HDIM).astype(F32) * HDIM ** (-0.5)
    high = (lanes >= HDIM).astype(F32) * HDIM ** (-0.5)
    key_slot = lax.broadcasted_iota(jnp.int32, (VB, 2 * VB), 0)
    query_lane = lax.broadcasted_iota(jnp.int32, (1, 2 * VB), 1)
    query_slot = jnp.where(query_lane >= VB, query_lane - VB, query_lane)
    rows8 = lax.broadcasted_iota(jnp.int32, (VPAD, 2 * VB), 0)
    lanes8 = lax.broadcasted_iota(jnp.int32, (VPAD, 2 * VB), 1)
    halves = ((lanes8 >= rows8 * VB) & (lanes8 < (rows8 + 1) * VB)).astype(BF16)

    def one_visit(v, carry):
        count = counts[v : v + 1, :]
        at = slice(v * VB, (v + 1) * VB)
        live_key = key_slot.astype(F32) < count
        weight = (query_slot.astype(F32) < count).astype(F32) / count
        for p in range(HEADS // 2):
            q = qk[at, p * LANES : (p + 1) * LANES].astype(F32)
            k = qk[at, D + p * LANES : D + (p + 1) * LANES]
            both = jnp.concatenate([(q * low).astype(BF16), (q * high).astype(BF16)], axis=0)
            scores = jnp.where(live_key, dot(k, both, NT), -1e30)
            top = jnp.max(scores, axis=0, keepdims=True)
            grown = jnp.exp(scores - top)
            total = jnp.sum(grown, axis=0, keepdims=True)
            shares = (grown * (weight / total)).astype(BF16)
            pbar[v, 2 * p : 2 * p + 2, :] = dot(halves, shares, NT)[:2]
        ctx[v] = dot(pbar[v].astype(BF16), normed[at, :]).astype(BF16)
        return carry

    for v in range(visits_dev):
        one_visit(v, 0)
    copies[1].wait()
    copies[2].wait()
    vals = dot(ctx[...].reshape(visits_dev * HEADS, D), wv[...]).reshape(visits_dev, HEADS, D)
    head_row = lax.broadcasted_iota(jnp.int32, (1, HEADS, D), 1) * HDIM
    col = lax.broadcasted_iota(jnp.int32, (1, HEADS, D), 2)
    own = (col >= head_row) & (col < head_row + HDIM)
    attended = jnp.sum(jnp.where(own, vals, 0.0), axis=1)
    attended = jnp.concatenate([attended, jnp.zeros((VPAD - visits_dev, D), F32)], axis=0)
    head_part = attended.astype(BF16)
    rest = (attended - head_part.astype(F32)).astype(BF16)
    mixed = dot(head_part, wo[...]) + dot(rest, wo[...])
    inverse = 1.0 / counts
    mean_input = sums * inverse
    vec_ref[:, :D] = (mean_input + mixed).astype(BF16)
    vec_ref[:, D:] = mean_input.astype(BF16)


def rms_factor(values):
    return lax.rsqrt(jnp.mean(values * values, axis=-1, keepdims=True) + EPS)


def fetch(pieces, scratch, sems, first=0):
    copies = [
        pltpu.make_async_copy(piece, buffer, sems.at[first + i])
        for i, (piece, buffer) in enumerate(zip(pieces, scratch, strict=True))
    ]
    for copy in copies:
        copy.start()
    return copies


def fetch_parts(pieces, plan, scratch, sems):
    copies = []
    for (_, parts), buffer in zip(plan, scratch, strict=True):
        group = []
        for i, first, rows in parts:
            span = slice(first, first + rows)
            place = buffer.at[:, span, :] if len(buffer.shape) == 3 else buffer.at[span, :]
            group.append(pltpu.make_async_copy(pieces[i], place, sems.at[i]))
            group[-1].start()
        copies.append(group)
    return copies


def project_kernel(n_mp, n_ev, plan, where_ref, *refs):
    n, groups = sum(len(parts) for _, parts in plan), len(plan)
    vec_in, (gain_ref, meta_ref, patient_ref), refs = refs[:n_mp], refs[n_mp : n_mp + 3], refs[n_mp + 3 :]
    pieces, refs = refs[:n], refs[n:]
    attended_ref, state, refs = refs[0], refs[1], refs[2:]
    scratch, refs = refs[:groups], refs[groups:]
    vec, blocks, sems, kept, out_sems = refs
    copies = fetch_parts(pieces, plan, scratch, sems)
    e, m = where_ref[0], where_ref[1]
    cols = attended_ref.shape[1]
    saves = [
        pltpu.make_async_copy(kept.at[:, lo:hi], state.at[:, lo:hi], out_sems.at[i])
        for i, (lo, hi) in enumerate(state_spans(cols))
    ]
    for k in range(n_mp):
        vec[m ^ k] = vec_in[k][...]
    rows = n_mp * VPAD
    full = vec[...].astype(F32).reshape(rows, DV)
    kept[:, :DV] = full
    saves[0].start()
    normed = (full * rms_factor(full) * gain_ref[...]).astype(BF16)
    width = DV // n_ev
    for j in range(n_ev):
        blocks[j] = normed[:, j * width : (j + 1) * width]
    totals = [jnp.zeros((rows, cols), F32) for _ in range(3)]
    for i, (k, _) in enumerate(plan):
        for copy in copies[i]:
            copy.wait()
        block = blocks[e ^ k]
        for t in range(3):
            totals[t] = totals[t] + dot(block, scratch[i][t])
    parts = [total.astype(BF16) for total in totals]
    for t in range(3):
        kept[:, DV + t * cols : DV + (t + 1) * cols] = parts[t].astype(F32)
    saves[1].start()
    q_at = lax.broadcasted_iota(jnp.int32, (rows, rows), 0)
    k_at = lax.broadcasted_iota(jnp.int32, (rows, rows), 1)
    allowed = (meta_ref[:, 2:3] == patient_ref[0:1, :]) & (k_at <= q_at)
    for h in range(cols // VHDIM):
        span = slice(h * VHDIM, (h + 1) * VHDIM)
        scores = dot(parts[0][:, span], parts[1][:, span], NT) * VHDIM ** (-0.5)
        scores = jnp.where(allowed, scores, -1e30)
        grown = jnp.exp(scores - jnp.max(scores, axis=-1, keepdims=True))
        prob = grown / jnp.sum(grown, axis=-1, keepdims=True)
        kept[:, DV + 3 * cols + h * rows : DV + 3 * cols + (h + 1) * rows] = prob
        attended_ref[:, span] = dot(prob.astype(BF16), parts[2][:, span]).astype(BF16)
    saves[2].start()
    for save in saves:
        save.wait()


def state_spans(cols):
    return ((0, DV), (DV, DV + 3 * cols), (DV + 3 * cols, DV + 3 * cols + LANES))


def pack_scalars(columns, rows):
    lane = lax.broadcasted_iota(jnp.int32, (rows, LANES), 1)
    spread = jnp.zeros((rows, LANES), F32)
    for c, column in enumerate(columns):
        at = (lane == c) | (lane == 8 + c) | (lane == 16 + c)
        spread = jnp.where(at, column, spread)
    one = spread.astype(BF16).astype(F32)
    two = (spread - one).astype(BF16).astype(F32)
    three = spread - one - two
    return jnp.where(lane < 8, one, jnp.where(lane < 16, two, three)).astype(BF16)


def unpack_scalar(packed, c):
    return packed[:, c : c + 1] + packed[:, 8 + c : 9 + c] + packed[:, 16 + c : 17 + c]


def ffn_kernel(
    n_mp, n_ev, plan, where_ref, bias_ref, gain_ref, meta_ref, head_ref, *refs
):
    n, groups = sum(len(parts) for _, parts in plan), len(plan)
    attn_in, state, refs = refs[:n_mp], refs[n_mp], refs[n_mp + 1 :]
    pieces, refs = refs[:n], refs[n:]
    outs, mid_ref, refs = refs[:n_mp], refs[n_mp], refs[n_mp + 1 :]
    scratch, refs = refs[:groups], refs[groups:]
    attn, vec_ref, blocks, grads, sems = refs
    e, m = where_ref[0], where_ref[1]
    cols = DV // n_mp
    small = fetch([state.at[:, :DV]], [vec_ref], sems, n)
    copies = fetch_parts(pieces, plan, scratch, sems)
    for k in range(n_mp):
        attn[m ^ k] = attn_in[k][...]
    for copy in small:
        copy.wait()
    rows = vec_ref.shape[0]
    mid = vec_ref[...] + jnp.concatenate([attn[k] for k in range(n_mp)], axis=1).astype(F32)
    at = pl.ds(pl.multiple_of(m * cols, cols), cols)
    factor = rms_factor(mid)
    mid_ref[:, :cols] = vec_ref[:, at] + attn[m].astype(F32)
    mid_ref[:, cols:] = jnp.broadcast_to(factor, (rows, LANES))
    gain = gain_ref[...]
    normed = (mid * factor * gain).astype(BF16)
    width = DV // n_ev
    for j in range(n_ev):
        blocks[j] = normed[:, j * width : (j + 1) * width]
    hidden = scratch[0].shape[1]
    pre = jnp.zeros((rows, hidden), F32)
    fw = jnp.zeros((2, hidden), F32)
    for i, (k, _) in enumerate(plan):
        for copy in copies[i]:
            copy.wait()
        pre = pre + dot(blocks[e ^ k], scratch[i][:width, :])
        parts = scratch[i][width : width + FW_ROWS, :].astype(F32)
        fw = fw + (parts[0:2] + parts[2:4] + parts[4:6])
    sigma = 1.0 / (1.0 + jnp.exp(-pre))
    act = (pre * sigma).astype(BF16).astype(F32)
    first = (m == 0).astype(F32)
    outcome = []
    for j in range(2):
        base = jnp.sum(mid * head_ref[j : j + 1, :], axis=-1, keepdims=True) + bias_ref[j]
        outcome.append(jnp.sum(act * fw[j : j + 1, :], axis=-1, keepdims=True) + first * base)
    chosen = jnp.where(meta_ref[:, 0:1] > 0.5, fw[1:2, :], fw[0:1, :])
    slope = (chosen * sigma * (1.0 + pre * (1.0 - sigma))).astype(BF16)
    moment = jnp.sum(slope.astype(F32) * pre, axis=-1, keepdims=True) / factor
    for i, (k, _) in enumerate(plan):
        grads[e ^ k] = dot(slope, scratch[i][:width, :], NT)
    scalars = pack_scalars([outcome[0], outcome[1], moment], rows)
    each = n_ev // n_mp
    for k in range(n_mp):
        for j in range(each):
            outs[k][:, j * width : (j + 1) * width] = grads[(m ^ k) * each + j].astype(BF16)
        outs[k][:, cols:] = scalars


def back_kernel(
    n_mp, n_ev, plan, where_ref, mid_ref, meta_ref, gain_ref, vgain_ref, head_ref, *refs
):
    n, groups = sum(len(parts) for _, parts in plan), len(plan)
    pay_in, state, refs = refs[:n_mp], refs[n_mp], refs[n_mp + 1 :]
    pieces, refs = refs[:n], refs[n:]
    outs, outcome_ref, coef_ref, refs = refs[:n_mp], refs[n_mp], refs[n_mp + 1], refs[n_mp + 2 :]
    scratch, refs = refs[:groups], refs[groups:]
    kept, grads, table, sems = refs
    (stored,) = fetch([state], [kept], sems, n)
    copies = fetch_parts(pieces, plan, scratch, sems)
    e, m = where_ref[0], where_ref[1]
    rows = mid_ref.shape[0]
    cols = DV // n_mp
    total = pay_in[0][...].astype(F32)
    for k in range(1, n_mp):
        total = total + pay_in[k][...].astype(F32)
    packed = total[:, cols:]
    outcome = [unpack_scalar(packed, 0), unpack_scalar(packed, 1)]
    moment = unpack_scalar(packed, 2) * (1.0 / DV)
    lane = lax.broadcasted_iota(jnp.int32, (rows, LANES), 1)
    outcome_ref[...] = jnp.where(lane == 0, outcome[0], outcome[1])
    treated = meta_ref[:, 0:1] > 0.5
    delta = 4096.0 * (jnp.where(treated, outcome[1], outcome[0]) - meta_ref[:, 1:2])
    factor = mid_ref[:, cols : cols + 1]
    at = pl.ds(pl.multiple_of(m * cols, cols), cols)
    mid = mid_ref[:, :cols]
    head = jnp.where(treated, head_ref[1:2, at], head_ref[0:1, at])
    scaled = total[:, :cols] * gain_ref[:, at]
    grad_mid = delta * (head + factor * (scaled - mid * (factor * factor * moment)))
    grad_c = grad_mid.astype(BF16)
    stored.wait()
    queries, keys, values = (
        kept[:, DV + t * cols : DV + (t + 1) * cols].astype(BF16) for t in range(3)
    )
    three = [[], [], []]
    for h in range(cols // VHDIM):
        span = slice(h * VHDIM, (h + 1) * VHDIM)
        prob = kept[:, DV + 3 * cols + h * rows : DV + 3 * cols + (h + 1) * rows]
        grad_p = dot(grad_c[:, span], values[:, span], NT)
        grad_s = prob * (grad_p - jnp.sum(grad_p * prob, axis=-1, keepdims=True))
        grad_s = (grad_s * VHDIM ** (-0.5)).astype(BF16)
        three[0].append(dot(grad_s, keys[:, span]).astype(BF16))
        three[1].append(dot(grad_s, queries[:, span], TN).astype(BF16))
        three[2].append(dot(prob.astype(BF16), grad_c[:, span], TN).astype(BF16))
    three = [jnp.concatenate(parts, axis=1) for parts in three]
    for i, (k, _) in enumerate(plan):
        for copy in copies[i]:
            copy.wait()
        part = dot(three[0], scratch[i][0], NT)
        part = part + dot(three[1], scratch[i][1], NT)
        part = part + dot(three[2], scratch[i][2], NT)
        grads[e ^ k] = part
    width = DV // n_ev
    vec = kept[:, :DV]
    spread = rms_factor(vec)
    moment = jnp.zeros((rows, 1), F32)
    for t in range(3):
        forward = kept[:, DV + t * cols : DV + (t + 1) * cols]
        moment = moment + jnp.sum(three[t].astype(F32) * forward, axis=-1, keepdims=True)
    moment = moment / spread
    for j in range(D // width):
        span = slice(j * width, (j + 1) * width)
        scaled = grads[j] * vgain_ref[:, span]
        table[:, :, span] = (scaled * spread).reshape(n_mp, VPAD, width)

    @pl.when(m * cols < D)
    def _():
        here = pl.ds(pl.multiple_of(m * cols, cols), cols)
        table[:, :, here] = table[:, :, here] + grad_mid.reshape(n_mp, VPAD, cols)

    scalars = pack_scalars([moment], rows).astype(F32)
    table[:, :, D:] = scalars.reshape(n_mp, VPAD, LANES)
    for k in range(n_mp):
        outs[k][...] = table[m ^ k].astype(BF16)
    table[:, :, :D] = (vec[:, :D] * (spread * spread * spread * (1.0 / DV))).reshape(n_mp, VPAD, D)
    coef_ref[...] = table[m][:, :D]


def finish_kernel(n_mp, visits_dev, count_ref, coef_ref, *refs):
    pays, out_ref = refs[:n_mp], refs[n_mp]
    total = pays[0][...].astype(F32)
    for k in range(1, n_mp):
        total = total + pays[k][...].astype(F32)
    grad = total[:, :D] - coef_ref[...] * unpack_scalar(total[:, D:], 0)
    row = lax.broadcasted_iota(jnp.int32, (VPAD, 1), 0)
    inverse = jnp.zeros((VPAD, 1), F32)
    for v in range(visits_dev):
        inverse = jnp.where(row == v, 1.0 / count_ref[v].astype(F32), inverse)
    out_ref[...] = (grad * inverse).astype(BF16).astype(F32)


def spread_kernel(n_ev, pick, *refs):
    tables, out, rows_ref, out_sems = refs[:n_ev], *refs[n_ev:]
    table = jnp.concatenate([each[...] for each in tables], axis=0).astype(BF16)
    rows = rows_ref.shape[0]
    step = rows // 3
    saves = []
    for c in range(3):
        span = slice(c * step, (c + 1) * step)
        rows_ref[span, :] = dot(pick[span, :], table).astype(BF16)
        saves.append(pltpu.make_async_copy(rows_ref.at[span, :], out.at[span, :], out_sems.at[c]))
        saves[c].start()
    for save in saves:
        save.wait()


def swap(x, axis, size, k):
    return lax.ppermute(x, axis, [(i, i ^ k) for i in range(size)])


def first_hop(shard, n_ev):
    if n_ev != 8:
        return [shard] + [swap(shard, "events", n_ev, k) for k in range(1, n_ev)]
    return [shard, swap(shard, "events", n_ev, 2), swap(shard, "events", n_ev, 4)]


def halves_kernel(low_ref, high_ref, low_out, high_out):
    half = low_out.shape[0]
    low_out[...] = low_ref[...]
    high_out[...] = high_ref[half:, :]


def halves_of(pieces, half):
    rows, cols = pieces[1].shape
    low = pl.BlockSpec((half, cols), lambda i: (0, 0))
    return pl.pallas_call(
        halves_kernel,
        grid=(1,),
        out_shape=[
            jax.ShapeDtypeStruct((half, cols), BF16),
            jax.ShapeDtypeStruct((rows - half, cols), BF16),
        ],
        in_specs=[low, vmem()],
        out_specs=[low, vmem()],
        compiler_params=params(SNUG),
        cost_estimate=cost(0),
        name="halves",
    )(pieces[1], pieces[2])


def split_kernel(half, low_ref, high_ref, low_out, high_out, low, high, sems):
    rows = high_ref.shape[1]
    sources = [low_ref.at[:, :half, :], high_ref.at[:, half:rows, :]]
    copies = fetch(sources, [low, high], sems)
    saves = []
    for i, (buffer, out) in enumerate(((low, low_out), (high, high_out))):
        copies[i].wait()
        saves += fetch([buffer], [out], sems, 2 + i)
    for save in saves:
        save.wait()


def split_of(pieces, half):
    lead, rows, cols = pieces[1].shape
    return pl.pallas_call(
        functools.partial(split_kernel, half),
        out_shape=[
            jax.ShapeDtypeStruct((lead, half, cols), BF16),
            jax.ShapeDtypeStruct((lead, rows - half, cols), BF16),
        ],
        in_specs=[hbm()] * 2,
        out_specs=[hbm()] * 2,
        scratch_shapes=[
            pltpu.VMEM((lead, half, cols), BF16),
            pltpu.VMEM((lead, rows - half, cols), BF16),
            pltpu.SemaphoreType.DMA((4,)),
        ],
        compiler_params=params(SNUG),
        cost_estimate=cost(0),
        name="split",
    )(pieces[1], pieces[2])


def second_hop(low, high, n_ev):
    return [swap(low, "events", n_ev, 4), swap(high, "events", n_ev, 2)]


def across(pieces, n_ev):
    return [swap(piece, "events", n_ev, 1) for piece in pieces]


def hop_places(n_ev, width):
    if n_ev != 8:
        return [(k, 0) for k in range(n_ev)]
    near = [(0, 0), (2, 0), (4, 0), (6, 0), (6, width // 2)]
    return near + [(k ^ 1, first) for k, first in near]


def grouped(places, pieces, row_axis):
    plan = {}
    for i, (k, first) in enumerate(places):
        plan.setdefault(k, []).append((i, first, pieces[i].shape[row_axis]))
    return list(plan.items())


def room(plan, piece, row_axis):
    shapes = []
    for _, parts in plan:
        shape = list(piece.shape)
        shape[row_axis] = max(first + rows for _, first, rows in parts)
        shapes.append(pltpu.VMEM(tuple(shape), BF16))
    return shapes


def event_order(n_ev):
    return list(range(n_ev)) if n_ev != 8 else [0, 2, 4, 6, 1, 3, 5, 7]


def gather_events(block, n_ev):
    if n_ev != 8:
        return [block] + [swap(block, "events", n_ev, k) for k in range(1, n_ev)]
    near = [block] + [swap(block, "events", n_ev, k) for k in (2, 4, 6)]
    return near + across(near, n_ev)


def local(
    event_x,
    event_visit,
    visit_count,
    visit_patient,
    treatment,
    outcome_target,
    enc_gain,
    enc_qkv,
    enc_out,
    visit_gain,
    visit_qkv,
    ffn_gain,
    ffn_in,
    ffn_out,
    head_weight,
    head_bias,
):
    n_ev = lax.axis_size("events")
    n_mp = lax.axis_size("mp")
    e = lax.axis_index("events")
    m = lax.axis_index("mp")
    rows_dev = event_x.shape[0]
    visits_dev = visit_count.shape[0]
    per_owner = visits_dev * n_mp
    group = n_mp * VPAD
    cols = DV // n_mp
    hidden = ffn_in.shape[1]
    where = jnp.stack([e, m]).astype(jnp.int32)
    ids = event_visit.reshape(rows_dev // LANES, LANES)

    send = pl.pallas_call(
        functools.partial(pack_kernel, n_ev, per_owner, visits_dev),
        out_shape=jax.ShapeDtypeStruct((rows_dev, D + LANES), BF16),
        in_specs=[smem(), vmem(), hbm()],
        out_specs=vmem(),
        scratch_shapes=[pltpu.VMEM((rows_dev, D), BF16), pltpu.SemaphoreType.DMA],
        compiler_params=params(12),
        cost_estimate=cost(0),
        name="pack",
    )(where, ids, event_x)
    got = lax.all_to_all(
        send.reshape(n_ev, rows_dev // n_ev, D + LANES), "events", split_axis=0, concat_axis=0,
        tiled=True,
    ).reshape(rows_dev, D + LANES)

    qkv_first = first_hop(visit_qkv, n_ev)

    head_t = head_weight.T
    width = DV // n_ev
    own_head = lax.dynamic_slice_in_dim(head_t, e * width, width, 1)
    head_hi = own_head.astype(BF16)
    head_mid = (own_head - head_hi.astype(F32)).astype(BF16)
    head_lo = (own_head - head_hi.astype(F32) - head_mid.astype(F32)).astype(BF16)
    heads = jnp.concatenate([head_hi, head_mid, head_lo, jnp.zeros((2, width), BF16)], axis=0)
    meta, patient_row = pl.pallas_call(
        functools.partial(prep_kernel, visits_dev),
        out_shape=[
            jax.ShapeDtypeStruct((group, LANES), F32),
            jax.ShapeDtypeStruct((VPAD, group), F32),
        ],
        in_specs=[smem()] * 3,
        out_specs=[vmem()] * 2,
        compiler_params=params(4),
        cost_estimate=cost(0),
        name="prep",
    )(visit_patient, treatment, outcome_target)
    two_hops = n_ev == 8
    inner = jnp.arange(VPAD, dtype=jnp.int32)
    named = (jnp.array(event_order(n_ev), jnp.int32) ^ e)[:, None] * per_owner
    named = jnp.where(inner < visits_dev, named + m * visits_dev + inner[None, :], -2).reshape(-1)
    chosen = (event_visit[:, None] == named[None, :]).astype(BF16)
    ready = [meta, patient_row, head_t, chosen]
    if two_hops:
        qkv_halves = split_of(qkv_first, width // 2)
        qkv_far = across(qkv_first, n_ev)
        ready += [*qkv_halves, *qkv_far]
    ffn_shard = pl.pallas_call(
        fold_kernel,
        out_shape=jax.ShapeDtypeStruct((width + FW_ROWS, hidden), BF16),
        in_specs=[vmem()] * 3,
        out_specs=vmem(),
        compiler_params=params(SNUG),
        cost_estimate=cost(30),
        name="fold",
    )(ffn_out, heads, after(ffn_in, *ready))
    gate = [got]
    if two_hops:
        qkv_second = second_hop(*qkv_halves, n_ev)
        qkv_far += across(qkv_second, n_ev)
        ffn_far = across([ffn_shard], n_ev)
        gate += qkv_second
    ffn_first = [ffn_shard] + first_hop(after(ffn_shard, *gate), n_ev)[1:]
    if two_hops:
        got = after(got, *ffn_far, *qkv_far)
    vec = pl.pallas_call(
        functools.partial(encode_kernel, visits_dev),
        out_shape=jax.ShapeDtypeStruct((VPAD, DV), BF16),
        in_specs=[vmem(), hbm(), hbm(), hbm()],
        out_specs=vmem(),
        scratch_shapes=[
            pltpu.VMEM((rows_dev, D + LANES), BF16),
            pltpu.VMEM((D, 2 * D), BF16),
            pltpu.VMEM((D, D), BF16),
            pltpu.VMEM((D, D), BF16),
            pltpu.VMEM((visits_dev * VB, D), BF16),
            pltpu.VMEM((visits_dev * VB, 2 * D), BF16),
            pltpu.VMEM((visits_dev, HEADS, VB), F32),
            pltpu.VMEM((visits_dev, HEADS, D), BF16),
            pltpu.SemaphoreType.DMA((5,)),
        ],
        compiler_params=params(53),
        cost_estimate=cost(0),
        name="encode",
    )(enc_gain.reshape(1, D), got, enc_qkv, enc_out)

    vecs = [vec] + [swap(vec, "mp", n_mp, k) for k in range(1, n_mp)]
    if two_hops:
        qkv_pieces = qkv_first + qkv_second + qkv_far
        ffn_next = [ffn_first[0]] + [after(piece, *vecs[1:]) for piece in ffn_first[1:]]
        ffn_second = second_hop(*halves_of(ffn_next, width // 2), n_ev)
        ffn_far += across(ffn_next[1:], n_ev)
        vecs[0] = after(vec, *ffn_far[1:])
    else:
        qkv_pieces = qkv_first
    n_q = len(qkv_pieces)
    qkv_plan = grouped(hop_places(n_ev, width), qkv_pieces, 1)
    vgain = visit_gain.reshape(1, DV)
    state_shape = (group, state_spans(cols)[2][1])
    attended, state = pl.pallas_call(
        functools.partial(project_kernel, n_mp, n_ev, qkv_plan),
        out_shape=[
            jax.ShapeDtypeStruct((group, cols), BF16),
            jax.ShapeDtypeStruct(state_shape, F32),
        ],
        in_specs=[smem()] + [vmem()] * (n_mp + 3) + [hbm()] * n_q,
        out_specs=[vmem(), hbm()],
        scratch_shapes=room(qkv_plan, visit_qkv, 1)
        + [
            pltpu.VMEM((n_mp, VPAD, DV), BF16),
            pltpu.VMEM((n_ev, group, width), BF16),
            pltpu.SemaphoreType.DMA((n_q,)),
            pltpu.VMEM(state_shape, F32),
            pltpu.SemaphoreType.DMA((3,)),
        ],
        compiler_params=params(SNUG),
        cost_estimate=cost(0),
        name="project",
    )(where, *vecs, vgain, meta, patient_row, *qkv_pieces)

    attns = [attended] + [swap(attended, "mp", n_mp, k) for k in range(1, n_mp)]
    if two_hops:
        ffn_second = [after(piece, *attns[1:]) for piece in ffn_second]
        ffn_pieces = ffn_first + ffn_second + ffn_far + across(ffn_second, n_ev)
    else:
        ffn_pieces = ffn_first
    n_f = len(ffn_pieces)
    ffn_plan = grouped(hop_places(n_ev, width), ffn_pieces, 0)
    fgain = ffn_gain.reshape(1, DV)
    ffn_outs = pl.pallas_call(
        functools.partial(ffn_kernel, n_mp, n_ev, ffn_plan),
        out_shape=[jax.ShapeDtypeStruct((group, cols + LANES), BF16)] * n_mp
        + [jax.ShapeDtypeStruct((group, cols + LANES), F32)],
        in_specs=[smem()] * 2 + [vmem()] * (3 + n_mp) + [hbm()] * (1 + n_f),
        out_specs=[vmem()] * (n_mp + 1),
        scratch_shapes=room(ffn_plan, ffn_shard, 0)
        + [
            pltpu.VMEM((n_mp, group, cols), BF16),
            pltpu.VMEM((group, DV), F32),
            pltpu.VMEM((n_ev, group, width), BF16),
            pltpu.VMEM((n_ev, group, width), F32),
            pltpu.SemaphoreType.DMA((n_f + 1,)),
        ],
        compiler_params=params(SNUG),
        cost_estimate=cost(0),
        name="ffn",
    )(where, head_bias, fgain, meta, head_t, *attns, state, *ffn_pieces)
    mid = ffn_outs[n_mp]
    pays = [ffn_outs[0]] + [swap(ffn_outs[k], "mp", n_mp, k) for k in range(1, n_mp)]

    back_outs = pl.pallas_call(
        functools.partial(back_kernel, n_mp, n_ev, qkv_plan),
        out_shape=[jax.ShapeDtypeStruct((VPAD, D + LANES), BF16)] * n_mp
        + [jax.ShapeDtypeStruct((group, LANES), F32), jax.ShapeDtypeStruct((VPAD, D), F32)],
        in_specs=[smem()] + [vmem()] * (5 + n_mp) + [hbm()] * (1 + n_q),
        out_specs=[vmem()] * (n_mp + 2),
        scratch_shapes=room(qkv_plan, visit_qkv, 1)
        + [
            pltpu.VMEM(state_shape, F32),
            pltpu.VMEM((n_ev, group, width), F32),
            pltpu.VMEM((n_mp, VPAD, D + LANES), F32),
            pltpu.SemaphoreType.DMA((n_q + 1,)),
        ],
        compiler_params=params(SNUG),
        cost_estimate=cost(0),
        name="back",
    )(where, mid, meta, fgain, vgain, head_t, *pays, state, *qkv_pieces)
    outcomes = back_outs[n_mp][:, :2].reshape(n_mp, VPAD, 2)[:, :visits_dev].reshape(per_owner, 2)
    shares = [back_outs[0]] + [swap(back_outs[k], "mp", n_mp, k) for k in range(1, n_mp)]
    visit_grad = pl.pallas_call(
        functools.partial(finish_kernel, n_mp, visits_dev),
        out_shape=jax.ShapeDtypeStruct((VPAD, D), F32),
        in_specs=[smem()] + [vmem()] * (1 + n_mp),
        out_specs=vmem(),
        compiler_params=params(4),
        cost_estimate=cost(0),
        name="finish",
    )(visit_count, after(back_outs[n_mp + 1], outcomes), *shares)

    tables = gather_events(visit_grad, n_ev)
    event_grads = pl.pallas_call(
        functools.partial(spread_kernel, n_ev),
        out_shape=jax.ShapeDtypeStruct((rows_dev, D), BF16),
        in_specs=[vmem()] * (n_ev + 1),
        out_specs=hbm(),
        scratch_shapes=[
            pltpu.VMEM((rows_dev, D), BF16),
            pltpu.SemaphoreType.DMA((3,)),
        ],
        compiler_params=params(8),
        cost_estimate=cost(0),
        name="spread",
    )(chosen, *tables)
    return (outcomes, event_grads)


def solution(mesh):
    in_specs = (
        P(("events", "mp"), None),
        P(("events", "mp")),
        P(("events", "mp")),
        P("events"),
        P("events"),
        P("events"),
        P(),
        P(),
        P(),
        P(),
        P(None, "events", "mp"),
        P(),
        P("events", "mp"),
        P("mp", "events"),
        P(),
        P(),
    )
    out_specs = (P("events", None), P(("events", "mp"), None))
    return jax.shard_map(local, mesh=mesh, in_specs=in_specs, out_specs=out_specs, check_vma=False)
```
